32 devices in a mesh: row: 4 (over x, core), col: 8 (over z, y).
Axes of the slice: x: 2, y: 2, z: 4, core: 2. Of those that a mesh axis runs over, the one named last changes fastest.
Arguments:
- history: bfloat16 [4, 16, 4096], P(None, None, ('col', 'row')), may hold values from -6 to 6
- incident: float32 [16, 4096], P(None, ('col', 'row')), may hold values from -6 to 6
- centroids: float32 [3, 4096], replicated, may hold values from 0 to 1
- moments: float32 [4, 4096], replicated, may hold values from -4 to 4
- dual_moments: float32 [3, 4096], replicated, may hold values from -4 to 4
- shell: int32 [32, 32], P('row', 'col'), may hold values from 0 to 3
- near_mask: int32 [32, 32], P('row', 'col'), may hold values 0 or 1
- neighbours: int32 [4, 4096], P(None, 'row'), may hold values from 0 to 4095, as said below
- gram_diag: float32 [4096], P('row'), may hold values from 2 to 3
- gram_off: float32 [4, 4096], P(None, 'row'), may hold values from -0.45 to 0.45, as said below
Outputs:
- march_rhs: float32 [16, 4096], P(None, ('col', 'row'))
- dual_field: float32 [16, 4096], P(None, ('row', 'col'))
The draws below stay inside these ranges and needn't reach their ends.
Inputs may be any that keep to these rules, and one draw needn't show every extreme that they name: neighbours[m, i] differs from i by 1 to 32; the first row is i + 32 (i - 32 where that leaves the range), the second i - 32 (i + 32 where that leaves the range). `gram_off`: each entry's magnitude is 0.25 to 0.45.
All inputs are finite; a program needn't handle non-finite values. No bound on the sum of `near_mask` on one device may be relied on, other than what follows from the above.
Results may differ from the reference program's by a relative error of at most 0.008.
Values may be sent and summed in bfloat16 or wider, within the bound.
No kernel may reach another device: no remote copies, remote signals or barrier semaphores. Data moves between devices by JAX's collectives and lax.ppermute only.
A program may use at most 64 MiB of HBM per device.

```python
import math
import jax
import jax.numpy as jnp
from jax import lax

E = 16
H = 4
SWEEPS = 2
W = 32
NRWG = 4096
NT = 32


def draw_neighbours(key, part):
    key = jax.random.fold_in(key, 7)
    key_reach, key_sign = jax.random.split(key, 2)
    positions = jnp.arange(NRWG, dtype=jnp.int32)
    reach = jax.random.randint(key_reach, (4, NRWG), 1, W + 1)
    reach = jnp.concatenate([jnp.full((2, NRWG), W, jnp.int32), reach[2:]], axis=0)
    signs = 2 * jax.random.randint(key_sign, (4, NRWG), 0, 2) - 1
    fixed_signs = jnp.concatenate([jnp.ones((1, NRWG), jnp.int32), -jnp.ones((1, NRWG), jnp.int32)], axis=0)
    signs = jnp.concatenate([fixed_signs, signs[2:]], axis=0)
    offsets = signs * reach
    forward = positions[None, :] + offsets
    inside = (forward >= 0) & (forward < NRWG)
    return jnp.where(inside, forward, positions[None, :] - offsets).astype(jnp.int32)


def draw_gram_off(key, part):
    key = jax.random.fold_in(key, 11)
    key_size, key_sign = jax.random.split(key, 2)
    magnitude = jax.random.uniform(key_size, (4, NRWG), jnp.float32, 0.25, 0.45)
    signs = (2 * jax.random.randint(key_sign, (4, NRWG), 0, 2) - 1).astype(jnp.float32)
    return magnitude * signs


def touch_ends(result, key, low, largest):
    extent = result.shape
    index_at = [jax.random.randint(jax.random.fold_in(key, axis), (), 0, extent[axis]) for axis in range(len(extent))]
    result = result.at[tuple(index_at)].set(low)
    longest = extent.index(max(extent))
    index_at[longest] = (index_at[longest] + 1) % extent[longest]
    return result.at[tuple(index_at)].set(largest)


def level_of(key, dims, cuts, least, top_value):
    def one(position, blocks):
        steps = jax.random.uniform(jax.random.fold_in(jax.random.fold_in(key, 6), position), (blocks,), jnp.float32, least / len(cuts), top_value / len(cuts))
        return jnp.repeat(jnp.exp(steps), dims[position] // blocks).reshape((-1,) + (1,) * (len(dims) - position - 1))

    gain = one(*cuts[0])
    for cut in cuts[1:]:
        gain = gain * one(*cut)
    return gain


def gaussian(stream_key, dims, deviation, limit, cuts=(), kind=jnp.bfloat16):
    drawn = deviation * jax.random.normal(stream_key, dims, jnp.float32)
    if cuts:
        drawn = drawn * level_of(stream_key, dims, cuts, -0.22, 0.18)
    return jnp.clip(drawn, -limit, limit).astype(kind)


def setup_inputs(seed: int = 0) -> dict:
    key_list = jax.random.split(jax.random.key(seed), 11)
    history = gaussian(key_list[0], (H, E, NRWG), 1.0, 6.0, ((2, 32),))
    incident = gaussian(key_list[1], (E, NRWG), 1.0, 6.0, ((1, 32),), jnp.float32)
    centroids = jnp.clip(jax.random.uniform(key_list[2], (3, NRWG), jnp.float32, 0.0, 1.0), 0.0, 1.0)
    moments = gaussian(key_list[3], (4, NRWG), 0.6, 4.0, (), jnp.float32)
    dual_moments = gaussian(key_list[4], (3, NRWG), 0.6, 4.0, (), jnp.float32)
    shell = touch_ends(jax.random.randint(key_list[5], (NT, NT), 0, H), jax.random.fold_in(key_list[5], 1), 0, H - 1).astype(jnp.int32)
    near_mask = touch_ends((jax.random.randint(key_list[6], (NT, NT), 0, 3) < 1).astype(jnp.int32), jax.random.fold_in(key_list[6], 1), 0, 1)
    neighbours = draw_neighbours(jax.random.fold_in(key_list[10], 71), 0)
    gram_diag = jnp.clip(2.0 + 1.0 * jax.random.uniform(key_list[8], (NRWG,), jnp.float32) ** level_of(key_list[8], (NRWG,), ((0, 4),), -0.2, 0.2), 2.0, 3.0)
    gram_off = draw_gram_off(jax.random.fold_in(key_list[10], 71), 0)
    return dict(history=history, incident=incident, centroids=centroids, moments=moments, dual_moments=dual_moments, shell=shell, near_mask=near_mask, neighbours=neighbours, gram_diag=gram_diag, gram_off=gram_off)


SOFT_T = 0.05
SOFT_S = 0.1
NEAR_GAIN = 2.0
NEAR_REACH = 0.5

def distances(row_xyz, col_xyz):
    delta_x = row_xyz[0][:, None] - col_xyz[0][None, :]
    delta_y = row_xyz[1][:, None] - col_xyz[1][None, :]
    delta_z = row_xyz[2][:, None] - col_xyz[2][None, :]
    return jnp.sqrt(delta_x * delta_x + delta_y * delta_y + delta_z * delta_z)

def reference(history, incident, centroids, moments, dual_moments, shell, near_mask, neighbours, gram_diag, gram_off):
    total_rwg = centroids.shape[1]
    tile_len = total_rwg // shell.shape[0]
    row_block = math.gcd(total_rwg, 512)
    tile_rows = row_block // tile_len
    norm_scale = 1.0 / math.sqrt(total_rwg)
    excitations = history.shape[1]
    weights = jnp.concatenate([moments[:3], -moments[3:]], axis=0)
    scaled = (moments[None, :, None, :] * history[:, None, :, :].astype(jnp.float32)).astype(jnp.bfloat16)

    def t_rows(block_id):
        row_lo = block_id * row_block
        row_xyz = lax.dynamic_slice_in_dim(centroids, row_lo, row_block, 1)
        row_weights = lax.dynamic_slice_in_dim(weights, row_lo, row_block, 1)
        shell_rows = jnp.repeat(lax.dynamic_slice_in_dim(shell, block_id * tile_rows, tile_rows, 0), tile_len, axis=1)
        mask_rows = jnp.repeat(lax.dynamic_slice_in_dim(near_mask, block_id * tile_rows, tile_rows, 0), tile_len, axis=1)
        spacing = distances(row_xyz, centroids).reshape(tile_rows, tile_len, total_rwg)
        kernel = (1.0 / (spacing + SOFT_T) + NEAR_GAIN * mask_rows[:, None, :].astype(jnp.float32) * jnp.exp(-spacing / NEAR_REACH)).astype(jnp.bfloat16)
        picked = jnp.zeros((tile_rows,) + scaled.shape[1:], jnp.bfloat16)
        for slot_id in range(H):
            picked = jnp.where((shell_rows == slot_id)[:, None, None, :], scaled[slot_id][None], picked)
        products = jnp.einsum('tqk,tabk->abtq', kernel.astype(jnp.float32), picked.astype(jnp.float32))
        products = products.reshape(products.shape[0], products.shape[1], row_block)
        return lax.optimization_barrier(jnp.sum(row_weights[:, None, :] * products, axis=0))
    block_out = lax.map(t_rows, jnp.arange(total_rwg // row_block, dtype=jnp.int32))
    field = jnp.moveaxis(block_out, 0, 1).reshape(excitations, total_rwg) * norm_scale
    dual_field = field / gram_diag[None, :]
    for sweep_id in range(SWEEPS):
        nearby = jnp.take(dual_field, neighbours.reshape(-1), axis=1).reshape(excitations, neighbours.shape[0], total_rwg)
        coupling = lax.optimization_barrier(jnp.sum(gram_off[None] * nearby, axis=1))
        dual_field = (field - coupling) / gram_diag[None, :]
    scaled_dual = (dual_moments[:, None, :] * dual_field[None]).astype(jnp.bfloat16)

    def s_rows(block_id):
        row_lo = block_id * row_block
        row_xyz = lax.dynamic_slice_in_dim(centroids, row_lo, row_block, 1)
        row_dual = lax.dynamic_slice_in_dim(dual_moments, row_lo, row_block, 1)
        kernel = (1.0 / (distances(row_xyz, centroids) + SOFT_S)).astype(jnp.bfloat16)
        products = jnp.einsum('qk,abk->abq', kernel.astype(jnp.float32), scaled_dual.astype(jnp.float32))
        return lax.optimization_barrier(jnp.sum(row_dual[:, None, :] * products, axis=0))
    block_out = lax.map(s_rows, jnp.arange(total_rwg // row_block, dtype=jnp.int32))
    potential = jnp.moveaxis(block_out, 0, 1).reshape(excitations, total_rwg)
    march_rhs = incident - potential * norm_scale
    return (march_rhs, dual_field)
```

```python
import math

import jax
import jax.numpy as jnp
from jax import lax
from jax.sharding import PartitionSpec as P

SWEEPS = 2
W = 32


SOFT_T = 0.05
SOFT_S = 0.1
NEAR_GAIN = 2.0
NEAR_REACH = 0.5


def extended_2(block, sides, width):
    for axis, dim in sides:
        count = lax.axis_size(axis)
        forward = [(i, i + 1) for i in range(count - 1)]
        backward = [(target, source) for source, target in forward]
        low = lax.ppermute(
            lax.slice_in_dim(block, block.shape[dim] - width, None, axis=dim), axis, forward
        )
        high = lax.ppermute(lax.slice_in_dim(block, 0, width, axis=dim), axis, backward)
        block = jnp.concatenate([low, block, high], axis=dim)
    return block


def distances(row_xyz, col_xyz):
    delta_x = row_xyz[0][:, None] - col_xyz[0][None, :]
    delta_y = row_xyz[1][:, None] - col_xyz[1][None, :]
    delta_z = row_xyz[2][:, None] - col_xyz[2][None, :]
    return jnp.sqrt(delta_x * delta_x + delta_y * delta_y + delta_z * delta_z)


def apply_t_tiles(row_xyz, row_weights, col_xyz, scaled, shell_rows, mask_rows, tile_len):
    tile_rows = shell_rows.shape[0]
    col_count = col_xyz.shape[1]
    spacing = distances(row_xyz, col_xyz).reshape(tile_rows, tile_len, col_count)
    kernel = (
        1.0 / (spacing + SOFT_T)
        + NEAR_GAIN * mask_rows[:, None, :].astype(jnp.float32) * jnp.exp(-spacing / NEAR_REACH)
    ).astype(jnp.bfloat16)
    picked = jnp.zeros((tile_rows,) + scaled.shape[1:], jnp.bfloat16)
    for slot_id in range(scaled.shape[0]):
        picked = jnp.where((shell_rows == slot_id)[:, None, None, :], scaled[slot_id][None], picked)
    products = jnp.einsum("tqk,tabk->abtq", kernel, picked, preferred_element_type=jnp.float32)
    products = products.reshape(products.shape[0], products.shape[1], tile_rows * tile_len)
    return jnp.sum(row_weights[:, None, :] * products, axis=0)


def sweep_mass(field_sum, diag, off_diag, links, base, extend):
    dual_iter = field_sum / diag[None, :]
    length = field_sum.shape[1]
    local_index = (links - base + W).reshape(-1)
    for sweep_id in range(SWEEPS):
        extended = extend(dual_iter)
        nearby = jnp.take(extended, local_index, axis=1).reshape(
            field_sum.shape[0], links.shape[0], length
        )
        coupling = jnp.sum(off_diag[None] * nearby, axis=1)
        dual_iter = (field_sum - coupling) / diag[None, :]
    return dual_iter


def per_device(
    history,
    incident,
    centroids,
    moments,
    dual_moments,
    shell,
    near_mask,
    neighbours,
    gram_diag,
    gram_off,
):
    row_devices = lax.axis_size("row")
    col_devices = lax.axis_size("col")
    row_id = lax.axis_index("row")
    col_id = lax.axis_index("col")
    shard_len = history.shape[2]
    excitations = history.shape[1]
    rows_t = shard_len * col_devices
    cols_t = shard_len * row_devices
    total_rwg = rows_t * row_devices
    tile_len = rows_t // shell.shape[0]
    norm_scale = 1.0 / math.sqrt(total_rwg)
    row_start = row_id * rows_t
    col_start = col_id * cols_t
    weights = jnp.concatenate([moments[:3], -moments[3:]], axis=0)
    t_block = math.gcd(rows_t, 512)
    t_tiles = t_block // tile_len
    row_xyz = lax.dynamic_slice_in_dim(centroids, row_start, rows_t, 1)
    row_weights = lax.dynamic_slice_in_dim(weights, row_start, rows_t, 1)
    shell_wide = jnp.repeat(shell, tile_len, axis=1)
    mask_wide = jnp.repeat(near_mask, tile_len, axis=1)
    hist_piece = lax.all_gather(history, "row", axis=2, tiled=True)
    col_count = hist_piece.shape[2]
    col_first = col_start
    col_xyz = lax.dynamic_slice_in_dim(centroids, col_first, col_count, 1)
    col_moments = lax.dynamic_slice_in_dim(moments, col_first, col_count, 1)
    scaled = (col_moments[None, :, None, :] * hist_piece[:, None, :, :].astype(jnp.float32)).astype(
        jnp.bfloat16
    )

    def one_block(block_id):
        row_lo = block_id * t_block
        return apply_t_tiles(
            lax.dynamic_slice_in_dim(row_xyz, row_lo, t_block, 1),
            lax.dynamic_slice_in_dim(row_weights, row_lo, t_block, 1),
            col_xyz,
            scaled,
            lax.dynamic_slice_in_dim(shell_wide, block_id * t_tiles, t_tiles, 0),
            lax.dynamic_slice_in_dim(mask_wide, block_id * t_tiles, t_tiles, 0),
            tile_len,
        )

    block_out = lax.map(one_block, jnp.arange(rows_t // t_block, dtype=jnp.int32))
    partial_field = jnp.moveaxis(block_out, 0, 1).reshape(excitations, rows_t)
    partial_field = partial_field * norm_scale
    pieces = partial_field.reshape(excitations, col_devices, shard_len).transpose(1, 0, 2)
    pieces = lax.all_to_all(pieces, "col", 0, 0)
    share_sum = jnp.sum(pieces, axis=0)
    shard_offset = col_id * shard_len
    own_dual = sweep_mass(
        share_sum,
        lax.dynamic_slice_in_dim(gram_diag, shard_offset, shard_len, 0),
        lax.dynamic_slice_in_dim(gram_off, shard_offset, shard_len, 1),
        lax.dynamic_slice_in_dim(neighbours, shard_offset, shard_len, 1),
        row_start + shard_offset,
        lambda values: extended_2(values, ((("row", "col"), 1),), W),
    )
    devices = row_devices * col_devices
    sent = jnp.broadcast_to(own_dual.astype(jnp.bfloat16)[None], (devices, excitations, shard_len))
    dual_all = lax.all_to_all(sent, ("row", "col"), 0, 0)
    scaled_dual = (
        dual_moments.reshape(3, devices, 1, shard_len) * dual_all[None].astype(jnp.float32)
    ).astype(jnp.bfloat16)
    out_start = (col_id * row_devices + row_id) * shard_len
    srow_xyz = lax.dynamic_slice_in_dim(centroids, out_start, shard_len, 1)
    srow_dual = lax.dynamic_slice_in_dim(dual_moments, out_start, shard_len, 1)
    kernel = (1.0 / (distances(srow_xyz, centroids) + SOFT_S)).astype(jnp.bfloat16)
    kernel = kernel.reshape(shard_len, devices, shard_len)
    products = jnp.einsum("qdk,adbk->abq", kernel, scaled_dual, preferred_element_type=jnp.float32)
    potential = jnp.sum(srow_dual[:, None, :] * products, axis=0)
    march_rhs = incident - potential * norm_scale
    return (march_rhs, own_dual)


def solution(mesh):
    placed = (
        P(None, None, ("col", "row")),
        P(None, ("col", "row")),
        P(),
        P(),
        P(),
        P("row", "col"),
        P("row", "col"),
        P(None, "row"),
        P("row"),
        P(None, "row"),
    )
    return jax.shard_map(
        per_device,
        mesh=mesh,
        in_specs=placed,
        out_specs=(P(None, ("col", "row")), P(None, ("row", "col"))),
        check_vma=False,
    )
```

```python
import functools
import math

import jax
import jax.numpy as jnp
from jax import lax
from jax.experimental import pallas as pl
from jax.experimental.pallas import tpu as pltpu
from jax.sharding import PartitionSpec as P

SWEEPS = 2

SOFT_T = 0.05
SOFT_S = 0.1
NEAR_GAIN = 2.0
NEAR_REACH = 0.5

LANES = 128
HALF = LANES // 2
CHUNK = 64

VMEM = pl.BlockSpec(memory_space=pltpu.VMEM)
SMEM = pl.BlockSpec(memory_space=pltpu.SMEM)
PARAMS = pltpu.CompilerParams(vmem_limit_bytes=56 * 1024 * 1024)


def lane_ids(rows=1):
    return lax.broadcasted_iota(jnp.int32, (rows, LANES), 1)


def tile_at(start):
    return pl.ds(pl.multiple_of(start, LANES), LANES)


def edges(ref, row, length):
    first = ref[row : row + 1, :LANES]
    last = ref[row : row + 1, length - LANES :]
    return jnp.where(lane_ids() < HALF, first, last)


def split3(value):
    high = value.astype(jnp.bfloat16).astype(jnp.float32)
    rest = value - high
    middle = rest.astype(jnp.bfloat16).astype(jnp.float32)
    return [high, middle, rest - middle]


def stack_rows(rows, height):
    row_ids = lax.broadcasted_iota(jnp.int32, (height, LANES), 0)
    out = jnp.zeros((height, LANES), jnp.float32)
    for position, row in enumerate(rows):
        out = jnp.where(row_ids == position, row, out)
    return out


def pack_kernel(history_ref, shell_ref, near_ref, diag_ref, off_ref, links_ref, out_ref):
    slots, excitations = history_ref.shape[:2]
    length = diag_ref.shape[1]
    tiles = shell_ref.shape[1]
    lanes = lane_ids()
    rows = []
    for tile in (0, tiles - 1):
        code = jnp.zeros((1, LANES), jnp.float32)
        for j in range(shell_ref.shape[0]):
            value = (shell_ref[j, tile] + slots * near_ref[j, tile]).astype(jnp.float32)
            code = jnp.where(lanes == j, value, code)
        rows.append(code)
    here = lax.axis_index("row") * length + jnp.where(lanes < HALF, lanes, length - LANES + lanes)
    for m in range(links_ref.shape[0]):
        rows.append((edges(links_ref, m, length) - here).astype(jnp.float32))
    rows += split3(edges(diag_ref, 0, length))
    coupling = []
    for m in range(off_ref.shape[0]):
        coupling += split3(edges(off_ref, m, length))
    out_ref[:slots] = history_ref[...]
    out_ref[slots] = stack_rows(rows, excitations).astype(jnp.bfloat16)
    out_ref[slots + 1] = stack_rows(coupling, excitations).astype(jnp.bfloat16)


def halo_row(packed_ref, row_count, plane, row):
    me = lax.axis_index("row")
    right = lax.rem(me + 1, row_count)
    left = lax.rem(me + row_count - 1, row_count)
    right_row = packed_ref[plane, :, tile_at(right * LANES)].astype(jnp.float32)[row : row + 1]
    left_row = packed_ref[plane, :, tile_at(left * LANES)].astype(jnp.float32)[row : row + 1]
    return right_row, left_row


def column_coords(centroids_ref, start, store):
    for axis in range(3):
        line = centroids_ref[axis : axis + 1, tile_at(start)]
        store(axis, jnp.broadcast_to(line, (LANES, LANES)).T)


def t_kernel(
    packed_ref, centroids_ref, moments_ref, shell_ref, near_ref, out_ref, scaled_ref, column_ref, tile_ref, norm, slots
):
    q_tiles, p_tiles = shell_ref.shape
    row_count = packed_ref.shape[2] // LANES
    excitations = packed_ref.shape[1]
    kinds = moments_ref.shape[0]
    copies = out_ref.shape[0]
    total = centroids_ref.shape[1]
    length = p_tiles * LANES
    row_start = lax.axis_index("row") * length
    col_start = lax.axis_index("col") * (q_tiles * LANES)
    low = lane_ids() < HALF

    code_right, code_left = halo_row(packed_ref, row_count, slots, 0)[0], halo_row(packed_ref, row_count, slots, 1)[1]
    near_right = jnp.where(code_right >= slots, 1.0, 0.0)
    near_left = jnp.where(code_left >= slots, 1.0, 0.0)
    slot_right = code_right - slots * near_right
    slot_left = code_left - slots * near_left

    for j in range(q_tiles):
        lanes = slice(j * LANES, (j + 1) * LANES)
        weights = [moments_ref[a : a + 1, tile_at(col_start + j * LANES)] for a in range(kinds)]
        picked = [packed_ref[s, :, lanes].astype(jnp.float32) for s in range(slots)]
        for code in (slot_right, slot_left):
            choice = jnp.broadcast_to(code[:, j : j + 1], (excitations, LANES))
            value = picked[0]
            for s in range(1, slots):
                value = jnp.where(choice == s, picked[s], value)
            picked.append(value)
        for s, value in enumerate(picked):
            for a in range(kinds):
                scaled_ref[s, a * excitations : (a + 1) * excitations, lanes] = (weights[a] * value).astype(jnp.bfloat16)

        def store(axis, value, j=j):
            column_ref[axis, j * LANES : (j + 1) * LANES, :] = value

        column_coords(centroids_ref, col_start + j * LANES, store)

    def fill(line, gain_of):
        for j in range(q_tiles):
            gain = gain_of(j)
            for k in range(LANES // CHUNK):
                at = slice(j * LANES + k * CHUNK, j * LANES + (k + 1) * CHUNK)
                dx = line[0] - column_ref[0, at, :]
                dy = line[1] - column_ref[1, at, :]
                dz = line[2] - column_ref[2, at, :]
                spacing = jnp.sqrt(dx * dx + dy * dy + dz * dz)
                tile_ref[at, :] = (
                    1.0 / (spacing + SOFT_T) + gain * jnp.exp(spacing * (-1.0 / NEAR_REACH))
                ).astype(jnp.bfloat16)

    def products(lhs):
        return jnp.dot(lhs, tile_ref[...], preferred_element_type=jnp.float32)

    def weighted(product, weights):
        field = weights[0] * product[:excitations]
        for a in range(1, kinds):
            term = weights[a] * product[a * excitations : (a + 1) * excitations]
            field = field + term if a < kinds - 1 else field - term
        return (field * norm).astype(jnp.bfloat16)

    def one_tile(t, carry):
        start = row_start + t * LANES
        line = [centroids_ref[axis : axis + 1, tile_at(start)] for axis in range(3)]
        fill(line, lambda j: NEAR_GAIN * near_ref[j, t].astype(jnp.float32))
        lhs = jnp.concatenate(
            [scaled_ref[shell_ref[j, t], :, j * LANES : (j + 1) * LANES] for j in range(q_tiles)], axis=1
        )
        weights = [moments_ref[a : a + 1, tile_at(start)] for a in range(kinds)]
        field = weighted(products(lhs), weights)
        for copy in range(copies):
            out_ref[copy, :, tile_at(t * LANES)] = field
        return carry

    lax.fori_loop(0, p_tiles, one_tile, 0)

    right_start = lax.rem(row_start + length, total)
    left_start = lax.rem(row_start + total - LANES, total)

    def halo(ref, row):
        return jnp.where(low, ref[row : row + 1, tile_at(right_start)], ref[row : row + 1, tile_at(left_start)])

    gains = NEAR_GAIN * jnp.where(low, 1.0, 0.0), NEAR_GAIN * jnp.where(low, 0.0, 1.0)
    fill(
        [halo(centroids_ref, axis) for axis in range(3)],
        lambda j: gains[0] * near_right[:, j : j + 1] + gains[1] * near_left[:, j : j + 1],
    )
    product = jnp.where(low, products(scaled_ref[slots]), products(scaled_ref[slots + 1]))
    field = weighted(product, [halo(moments_ref, a) for a in range(kinds)])
    for copy in range(copies):
        out_ref[copy, :, length:] = field


def s_tiles_kernel(centroids_ref, out_ref, column_ref):
    length, width = out_ref.shape
    row_start = lax.axis_index("row") * length
    col_start = lax.axis_index("col") * width

    def one_tile(t, carry):
        def store(axis, value):
            column_ref[axis] = value

        column_coords(centroids_ref, row_start + t * LANES, store)
        for k in range(width // LANES):
            line = [centroids_ref[axis : axis + 1, tile_at(col_start + k * LANES)] for axis in range(3)]
            for piece in range(LANES // CHUNK):
                at = slice(piece * CHUNK, (piece + 1) * CHUNK)
                dx = line[0] - column_ref[0, at, :]
                dy = line[1] - column_ref[1, at, :]
                dz = line[2] - column_ref[2, at, :]
                spacing = jnp.sqrt(dx * dx + dy * dy + dz * dz)
                rows = pl.ds(pl.multiple_of(t * LANES + piece * CHUNK, CHUNK), CHUNK)
                out_ref[rows, k * LANES : (k + 1) * LANES] = (1.0 / (spacing + SOFT_S)).astype(jnp.bfloat16)
        return carry

    lax.fori_loop(0, length // LANES, one_tile, 0)


def sweep_kernel(
    parts_ref, packed_ref, diag_ref, off_ref, links_ref, tiles_ref, dual_moments_ref, dual_ref, out_ref, iter_ref, scaled_ref, slots
):
    length = diag_ref.shape[1]
    tiles = length // LANES
    row_count = packed_ref.shape[2] // LANES
    excitations = parts_ref.shape[1]
    link_count = links_ref.shape[0]
    kinds = dual_moments_ref.shape[0]
    row_start = lax.axis_index("row") * length
    col_start = lax.axis_index("col") * tiles_ref.shape[1]
    lanes = lane_ids()
    low = lanes < HALF

    def halo(plane, row):
        return jnp.where(low, *halo_row(packed_ref, row_count, plane, row))

    def sum3(plane, row):
        return halo(plane, row) + halo(plane, row + 1) + halo(plane, row + 2)

    def tile(t):
        return slice(t * LANES, (t + 1) * LANES)

    field, diag = [], []
    for t in range(tiles + 1):
        total = parts_ref[0, :, tile(t)].astype(jnp.float32)
        for c in range(1, parts_ref.shape[0]):
            total = total + parts_ref[c, :, tile(t)].astype(jnp.float32)
        field.append(total)
        diag.append(diag_ref[:, tile(t)] if t < tiles else sum3(slots, 2 + link_count))

    dual = [f / d for f, d in zip(field, diag)]
    for sweep_id in range(SWEEPS):
        last = sweep_id == SWEEPS - 1
        updated = []
        for t in range(tiles if last else tiles + 1):
            around = jnp.where(low, dual[(t + 1) % (tiles + 1)], dual[t - 1])
            coupled = jnp.zeros_like(field[t])
            for m in range(link_count):
                if t < tiles:
                    source = links_ref[m : m + 1, tile(t)] - (row_start + t * LANES)
                    gram = off_ref[m : m + 1, tile(t)]
                else:
                    source = halo(slots, 2 + m).astype(jnp.int32) + lanes
                    gram = sum3(slots + 1, 3 * m)
                inside = (source >= 0) & (source < LANES)
                index = jnp.broadcast_to(source & (LANES - 1), (excitations, LANES))
                here = jnp.take_along_axis(dual[t], index, axis=1)
                beside = jnp.take_along_axis(around, index, axis=1)
                coupled = coupled + gram * jnp.where(inside, here, beside)
            updated.append((field[t] - coupled) / diag[t])
        dual = updated

    for t in range(tiles):
        iter_ref[t] = dual[t]
        for a in range(kinds):
            weight = dual_moments_ref[a : a + 1, tile_at(row_start + t * LANES)]
            scaled_ref[a * excitations : (a + 1) * excitations, tile(t)] = (weight * dual[t]).astype(jnp.bfloat16)
    dual_ref[...] = iter_ref[lax.axis_index("col")]
    product = jnp.dot(scaled_ref[...], tiles_ref[...], preferred_element_type=jnp.float32)
    for k in range(out_ref.shape[0]):
        term = jnp.zeros((excitations, LANES), jnp.float32)
        for a in range(kinds):
            weight = dual_moments_ref[a : a + 1, tile_at(col_start + k * LANES)]
            term = term + weight * product[a * excitations : (a + 1) * excitations, tile(k)]
        out_ref[k] = term.astype(jnp.bfloat16)


def final_kernel(shares_ref, incident_ref, out_ref, norm):
    me = lax.axis_index("row")
    total = jnp.zeros(out_ref.shape, jnp.float32)
    for share in range(shares_ref.shape[2] // LANES):
        total = total + shares_ref[me, :, share * LANES : (share + 1) * LANES].astype(jnp.float32)
    out_ref[...] = incident_ref[...] - total * norm


def per_device(
    history,
    incident,
    centroids,
    moments,
    dual_moments,
    shell,
    near_mask,
    neighbours,
    gram_diag,
    gram_off,
):
    col_devices = lax.axis_size("col")
    slots, excitations, shard_len = history.shape
    p_tiles, q_tiles = shell.shape
    rows_t = gram_diag.shape[0]
    cols_t = q_tiles * LANES
    norm = 1.0 / math.sqrt(centroids.shape[1])
    shell, near_mask = shell.T, near_mask.T
    gram_diag = gram_diag.reshape(1, rows_t)

    packed = pl.pallas_call(
        pack_kernel,
        out_shape=jax.ShapeDtypeStruct((slots + 2, excitations, shard_len), jnp.bfloat16),
        in_specs=[VMEM, SMEM, SMEM, VMEM, VMEM, VMEM],
        out_specs=VMEM,
        compiler_params=PARAMS,
    )(history, shell, near_mask, gram_diag, gram_off, neighbours)
    packed = lax.all_gather(packed, "row", axis=2, tiled=True)

    parts = pl.pallas_call(
        functools.partial(t_kernel, norm=norm, slots=slots),
        out_shape=jax.ShapeDtypeStruct((col_devices, excitations, rows_t + LANES), jnp.bfloat16),
        in_specs=[VMEM, VMEM, VMEM, SMEM, SMEM],
        out_specs=VMEM,
        scratch_shapes=[
            pltpu.VMEM((slots + 2, moments.shape[0] * excitations, cols_t), jnp.bfloat16),
            pltpu.VMEM((3, cols_t, LANES), jnp.float32),
            pltpu.VMEM((cols_t, LANES), jnp.bfloat16),
        ],
        compiler_params=PARAMS,
    )(packed, centroids, moments, shell, near_mask)
    parts, late_centroids = lax.optimization_barrier((parts, centroids))
    parts = lax.all_to_all(parts, "col", 0, 0)

    entries = rows_t * cols_t
    s_tiles = pl.pallas_call(
        s_tiles_kernel,
        out_shape=jax.ShapeDtypeStruct((rows_t, cols_t), jnp.bfloat16),
        in_specs=[VMEM],
        out_specs=VMEM,
        scratch_shapes=[pltpu.VMEM((3, LANES, LANES), jnp.float32)],
        compiler_params=PARAMS,
        cost_estimate=pl.CostEstimate(flops=12 * entries, bytes_accessed=2 * entries, transcendentals=2 * entries),
    )(late_centroids)

    own_dual, potential = pl.pallas_call(
        functools.partial(sweep_kernel, slots=slots),
        out_shape=(
            jax.ShapeDtypeStruct((excitations, shard_len), jnp.float32),
            jax.ShapeDtypeStruct((q_tiles, excitations, LANES), jnp.bfloat16),
        ),
        in_specs=[VMEM] * 7,
        out_specs=(VMEM, VMEM),
        scratch_shapes=[
            pltpu.VMEM((p_tiles, excitations, LANES), jnp.float32),
            pltpu.VMEM((dual_moments.shape[0] * excitations, rows_t), jnp.bfloat16),
        ],
        compiler_params=PARAMS,
    )(parts, packed, gram_diag, gram_off, neighbours, s_tiles, dual_moments)
    shares = lax.all_gather(potential, "row", axis=2, tiled=True)
    march_rhs = pl.pallas_call(
        functools.partial(final_kernel, norm=norm),
        out_shape=jax.ShapeDtypeStruct(incident.shape, jnp.float32),
        in_specs=[VMEM, VMEM],
        out_specs=VMEM,
        compiler_params=PARAMS,
    )(shares, incident)
    return (march_rhs, own_dual)


def solution(mesh):
    placed = (
        P(None, None, ("col", "row")),
        P(None, ("col", "row")),
        P(),
        P(),
        P(),
        P("row", "col"),
        P("row", "col"),
        P(None, "row"),
        P("row"),
        P(None, "row"),
    )
    return jax.shard_map(
        per_device,
        mesh=mesh,
        in_specs=placed,
        out_specs=(P(None, ("col", "row")), P(None, ("row", "col"))),
        check_vma=False,
    )
```

```python
import functools
import math

import jax
import jax.numpy as jnp
from jax import lax
from jax.experimental import pallas as pl
from jax.experimental.pallas import tpu as pltpu
from jax.sharding import PartitionSpec as P

SWEEPS = 2

SOFT_T = 0.05
SOFT_S = 0.1
NEAR_GAIN = 2.0
NEAR_REACH = 0.5

LANES = 128
HALF = LANES // 2
CHUNK = 64

VMEM = pl.BlockSpec(memory_space=pltpu.VMEM)
SMEM = pl.BlockSpec(memory_space=pltpu.SMEM)
LOG2_E = 1.4426950408889634
TINY = 1e-30
MIB = 1024 * 1024


def grant(*shapes):
    total = 0
    for shape in shapes:
        size = 4
        for extent in shape[:-2] + (-(-shape[-2] // 8) * 8, shape[-1]):
            size *= extent
        total += size
    return pltpu.CompilerParams(vmem_limit_bytes=min(56 * MIB, 2 * total + 2 * MIB))


def root(square):
    square = jnp.maximum(square, TINY)
    return square * lax.rsqrt(square)


def inverse(value):
    return pl.reciprocal(value, approx=True)


def lane_ids(rows=1):
    return lax.broadcasted_iota(jnp.int32, (rows, LANES), 1)


def tile_at(start):
    return pl.ds(pl.multiple_of(start, LANES), LANES)


def edges(ref, row, length):
    first = ref[row : row + 1, :LANES]
    last = ref[row : row + 1, length - LANES :]
    return jnp.where(lane_ids() < HALF, first, last)


def split3(value):
    high = value.astype(jnp.bfloat16).astype(jnp.float32)
    rest = value - high
    middle = rest.astype(jnp.bfloat16).astype(jnp.float32)
    return [high, middle, rest - middle]


def stack_rows(rows, height):
    row_ids = lax.broadcasted_iota(jnp.int32, (height, LANES), 0)
    out = jnp.zeros((height, LANES), jnp.float32)
    for position, row in enumerate(rows):
        out = jnp.where(row_ids == position, row, out)
    return out


def pack_kernel(history_ref, shell_ref, near_ref, diag_ref, off_ref, links_ref, out_ref):
    slots, excitations = history_ref.shape[:2]
    length = diag_ref.shape[1]
    tiles = shell_ref.shape[1]
    lanes = lane_ids()
    rows = []
    for tile in (0, tiles - 1):
        code = jnp.zeros((1, LANES), jnp.float32)
        for j in range(shell_ref.shape[0]):
            value = (shell_ref[j, tile] + slots * near_ref[j, tile]).astype(jnp.float32)
            code = jnp.where(lanes == j, value, code)
        rows.append(code)
    here = lax.axis_index("row") * length + jnp.where(lanes < HALF, lanes, length - LANES + lanes)
    for m in range(links_ref.shape[0]):
        rows.append((edges(links_ref, m, length) - here).astype(jnp.float32))
    rows += split3(edges(diag_ref, 0, length))
    coupling = []
    for m in range(off_ref.shape[0]):
        coupling += split3(edges(off_ref, m, length))
    out_ref[:slots] = history_ref[...]
    out_ref[slots] = stack_rows(rows, excitations).astype(jnp.bfloat16)
    out_ref[slots + 1] = stack_rows(coupling, excitations).astype(jnp.bfloat16)


def halo_row(packed_ref, row_count, plane, row):
    me = lax.axis_index("row")
    right = lax.rem(me + 1, row_count)
    left = lax.rem(me + row_count - 1, row_count)
    right_row = packed_ref[plane, :, tile_at(right * LANES)].astype(jnp.float32)[row : row + 1]
    left_row = packed_ref[plane, :, tile_at(left * LANES)].astype(jnp.float32)[row : row + 1]
    return right_row, left_row


def column_coords(centroids_ref, start, store):
    for axis in range(3):
        line = centroids_ref[axis : axis + 1, tile_at(start)]
        store(axis, jnp.broadcast_to(line, (LANES, LANES)).T)


def t_kernel(
    packed_ref, centroids_ref, moments_ref, shell_ref, near_ref, out_ref, scaled_ref, column_ref, tile_ref, norm, slots
):
    q_tiles, p_tiles = shell_ref.shape
    row_count = packed_ref.shape[2] // LANES
    excitations = packed_ref.shape[1]
    kinds = moments_ref.shape[0]
    total = centroids_ref.shape[1]
    length = p_tiles * LANES
    row_start = lax.axis_index("row") * length
    col_start = lax.axis_index("col") * (q_tiles * LANES)
    low = lane_ids() < HALF

    code_right, code_left = halo_row(packed_ref, row_count, slots, 0)[0], halo_row(packed_ref, row_count, slots, 1)[1]
    near_right = jnp.where(code_right >= slots, 1.0, 0.0)
    near_left = jnp.where(code_left >= slots, 1.0, 0.0)
    slot_right = code_right - slots * near_right
    slot_left = code_left - slots * near_left

    for j in range(q_tiles):
        lanes = slice(j * LANES, (j + 1) * LANES)
        weights = [moments_ref[a : a + 1, tile_at(col_start + j * LANES)] for a in range(kinds)]
        picked = [packed_ref[s, :, lanes].astype(jnp.float32) for s in range(slots)]
        for code in (slot_right, slot_left):
            choice = jnp.broadcast_to(code[:, j : j + 1], (excitations, LANES))
            value = picked[0]
            for s in range(1, slots):
                value = jnp.where(choice == s, picked[s], value)
            picked.append(value)
        for s, value in enumerate(picked):
            for a in range(kinds):
                scaled_ref[s, a * excitations : (a + 1) * excitations, lanes] = (weights[a] * value).astype(jnp.bfloat16)

        def store(axis, value, j=j):
            column_ref[axis, j * LANES : (j + 1) * LANES, :] = value

        column_coords(centroids_ref, col_start + j * LANES, store)

    def fill(slot, line, gain_of):
        for j in range(q_tiles):
            gain = gain_of(j)
            for k in range(LANES // CHUNK):
                at = slice(j * LANES + k * CHUNK, j * LANES + (k + 1) * CHUNK)
                dx = line[0] - column_ref[0, at, :]
                dy = line[1] - column_ref[1, at, :]
                dz = line[2] - column_ref[2, at, :]
                spacing = root(dx * dx + dy * dy + dz * dz)
                tile_ref[slot, at, :] = (
                    inverse(spacing + SOFT_T) + gain * jnp.exp2(spacing * (-LOG2_E / NEAR_REACH))
                ).astype(jnp.bfloat16)

    def products(slot, lhs):
        return jnp.dot(lhs, tile_ref[slot], preferred_element_type=jnp.float32)

    def weighted(product, weights):
        field = weights[0] * product[:excitations]
        for a in range(1, kinds):
            term = weights[a] * product[a * excitations : (a + 1) * excitations]
            field = field + term if a < kinds - 1 else field - term
        return (field * norm).astype(jnp.bfloat16)

    group = max(1, 16 // q_tiles)
    while p_tiles % group:
        group -= 1

    def one_group(g, carry):
        for k in range(group):
            t = g * group + k
            start = row_start + t * LANES
            line = [centroids_ref[axis : axis + 1, tile_at(start)] for axis in range(3)]
            fill(k % 2, line, lambda j: NEAR_GAIN * near_ref[j, t].astype(jnp.float32))
            lhs = jnp.concatenate(
                [scaled_ref[shell_ref[j, t], :, j * LANES : (j + 1) * LANES] for j in range(q_tiles)], axis=1
            )
            weights = [moments_ref[a : a + 1, tile_at(start)] for a in range(kinds)]
            out_ref[:, tile_at(t * LANES)] = weighted(products(k % 2, lhs), weights)
        return carry

    lax.fori_loop(0, p_tiles // group, one_group, 0)

    right_start = lax.rem(row_start + length, total)
    left_start = lax.rem(row_start + total - LANES, total)

    def halo(ref, row):
        return jnp.where(low, ref[row : row + 1, tile_at(right_start)], ref[row : row + 1, tile_at(left_start)])

    gains = NEAR_GAIN * jnp.where(low, 1.0, 0.0), NEAR_GAIN * jnp.where(low, 0.0, 1.0)
    fill(
        0,
        [halo(centroids_ref, axis) for axis in range(3)],
        lambda j: gains[0] * near_right[:, j : j + 1] + gains[1] * near_left[:, j : j + 1],
    )
    product = jnp.where(low, products(0, scaled_ref[slots]), products(0, scaled_ref[slots + 1]))
    out_ref[:, length:] = weighted(product, [halo(moments_ref, a) for a in range(kinds)])


def s_tiles_kernel(centroids_ref, out_ref, column_ref):
    length, width = out_ref.shape
    row_start = lax.axis_index("row") * length
    col_start = lax.axis_index("col") * width

    def one_tile(t, carry):
        def store(axis, value):
            column_ref[axis] = value

        column_coords(centroids_ref, row_start + t * LANES, store)
        for k in range(width // LANES):
            line = [centroids_ref[axis : axis + 1, tile_at(col_start + k * LANES)] for axis in range(3)]
            for piece in range(LANES // CHUNK):
                at = slice(piece * CHUNK, (piece + 1) * CHUNK)
                dx = line[0] - column_ref[0, at, :]
                dy = line[1] - column_ref[1, at, :]
                dz = line[2] - column_ref[2, at, :]
                spacing = root(dx * dx + dy * dy + dz * dz)
                rows = pl.ds(pl.multiple_of(t * LANES + piece * CHUNK, CHUNK), CHUNK)
                out_ref[rows, k * LANES : (k + 1) * LANES] = inverse(spacing + SOFT_S).astype(jnp.bfloat16)
        return carry

    lax.fori_loop(0, length // LANES, one_tile, 0)


def sweep_kernel(
    parts_ref, packed_ref, diag_ref, off_ref, links_ref, tiles_ref, dual_moments_ref, dual_ref, out_ref, iter_ref, scaled_ref, slots
):
    length = diag_ref.shape[1]
    tiles = length // LANES
    row_count = packed_ref.shape[2] // LANES
    excitations = parts_ref.shape[1]
    link_count = links_ref.shape[0]
    kinds = dual_moments_ref.shape[0]
    row_start = lax.axis_index("row") * length
    col_start = lax.axis_index("col") * tiles_ref.shape[1]
    lanes = lane_ids()
    low = lanes < HALF

    def halo(plane, row):
        return jnp.where(low, *halo_row(packed_ref, row_count, plane, row))

    def sum3(plane, row):
        return halo(plane, row) + halo(plane, row + 1) + halo(plane, row + 2)

    def tile(t):
        return slice(t * LANES, (t + 1) * LANES)

    field, diag = [], []
    for t in range(tiles + 1):
        total = parts_ref[0, :, tile(t)].astype(jnp.float32)
        for c in range(1, parts_ref.shape[0]):
            total = total + parts_ref[c, :, tile(t)].astype(jnp.float32)
        field.append(total)
        diag.append(diag_ref[:, tile(t)] if t < tiles else sum3(slots, 2 + link_count))

    dual = [f / d for f, d in zip(field, diag)]
    for sweep_id in range(SWEEPS):
        last = sweep_id == SWEEPS - 1
        updated = []
        for t in range(tiles if last else tiles + 1):
            around = jnp.where(low, dual[(t + 1) % (tiles + 1)], dual[t - 1])
            coupled = jnp.zeros_like(field[t])
            for m in range(link_count):
                if t < tiles:
                    source = links_ref[m : m + 1, tile(t)] - (row_start + t * LANES)
                    gram = off_ref[m : m + 1, tile(t)]
                else:
                    source = halo(slots, 2 + m).astype(jnp.int32) + lanes
                    gram = sum3(slots + 1, 3 * m)
                inside = (source >= 0) & (source < LANES)
                index = jnp.broadcast_to(source & (LANES - 1), (excitations, LANES))
                here = jnp.take_along_axis(dual[t], index, axis=1)
                beside = jnp.take_along_axis(around, index, axis=1)
                coupled = coupled + gram * jnp.where(inside, here, beside)
            updated.append((field[t] - coupled) / diag[t])
        dual = updated

    for t in range(tiles):
        iter_ref[t] = dual[t]
        for a in range(kinds):
            weight = dual_moments_ref[a : a + 1, tile_at(row_start + t * LANES)]
            scaled_ref[a * excitations : (a + 1) * excitations, tile(t)] = (weight * dual[t]).astype(jnp.bfloat16)
    dual_ref[...] = iter_ref[lax.axis_index("col")]
    product = jnp.dot(scaled_ref[...], tiles_ref[...], preferred_element_type=jnp.float32)
    for k in range(out_ref.shape[0]):
        term = jnp.zeros((excitations, LANES), jnp.float32)
        for a in range(kinds):
            weight = dual_moments_ref[a : a + 1, tile_at(col_start + k * LANES)]
            term = term + weight * product[a * excitations : (a + 1) * excitations, tile(k)]
        out_ref[k] = term.astype(jnp.bfloat16)


def per_device(
    history,
    incident,
    centroids,
    moments,
    dual_moments,
    shell,
    near_mask,
    neighbours,
    gram_diag,
    gram_off,
):
    slots, excitations, shard_len = history.shape
    p_tiles, q_tiles = shell.shape
    rows_t = gram_diag.shape[0]
    cols_t = q_tiles * LANES
    norm = 1.0 / math.sqrt(centroids.shape[1])
    shell, near_mask = shell.T, near_mask.T
    gram_diag = gram_diag.reshape(1, rows_t)

    packed = pl.pallas_call(
        pack_kernel,
        out_shape=jax.ShapeDtypeStruct((slots + 2, excitations, shard_len), jnp.bfloat16),
        in_specs=[VMEM, SMEM, SMEM, VMEM, VMEM, VMEM],
        out_specs=VMEM,
        compiler_params=grant(history.shape, gram_diag.shape, gram_off.shape, neighbours.shape),
    )(history, shell, near_mask, gram_diag, gram_off, neighbours)
    packed = lax.all_gather(packed, "row", axis=2, tiled=True)

    parts = pl.pallas_call(
        functools.partial(t_kernel, norm=norm, slots=slots),
        out_shape=jax.ShapeDtypeStruct((excitations, rows_t + LANES), jnp.bfloat16),
        in_specs=[VMEM, VMEM, VMEM, SMEM, SMEM],
        out_specs=VMEM,
        scratch_shapes=[
            pltpu.VMEM((slots + 2, moments.shape[0] * excitations, cols_t), jnp.bfloat16),
            pltpu.VMEM((3, cols_t, LANES), jnp.float32),
            pltpu.VMEM((2, cols_t, LANES), jnp.bfloat16),
        ],
        compiler_params=grant((excitations, rows_t), (slots + 2, moments.shape[0] * excitations, cols_t), (5, cols_t, LANES), moments.shape, centroids.shape),
    )(packed, centroids, moments, shell, near_mask)
    parts, late_centroids = lax.optimization_barrier((parts, centroids))
    parts = lax.all_gather(parts, "col")

    entries = rows_t * cols_t
    s_tiles = pl.pallas_call(
        s_tiles_kernel,
        out_shape=jax.ShapeDtypeStruct((rows_t, cols_t), jnp.bfloat16),
        in_specs=[VMEM],
        out_specs=VMEM,
        scratch_shapes=[pltpu.VMEM((3, LANES, LANES), jnp.float32)],
        compiler_params=grant((rows_t, cols_t // 2), centroids.shape),
        cost_estimate=pl.CostEstimate(flops=12 * entries, bytes_accessed=2 * entries, transcendentals=2 * entries),
    )(late_centroids)

    own_dual, potential = pl.pallas_call(
        functools.partial(sweep_kernel, slots=slots),
        out_shape=(
            jax.ShapeDtypeStruct((excitations, shard_len), jnp.float32),
            jax.ShapeDtypeStruct((q_tiles, excitations, LANES), jnp.bfloat16),
        ),
        in_specs=[VMEM] * 7,
        out_specs=(VMEM, VMEM),
        scratch_shapes=[
            pltpu.VMEM((p_tiles, excitations, LANES), jnp.float32),
            pltpu.VMEM((dual_moments.shape[0] * excitations, rows_t), jnp.bfloat16),
        ],
        compiler_params=grant(parts.shape, (rows_t, cols_t // 2), (excitations, 8 * rows_t)),
    )(parts, packed, gram_diag, gram_off, neighbours, s_tiles, dual_moments)
    shares = lax.all_gather(potential, "row")
    share = lax.dynamic_index_in_dim(shares, lax.axis_index("row"), 1, keepdims=False)
    march_rhs = incident - jnp.sum(share.astype(jnp.float32), axis=0) * norm
    return (march_rhs, own_dual)


def solution(mesh):
    placed = (
        P(None, None, ("col", "row")),
        P(None, ("col", "row")),
        P(),
        P(),
        P(),
        P("row", "col"),
        P("row", "col"),
        P(None, "row"),
        P("row"),
        P(None, "row"),
    )
    return jax.shard_map(
        per_device,
        mesh=mesh,
        in_specs=placed,
        out_specs=(P(None, ("col", "row")), P(None, ("row", "col"))),
        check_vma=False,
    )
```

```python
import functools
import math

import jax
import jax.numpy as jnp
from jax import lax
from jax.experimental import pallas as pl
from jax.experimental.pallas import tpu as pltpu
from jax.sharding import PartitionSpec as P

SWEEPS = 2

SOFT_T = 0.05
SOFT_S = 0.1
NEAR_GAIN = 2.0
NEAR_REACH = 0.5

LANES = 128
HALF = LANES // 2
CHUNK = 64

VMEM = pl.BlockSpec(memory_space=pltpu.VMEM)
SMEM = pl.BlockSpec(memory_space=pltpu.SMEM)
LOG2_E = 1.4426950408889634
TINY = 1e-30
MIB = 1024 * 1024


def grant(*shapes):
    total = 0
    for shape in shapes:
        size = 4
        for extent in shape[:-2] + (-(-shape[-2] // 8) * 8, shape[-1]):
            size *= extent
        total += size
    return pltpu.CompilerParams(vmem_limit_bytes=min(56 * MIB, 2 * total + 2 * MIB))


def root(square):
    square = jnp.maximum(square, TINY)
    return square * lax.rsqrt(square)


def inverse(value):
    return pl.reciprocal(value, approx=True)


def lane_ids(rows=1):
    return lax.broadcasted_iota(jnp.int32, (rows, LANES), 1)


def tile_at(start):
    return pl.ds(pl.multiple_of(start, LANES), LANES)


def edges(ref, row, length):
    first = ref[row : row + 1, :LANES]
    last = ref[row : row + 1, length - LANES :]
    return jnp.where(lane_ids() < HALF, first, last)


def split3(value):
    high = value.astype(jnp.bfloat16).astype(jnp.float32)
    rest = value - high
    middle = rest.astype(jnp.bfloat16).astype(jnp.float32)
    return [high, middle, rest - middle]


def stack_rows(rows, height):
    row_ids = lax.broadcasted_iota(jnp.int32, (height, LANES), 0)
    out = jnp.zeros((height, LANES), jnp.float32)
    for position, row in enumerate(rows):
        out = jnp.where(row_ids == position, row, out)
    return out


def pack_kernel(history_ref, shell_ref, near_ref, diag_ref, off_ref, links_ref, out_ref):
    slots, excitations = history_ref.shape[:2]
    length = diag_ref.shape[1]
    tiles = shell_ref.shape[1]
    lanes = lane_ids()
    rows = []
    for tile in (0, tiles - 1):
        code = jnp.zeros((1, LANES), jnp.float32)
        for j in range(shell_ref.shape[0]):
            value = (shell_ref[j, tile] + slots * near_ref[j, tile]).astype(jnp.float32)
            code = jnp.where(lanes == j, value, code)
        rows.append(code)
    here = lax.axis_index("row") * length + jnp.where(lanes < HALF, lanes, length - LANES + lanes)
    for m in range(links_ref.shape[0]):
        rows.append((edges(links_ref, m, length) - here).astype(jnp.float32))
    rows += split3(edges(diag_ref, 0, length))
    coupling = []
    for m in range(off_ref.shape[0]):
        coupling += split3(edges(off_ref, m, length))
    out_ref[:slots] = history_ref[...]
    out_ref[slots] = stack_rows(rows, excitations).astype(jnp.bfloat16)
    out_ref[slots + 1] = stack_rows(coupling, excitations).astype(jnp.bfloat16)


def halo_row(packed_ref, row_count, plane, row):
    me = lax.axis_index("row")
    right = lax.rem(me + 1, row_count)
    left = lax.rem(me + row_count - 1, row_count)
    right_row = packed_ref[plane, :, tile_at(right * LANES)].astype(jnp.float32)[row : row + 1]
    left_row = packed_ref[plane, :, tile_at(left * LANES)].astype(jnp.float32)[row : row + 1]
    return right_row, left_row


def column_coords(centroids_ref, start, store):
    for axis in range(3):
        line = centroids_ref[axis : axis + 1, tile_at(start)]
        store(axis, jnp.broadcast_to(line, (LANES, LANES)).T)


def t_kernel(
    packed_ref, centroids_ref, moments_ref, shell_ref, near_ref, out_ref, scaled_ref, column_ref, tile_ref, norm, slots
):
    q_tiles, p_tiles = shell_ref.shape
    row_count = packed_ref.shape[2] // LANES
    excitations = packed_ref.shape[1]
    kinds = moments_ref.shape[0]
    total = centroids_ref.shape[1]
    length = p_tiles * LANES
    row_start = lax.axis_index("row") * length
    col_start = lax.axis_index("col") * (q_tiles * LANES)
    low = lane_ids() < HALF

    code_right, code_left = halo_row(packed_ref, row_count, slots, 0)[0], halo_row(packed_ref, row_count, slots, 1)[1]
    near_right = jnp.where(code_right >= slots, 1.0, 0.0)
    near_left = jnp.where(code_left >= slots, 1.0, 0.0)
    slot_right = code_right - slots * near_right
    slot_left = code_left - slots * near_left

    for j in range(q_tiles):
        lanes = slice(j * LANES, (j + 1) * LANES)
        weights = [moments_ref[a : a + 1, tile_at(col_start + j * LANES)] for a in range(kinds)]
        picked = [packed_ref[s, :, lanes].astype(jnp.float32) for s in range(slots)]
        for code in (slot_right, slot_left):
            choice = jnp.broadcast_to(code[:, j : j + 1], (excitations, LANES))
            value = picked[0]
            for s in range(1, slots):
                value = jnp.where(choice == s, picked[s], value)
            picked.append(value)
        for s, value in enumerate(picked):
            for a in range(kinds):
                scaled_ref[s, a * excitations : (a + 1) * excitations, lanes] = (weights[a] * value).astype(jnp.bfloat16)

        def store(axis, value, j=j):
            column_ref[axis, j * LANES : (j + 1) * LANES, :] = value

        column_coords(centroids_ref, col_start + j * LANES, store)

    def fill(slot, line, gain_of):
        for j in range(q_tiles):
            gain = gain_of(j)
            for k in range(LANES // CHUNK):
                at = slice(j * LANES + k * CHUNK, j * LANES + (k + 1) * CHUNK)
                dx = line[0] - column_ref[0, at, :]
                dy = line[1] - column_ref[1, at, :]
                dz = line[2] - column_ref[2, at, :]
                spacing = root(dx * dx + dy * dy + dz * dz)
                tile_ref[slot, at, :] = (
                    inverse(spacing + SOFT_T) + gain * jnp.exp2(spacing * (-LOG2_E / NEAR_REACH))
                ).astype(jnp.bfloat16)

    def products(slot, lhs):
        return jnp.dot(lhs, tile_ref[slot], preferred_element_type=jnp.float32)

    def weighted(product, weights):
        field = weights[0] * product[:excitations]
        for a in range(1, kinds):
            term = weights[a] * product[a * excitations : (a + 1) * excitations]
            field = field + term if a < kinds - 1 else field - term
        return (field * norm).astype(jnp.bfloat16)

    def emit(lanes, field):
        for copy in range(out_ref.shape[0]):
            out_ref[copy, :, lanes] = field

    group = max(1, 16 // q_tiles)
    while p_tiles % group:
        group -= 1

    def one_group(g, carry):
        for k in range(group):
            t = g * group + k
            start = row_start + t * LANES
            line = [centroids_ref[axis : axis + 1, tile_at(start)] for axis in range(3)]
            fill(k % 2, line, lambda j: NEAR_GAIN * near_ref[j, t].astype(jnp.float32))
            lhs = jnp.concatenate(
                [scaled_ref[shell_ref[j, t], :, j * LANES : (j + 1) * LANES] for j in range(q_tiles)], axis=1
            )
            weights = [moments_ref[a : a + 1, tile_at(start)] for a in range(kinds)]
            emit(tile_at(t * LANES), weighted(products(k % 2, lhs), weights))
        return carry

    lax.fori_loop(0, p_tiles // group, one_group, 0)

    right_start = lax.rem(row_start + length, total)
    left_start = lax.rem(row_start + total - LANES, total)

    def halo(ref, row):
        return jnp.where(low, ref[row : row + 1, tile_at(right_start)], ref[row : row + 1, tile_at(left_start)])

    gains = NEAR_GAIN * jnp.where(low, 1.0, 0.0), NEAR_GAIN * jnp.where(low, 0.0, 1.0)
    fill(
        0,
        [halo(centroids_ref, axis) for axis in range(3)],
        lambda j: gains[0] * near_right[:, j : j + 1] + gains[1] * near_left[:, j : j + 1],
    )
    product = jnp.where(low, products(0, scaled_ref[slots]), products(0, scaled_ref[slots + 1]))
    emit(slice(length, length + LANES), weighted(product, [halo(moments_ref, a) for a in range(kinds)]))


def s_tiles_kernel(centroids_ref, out_ref, column_ref):
    length, width = out_ref.shape
    row_start = lax.axis_index("row") * length
    col_start = lax.axis_index("col") * width

    def one_tile(t, carry):
        def store(axis, value):
            column_ref[axis] = value

        column_coords(centroids_ref, row_start + t * LANES, store)
        for k in range(width // LANES):
            line = [centroids_ref[axis : axis + 1, tile_at(col_start + k * LANES)] for axis in range(3)]
            for piece in range(LANES // CHUNK):
                at = slice(piece * CHUNK, (piece + 1) * CHUNK)
                dx = line[0] - column_ref[0, at, :]
                dy = line[1] - column_ref[1, at, :]
                dz = line[2] - column_ref[2, at, :]
                spacing = root(dx * dx + dy * dy + dz * dz)
                rows = pl.ds(pl.multiple_of(t * LANES + piece * CHUNK, CHUNK), CHUNK)
                out_ref[rows, k * LANES : (k + 1) * LANES] = inverse(spacing + SOFT_S).astype(jnp.bfloat16)
        return carry

    lax.fori_loop(0, length // LANES, one_tile, 0)


def sweep_kernel(
    parts_ref, packed_ref, diag_ref, off_ref, links_ref, tiles_ref, dual_moments_ref, dual_ref, out_ref, iter_ref, scaled_ref, slots
):
    length = diag_ref.shape[1]
    tiles = length // LANES
    row_count = packed_ref.shape[2] // LANES
    excitations = parts_ref.shape[1]
    link_count = links_ref.shape[0]
    kinds = dual_moments_ref.shape[0]
    row_start = lax.axis_index("row") * length
    col_start = lax.axis_index("col") * tiles_ref.shape[1]
    lanes = lane_ids()
    low = lanes < HALF

    def halo(plane, row):
        return jnp.where(low, *halo_row(packed_ref, row_count, plane, row))

    def sum3(plane, row):
        return halo(plane, row) + halo(plane, row + 1) + halo(plane, row + 2)

    def tile(t):
        return slice(t * LANES, (t + 1) * LANES)

    field, diag = [], []
    for t in range(tiles + 1):
        total = parts_ref[0, :, tile(t)].astype(jnp.float32)
        for c in range(1, parts_ref.shape[0]):
            total = total + parts_ref[c, :, tile(t)].astype(jnp.float32)
        field.append(total)
        diag.append(diag_ref[:, tile(t)] if t < tiles else sum3(slots, 2 + link_count))

    dual = [f / d for f, d in zip(field, diag)]
    for sweep_id in range(SWEEPS):
        last = sweep_id == SWEEPS - 1
        updated = []
        for t in range(tiles if last else tiles + 1):
            around = jnp.where(low, dual[(t + 1) % (tiles + 1)], dual[t - 1])
            coupled = jnp.zeros_like(field[t])
            for m in range(link_count):
                if t < tiles:
                    source = links_ref[m : m + 1, tile(t)] - (row_start + t * LANES)
                    gram = off_ref[m : m + 1, tile(t)]
                else:
                    source = halo(slots, 2 + m).astype(jnp.int32) + lanes
                    gram = sum3(slots + 1, 3 * m)
                inside = (source >= 0) & (source < LANES)
                index = jnp.broadcast_to(source & (LANES - 1), (excitations, LANES))
                here = jnp.take_along_axis(dual[t], index, axis=1)
                beside = jnp.take_along_axis(around, index, axis=1)
                coupled = coupled + gram * jnp.where(inside, here, beside)
            updated.append((field[t] - coupled) / diag[t])
        dual = updated

    for t in range(tiles):
        iter_ref[t] = dual[t]
        for a in range(kinds):
            weight = dual_moments_ref[a : a + 1, tile_at(row_start + t * LANES)]
            scaled_ref[a * excitations : (a + 1) * excitations, tile(t)] = (weight * dual[t]).astype(jnp.bfloat16)
    dual_ref[...] = iter_ref[lax.axis_index("col")]
    product = jnp.dot(scaled_ref[...], tiles_ref[...], preferred_element_type=jnp.float32)
    for k in range(out_ref.shape[0]):
        term = jnp.zeros((excitations, LANES), jnp.float32)
        for a in range(kinds):
            weight = dual_moments_ref[a : a + 1, tile_at(col_start + k * LANES)]
            term = term + weight * product[a * excitations : (a + 1) * excitations, tile(k)]
        out_ref[k] = term.astype(jnp.bfloat16)


def final_kernel(shares_ref, incident_ref, out_ref, norm):
    me = lax.axis_index("row")
    total = shares_ref[0, me].astype(jnp.float32)
    for share in range(1, shares_ref.shape[0]):
        total = total + shares_ref[share, me].astype(jnp.float32)
    out_ref[...] = incident_ref[...] - total * norm


def per_device(
    history,
    incident,
    centroids,
    moments,
    dual_moments,
    shell,
    near_mask,
    neighbours,
    gram_diag,
    gram_off,
):
    col_devices = lax.axis_size("col")
    slots, excitations, shard_len = history.shape
    p_tiles, q_tiles = shell.shape
    rows_t = gram_diag.shape[0]
    cols_t = q_tiles * LANES
    norm = 1.0 / math.sqrt(centroids.shape[1])
    shell, near_mask = shell.T, near_mask.T
    gram_diag = gram_diag.reshape(1, rows_t)

    packed = pl.pallas_call(
        pack_kernel,
        out_shape=jax.ShapeDtypeStruct((slots + 2, excitations, shard_len), jnp.bfloat16),
        in_specs=[VMEM, SMEM, SMEM, VMEM, VMEM, VMEM],
        out_specs=VMEM,
        compiler_params=pltpu.CompilerParams(vmem_limit_bytes=56 * MIB),
    )(history, shell, near_mask, gram_diag, gram_off, neighbours)
    packed = lax.all_gather(packed, "row", axis=2, tiled=True)

    parts = pl.pallas_call(
        functools.partial(t_kernel, norm=norm, slots=slots),
        out_shape=jax.ShapeDtypeStruct((col_devices, excitations, rows_t + LANES), jnp.bfloat16),
        in_specs=[VMEM, VMEM, VMEM, SMEM, SMEM],
        out_specs=VMEM,
        scratch_shapes=[
            pltpu.VMEM((slots + 2, moments.shape[0] * excitations, cols_t), jnp.bfloat16),
            pltpu.VMEM((3, cols_t, LANES), jnp.float32),
            pltpu.VMEM((2, cols_t, LANES), jnp.bfloat16),
        ],
        compiler_params=grant((col_devices, excitations, rows_t // 2), (slots + 2, moments.shape[0] * excitations, cols_t), (5, cols_t, LANES), moments.shape, centroids.shape),
    )(packed, centroids, moments, shell, near_mask)
    parts, late_centroids = lax.optimization_barrier((parts, centroids))
    parts = lax.all_to_all(parts, "col", 0, 0)

    entries = rows_t * cols_t
    s_tiles = pl.pallas_call(
        s_tiles_kernel,
        out_shape=jax.ShapeDtypeStruct((rows_t, cols_t), jnp.bfloat16),
        in_specs=[VMEM],
        out_specs=VMEM,
        scratch_shapes=[pltpu.VMEM((3, LANES, LANES), jnp.float32)],
        compiler_params=grant((rows_t, cols_t // 2), centroids.shape),
        cost_estimate=pl.CostEstimate(flops=12 * entries, bytes_accessed=2 * entries, transcendentals=2 * entries),
    )(late_centroids)

    own_dual, potential = pl.pallas_call(
        functools.partial(sweep_kernel, slots=slots),
        out_shape=(
            jax.ShapeDtypeStruct((excitations, shard_len), jnp.float32),
            jax.ShapeDtypeStruct((q_tiles, excitations, LANES), jnp.bfloat16),
        ),
        in_specs=[VMEM] * 7,
        out_specs=(VMEM, VMEM),
        scratch_shapes=[
            pltpu.VMEM((p_tiles, excitations, LANES), jnp.float32),
            pltpu.VMEM((dual_moments.shape[0] * excitations, rows_t), jnp.bfloat16),
        ],
        compiler_params=grant(parts.shape, (rows_t, cols_t // 2), (excitations, 8 * rows_t)),
    )(parts, packed, gram_diag, gram_off, neighbours, s_tiles, dual_moments)
    shares = lax.all_gather(potential, "row")
    march_rhs = pl.pallas_call(
        functools.partial(final_kernel, norm=norm),
        out_shape=jax.ShapeDtypeStruct(incident.shape, jnp.float32),
        in_specs=[VMEM, VMEM],
        out_specs=VMEM,
        compiler_params=grant(shares.shape),
    )(shares, incident)
    return (march_rhs, own_dual)


def solution(mesh):
    placed = (
        P(None, None, ("col", "row")),
        P(None, ("col", "row")),
        P(),
        P(),
        P(),
        P("row", "col"),
        P("row", "col"),
        P(None, "row"),
        P("row"),
        P(None, "row"),
    )
    return jax.shard_map(
        per_device,
        mesh=mesh,
        in_specs=placed,
        out_specs=(P(None, ("col", "row")), P(None, ("row", "col"))),
        check_vma=False,
    )
```

```python
import functools
import math

import jax
import jax.numpy as jnp
from jax import lax
from jax.experimental import pallas as pl
from jax.experimental.pallas import tpu as pltpu
from jax.sharding import PartitionSpec as P

SWEEPS = 2

SOFT_T = 0.05
SOFT_S = 0.1
NEAR_GAIN = 2.0
NEAR_REACH = 0.5

LANES = 128
HALF = LANES // 2
CHUNK = 64

VMEM = pl.BlockSpec(memory_space=pltpu.VMEM)
SMEM = pl.BlockSpec(memory_space=pltpu.SMEM)
LOG2_E = 1.4426950408889634
TINY = 1e-30
MIB = 1024 * 1024


def grant(*shapes):
    total = 0
    for shape in shapes:
        size = 4
        for extent in shape[:-2] + (-(-shape[-2] // 8) * 8, shape[-1]):
            size *= extent
        total += size
    return pltpu.CompilerParams(vmem_limit_bytes=min(56 * MIB, 2 * total + 2 * MIB))


def root(square):
    square = jnp.maximum(square, TINY)
    return square * lax.rsqrt(square)


def inverse(value):
    return pl.reciprocal(value, approx=True)


def lane_ids(rows=1):
    return lax.broadcasted_iota(jnp.int32, (rows, LANES), 1)


def tile_at(start):
    return pl.ds(pl.multiple_of(start, LANES), LANES)


def edges(ref, row, length):
    first = ref[row : row + 1, :LANES]
    last = ref[row : row + 1, length - LANES :]
    return jnp.where(lane_ids() < HALF, first, last)


def split3(value):
    high = value.astype(jnp.bfloat16).astype(jnp.float32)
    rest = value - high
    middle = rest.astype(jnp.bfloat16).astype(jnp.float32)
    return [high, middle, rest - middle]


def stack_rows(rows, height):
    row_ids = lax.broadcasted_iota(jnp.int32, (height, LANES), 0)
    out = jnp.zeros((height, LANES), jnp.float32)
    for position, row in enumerate(rows):
        out = jnp.where(row_ids == position, row, out)
    return out


def pack_kernel(history_ref, shell_ref, near_ref, diag_ref, off_ref, links_ref, out_ref):
    slots, excitations = history_ref.shape[:2]
    length = diag_ref.shape[1]
    tiles = shell_ref.shape[1]
    lanes = lane_ids()
    rows = []
    for tile in (0, tiles - 1):
        code = jnp.zeros((1, LANES), jnp.float32)
        for j in range(shell_ref.shape[0]):
            value = (shell_ref[j, tile] + slots * near_ref[j, tile]).astype(jnp.float32)
            code = jnp.where(lanes == j, value, code)
        rows.append(code)
    here = lax.axis_index("row") * length + jnp.where(lanes < HALF, lanes, length - LANES + lanes)
    for m in range(links_ref.shape[0]):
        rows.append((edges(links_ref, m, length) - here).astype(jnp.float32))
    rows += split3(edges(diag_ref, 0, length))
    coupling = []
    for m in range(off_ref.shape[0]):
        coupling += split3(edges(off_ref, m, length))
    out_ref[:slots] = history_ref[...]
    out_ref[slots] = stack_rows(rows, excitations).astype(jnp.bfloat16)
    out_ref[slots + 1] = stack_rows(coupling, excitations).astype(jnp.bfloat16)


def halo_row(packed_ref, row_count, plane, row):
    me = lax.axis_index("row")
    right = lax.rem(me + 1, row_count)
    left = lax.rem(me + row_count - 1, row_count)
    right_row = packed_ref[plane, :, tile_at(right * LANES)].astype(jnp.float32)[row : row + 1]
    left_row = packed_ref[plane, :, tile_at(left * LANES)].astype(jnp.float32)[row : row + 1]
    return right_row, left_row


def column_coords(centroids_ref, start, store):
    for axis in range(3):
        line = centroids_ref[axis : axis + 1, tile_at(start)]
        store(axis, jnp.broadcast_to(line, (LANES, LANES)).T)


def t_kernel(
    packed_ref, centroids_ref, moments_ref, shell_ref, near_ref, out_ref, scaled_ref, column_ref, tile_ref, norm, slots
):
    q_tiles, p_tiles = shell_ref.shape
    row_count = packed_ref.shape[2] // LANES
    excitations = packed_ref.shape[1]
    kinds = moments_ref.shape[0]
    total = centroids_ref.shape[1]
    length = p_tiles * LANES
    row_start = lax.axis_index("row") * length
    col_start = lax.axis_index("col") * (q_tiles * LANES)
    low = lane_ids() < HALF

    code_right, code_left = halo_row(packed_ref, row_count, slots, 0)[0], halo_row(packed_ref, row_count, slots, 1)[1]
    near_right = jnp.where(code_right >= slots, 1.0, 0.0)
    near_left = jnp.where(code_left >= slots, 1.0, 0.0)
    slot_right = code_right - slots * near_right
    slot_left = code_left - slots * near_left

    for j in range(q_tiles):
        lanes = slice(j * LANES, (j + 1) * LANES)
        weights = [moments_ref[a : a + 1, tile_at(col_start + j * LANES)] for a in range(kinds)]
        picked = [packed_ref[s, :, lanes].astype(jnp.float32) for s in range(slots)]
        for code in (slot_right, slot_left):
            choice = jnp.broadcast_to(code[:, j : j + 1], (excitations, LANES))
            value = picked[0]
            for s in range(1, slots):
                value = jnp.where(choice == s, picked[s], value)
            picked.append(value)
        for s, value in enumerate(picked):
            for a in range(kinds):
                scaled_ref[s, a * excitations : (a + 1) * excitations, lanes] = (weights[a] * value).astype(jnp.bfloat16)

        def store(axis, value, j=j):
            column_ref[axis, j * LANES : (j + 1) * LANES, :] = value

        column_coords(centroids_ref, col_start + j * LANES, store)

    def fill(slot, line, gain_of):
        for j in range(q_tiles):
            gain = gain_of(j)
            for k in range(LANES // CHUNK):
                at = slice(j * LANES + k * CHUNK, j * LANES + (k + 1) * CHUNK)
                dx = line[0] - column_ref[0, at, :]
                dy = line[1] - column_ref[1, at, :]
                dz = line[2] - column_ref[2, at, :]
                spacing = root(dx * dx + dy * dy + dz * dz)
                tile_ref[slot, at, :] = (
                    inverse(spacing + SOFT_T) + gain * jnp.exp2(spacing * (-LOG2_E / NEAR_REACH))
                ).astype(jnp.bfloat16)

    def products(slot, lhs):
        return jnp.dot(lhs, tile_ref[slot], preferred_element_type=jnp.float32)

    def weighted(product, weights):
        field = weights[0] * product[:excitations]
        for a in range(1, kinds):
            term = weights[a] * product[a * excitations : (a + 1) * excitations]
            field = field + term if a < kinds - 1 else field - term
        return (field * norm).astype(jnp.bfloat16)

    group = max(1, 16 // q_tiles)
    while p_tiles % group:
        group -= 1

    def one_group(g, carry):
        for k in range(group):
            t = g * group + k
            start = row_start + t * LANES
            line = [centroids_ref[axis : axis + 1, tile_at(start)] for axis in range(3)]
            fill(k % 2, line, lambda j: NEAR_GAIN * near_ref[j, t].astype(jnp.float32))
            lhs = jnp.concatenate(
                [scaled_ref[shell_ref[j, t], :, j * LANES : (j + 1) * LANES] for j in range(q_tiles)], axis=1
            )
            weights = [moments_ref[a : a + 1, tile_at(start)] for a in range(kinds)]
            out_ref[:, tile_at(t * LANES)] = weighted(products(k % 2, lhs), weights)
        return carry

    lax.fori_loop(0, p_tiles // group, one_group, 0)

    right_start = lax.rem(row_start + length, total)
    left_start = lax.rem(row_start + total - LANES, total)

    def halo(ref, row):
        return jnp.where(low, ref[row : row + 1, tile_at(right_start)], ref[row : row + 1, tile_at(left_start)])

    gains = NEAR_GAIN * jnp.where(low, 1.0, 0.0), NEAR_GAIN * jnp.where(low, 0.0, 1.0)
    fill(
        0,
        [halo(centroids_ref, axis) for axis in range(3)],
        lambda j: gains[0] * near_right[:, j : j + 1] + gains[1] * near_left[:, j : j + 1],
    )
    product = jnp.where(low, products(0, scaled_ref[slots]), products(0, scaled_ref[slots + 1]))
    out_ref[:, length:] = weighted(product, [halo(moments_ref, a) for a in range(kinds)])


def s_tiles_kernel(centroids_ref, out_ref, column_ref):
    length, width = out_ref.shape
    row_start = lax.axis_index("row") * length
    col_start = lax.axis_index("col") * width

    def one_tile(t, carry):
        def store(axis, value):
            column_ref[axis] = value

        column_coords(centroids_ref, row_start + t * LANES, store)
        for k in range(width // LANES):
            line = [centroids_ref[axis : axis + 1, tile_at(col_start + k * LANES)] for axis in range(3)]
            for piece in range(LANES // CHUNK):
                at = slice(piece * CHUNK, (piece + 1) * CHUNK)
                dx = line[0] - column_ref[0, at, :]
                dy = line[1] - column_ref[1, at, :]
                dz = line[2] - column_ref[2, at, :]
                spacing = root(dx * dx + dy * dy + dz * dz)
                rows = pl.ds(pl.multiple_of(t * LANES + piece * CHUNK, CHUNK), CHUNK)
                out_ref[rows, k * LANES : (k + 1) * LANES] = inverse(spacing + SOFT_S).astype(jnp.bfloat16)
        return carry

    lax.fori_loop(0, length // LANES, one_tile, 0)


def sweep_kernel(*refs, slots, part_count):
    parts = refs[:part_count]
    packed_ref, diag_ref, off_ref, links_ref, tiles_ref, dual_moments_ref = refs[part_count:-4]
    dual_ref, out_ref, iter_ref, scaled_ref = refs[-4:]
    length = diag_ref.shape[1]
    tiles = length // LANES
    row_count = packed_ref.shape[2] // LANES
    excitations = parts[0].shape[0]
    link_count = links_ref.shape[0]
    kinds = dual_moments_ref.shape[0]
    row_start = lax.axis_index("row") * length
    col_start = lax.axis_index("col") * tiles_ref.shape[1]
    lanes = lane_ids()
    low = lanes < HALF

    def halo(plane, row):
        return jnp.where(low, *halo_row(packed_ref, row_count, plane, row))

    def sum3(plane, row):
        return halo(plane, row) + halo(plane, row + 1) + halo(plane, row + 2)

    def tile(t):
        return slice(t * LANES, (t + 1) * LANES)

    field, diag = [], []
    for t in range(tiles + 1):
        total = parts[0][:, tile(t)].astype(jnp.float32)
        for part in parts[1:]:
            total = total + part[:, tile(t)].astype(jnp.float32)
        field.append(total)
        diag.append(diag_ref[:, tile(t)] if t < tiles else sum3(slots, 2 + link_count))

    dual = [f / d for f, d in zip(field, diag)]
    for sweep_id in range(SWEEPS):
        last = sweep_id == SWEEPS - 1
        updated = []
        for t in range(tiles if last else tiles + 1):
            around = jnp.where(low, dual[(t + 1) % (tiles + 1)], dual[t - 1])
            coupled = jnp.zeros_like(field[t])
            for m in range(link_count):
                if t < tiles:
                    source = links_ref[m : m + 1, tile(t)] - (row_start + t * LANES)
                    gram = off_ref[m : m + 1, tile(t)]
                else:
                    source = halo(slots, 2 + m).astype(jnp.int32) + lanes
                    gram = sum3(slots + 1, 3 * m)
                inside = (source >= 0) & (source < LANES)
                index = jnp.broadcast_to(source & (LANES - 1), (excitations, LANES))
                here = jnp.take_along_axis(dual[t], index, axis=1)
                beside = jnp.take_along_axis(around, index, axis=1)
                coupled = coupled + gram * jnp.where(inside, here, beside)
            updated.append((field[t] - coupled) / diag[t])
        dual = updated

    for t in range(tiles):
        iter_ref[t] = dual[t]
        for a in range(kinds):
            weight = dual_moments_ref[a : a + 1, tile_at(row_start + t * LANES)]
            scaled_ref[a * excitations : (a + 1) * excitations, tile(t)] = (weight * dual[t]).astype(jnp.bfloat16)
    dual_ref[...] = iter_ref[lax.axis_index("col")]
    product = jnp.dot(scaled_ref[...], tiles_ref[...], preferred_element_type=jnp.float32)
    for k in range(out_ref.shape[0]):
        term = jnp.zeros((excitations, LANES), jnp.float32)
        for a in range(kinds):
            weight = dual_moments_ref[a : a + 1, tile_at(col_start + k * LANES)]
            term = term + weight * product[a * excitations : (a + 1) * excitations, tile(k)]
        out_ref[k] = term.astype(jnp.bfloat16)


def final_kernel(shares_ref, incident_ref, out_ref, norm):
    me = lax.axis_index("row")
    total = shares_ref[0, me].astype(jnp.float32)
    for share in range(1, shares_ref.shape[0]):
        total = total + shares_ref[share, me].astype(jnp.float32)
    out_ref[...] = incident_ref[...] - total * norm


def exchange(value, axis):
    count = lax.axis_size(axis)
    pairwise = count & (count - 1) == 0
    values = [value]
    for step in range(count - 1, 0, -1):
        pairs = [(i, i ^ step if pairwise else (i + step) % count) for i in range(count)]
        values.append(lax.ppermute(value, axis, pairs))
    return values


def per_device(
    history,
    incident,
    centroids,
    moments,
    dual_moments,
    shell,
    near_mask,
    neighbours,
    gram_diag,
    gram_off,
):
    col_devices = lax.axis_size("col")
    slots, excitations, shard_len = history.shape
    p_tiles, q_tiles = shell.shape
    rows_t = gram_diag.shape[0]
    cols_t = q_tiles * LANES
    norm = 1.0 / math.sqrt(centroids.shape[1])
    shell, near_mask = shell.T, near_mask.T
    gram_diag = gram_diag.reshape(1, rows_t)

    packed = pl.pallas_call(
        pack_kernel,
        out_shape=jax.ShapeDtypeStruct((slots + 2, excitations, shard_len), jnp.bfloat16),
        in_specs=[VMEM, SMEM, SMEM, VMEM, VMEM, VMEM],
        out_specs=VMEM,
        compiler_params=pltpu.CompilerParams(vmem_limit_bytes=56 * MIB),
    )(history, shell, near_mask, gram_diag, gram_off, neighbours)
    packed = lax.all_gather(packed, "row", axis=2, tiled=True)

    parts = pl.pallas_call(
        functools.partial(t_kernel, norm=norm, slots=slots),
        out_shape=jax.ShapeDtypeStruct((excitations, rows_t + LANES), jnp.bfloat16),
        in_specs=[VMEM, VMEM, VMEM, SMEM, SMEM],
        out_specs=VMEM,
        scratch_shapes=[
            pltpu.VMEM((slots + 2, moments.shape[0] * excitations, cols_t), jnp.bfloat16),
            pltpu.VMEM((3, cols_t, LANES), jnp.float32),
            pltpu.VMEM((2, cols_t, LANES), jnp.bfloat16),
        ],
        compiler_params=grant((excitations, rows_t), (slots + 2, moments.shape[0] * excitations, cols_t), (5, cols_t, LANES), moments.shape, centroids.shape),
    )(packed, centroids, moments, shell, near_mask)
    parts, late_centroids = lax.optimization_barrier((parts, centroids))
    parts = exchange(parts, "col")

    entries = rows_t * cols_t
    s_tiles = pl.pallas_call(
        s_tiles_kernel,
        out_shape=jax.ShapeDtypeStruct((rows_t, cols_t), jnp.bfloat16),
        in_specs=[VMEM],
        out_specs=VMEM,
        scratch_shapes=[pltpu.VMEM((3, LANES, LANES), jnp.float32)],
        compiler_params=grant((rows_t, cols_t // 2), centroids.shape),
        cost_estimate=pl.CostEstimate(flops=12 * entries, bytes_accessed=2 * entries, transcendentals=2 * entries),
    )(late_centroids)

    own_dual, potential = pl.pallas_call(
        functools.partial(sweep_kernel, slots=slots, part_count=col_devices),
        out_shape=(
            jax.ShapeDtypeStruct((excitations, shard_len), jnp.float32),
            jax.ShapeDtypeStruct((q_tiles, excitations, LANES), jnp.bfloat16),
        ),
        in_specs=[VMEM] * (col_devices + 6),
        out_specs=(VMEM, VMEM),
        scratch_shapes=[
            pltpu.VMEM((p_tiles, excitations, LANES), jnp.float32),
            pltpu.VMEM((dual_moments.shape[0] * excitations, rows_t), jnp.bfloat16),
        ],
        compiler_params=grant((col_devices, excitations, rows_t), (rows_t, cols_t // 2), (excitations, 8 * rows_t)),
    )(*parts, packed, gram_diag, gram_off, neighbours, s_tiles, dual_moments)
    shares = lax.all_gather(potential, "row")
    march_rhs = pl.pallas_call(
        functools.partial(final_kernel, norm=norm),
        out_shape=jax.ShapeDtypeStruct(incident.shape, jnp.float32),
        in_specs=[VMEM, VMEM],
        out_specs=VMEM,
        compiler_params=grant(shares.shape),
    )(shares, incident)
    return (march_rhs, own_dual)


def solution(mesh):
    placed = (
        P(None, None, ("col", "row")),
        P(None, ("col", "row")),
        P(),
        P(),
        P(),
        P("row", "col"),
        P("row", "col"),
        P(None, "row"),
        P("row"),
        P(None, "row"),
    )
    return jax.shard_map(
        per_device,
        mesh=mesh,
        in_specs=placed,
        out_specs=(P(None, ("col", "row")), P(None, ("row", "col"))),
        check_vma=False,
    )
```

```python
import functools
import math

import jax
import jax.numpy as jnp
from jax import lax
from jax.experimental import pallas as pl
from jax.experimental.pallas import tpu as pltpu
from jax.sharding import PartitionSpec as P

SWEEPS = 2

SOFT_T = 0.05
SOFT_S = 0.1
NEAR_GAIN = 2.0
NEAR_REACH = 0.5

LANES = 128
HALF = LANES // 2
CHUNK = 64

VMEM = pl.BlockSpec(memory_space=pltpu.VMEM)
SMEM = pl.BlockSpec(memory_space=pltpu.SMEM)
LOG2_E = 1.4426950408889634
TINY = 1e-30
MIB = 1024 * 1024


def grant(*shapes):
    total = 0
    for shape in shapes:
        size = 4
        for extent in shape[:-2] + (-(-shape[-2] // 8) * 8, shape[-1]):
            size *= extent
        total += size
    return pltpu.CompilerParams(vmem_limit_bytes=min(56 * MIB, 2 * total + 2 * MIB))


def root(square):
    square = jnp.maximum(square, TINY)
    return square * lax.rsqrt(square)


def inverse(value):
    return pl.reciprocal(value, approx=True)


def lane_ids(rows=1):
    return lax.broadcasted_iota(jnp.int32, (rows, LANES), 1)


def tile_at(start):
    return pl.ds(pl.multiple_of(start, LANES), LANES)


def edges(ref, row, length):
    first = ref[row : row + 1, :LANES]
    last = ref[row : row + 1, length - LANES :]
    return jnp.where(lane_ids() < HALF, first, last)


def split3(value):
    high = value.astype(jnp.bfloat16).astype(jnp.float32)
    rest = value - high
    middle = rest.astype(jnp.bfloat16).astype(jnp.float32)
    return [high, middle, rest - middle]


def stack_rows(rows, height):
    row_ids = lax.broadcasted_iota(jnp.int32, (height, LANES), 0)
    out = jnp.zeros((height, LANES), jnp.float32)
    for position, row in enumerate(rows):
        out = jnp.where(row_ids == position, row, out)
    return out


def pack_kernel(history_ref, shell_ref, near_ref, diag_ref, off_ref, links_ref, out_ref):
    slots, excitations = history_ref.shape[:2]
    length = diag_ref.shape[1]
    tiles = shell_ref.shape[1]
    lanes = lane_ids()
    rows = []
    for tile in (0, tiles - 1):
        code = jnp.zeros((1, LANES), jnp.float32)
        for j in range(shell_ref.shape[0]):
            value = (shell_ref[j, tile] + slots * near_ref[j, tile]).astype(jnp.float32)
            code = jnp.where(lanes == j, value, code)
        rows.append(code)
    here = lax.axis_index("row") * length + jnp.where(lanes < HALF, lanes, length - LANES + lanes)
    for m in range(links_ref.shape[0]):
        rows.append((edges(links_ref, m, length) - here).astype(jnp.float32))
    rows += split3(edges(diag_ref, 0, length))
    coupling = []
    for m in range(off_ref.shape[0]):
        coupling += split3(edges(off_ref, m, length))
    out_ref[:slots] = history_ref[...]
    out_ref[slots] = stack_rows(rows, excitations).astype(jnp.bfloat16)
    out_ref[slots + 1] = stack_rows(coupling, excitations).astype(jnp.bfloat16)


def halo_row(packed_ref, row_count, plane, row):
    me = lax.axis_index("row")
    right = lax.rem(me + 1, row_count)
    left = lax.rem(me + row_count - 1, row_count)
    right_row = packed_ref[plane, :, tile_at(right * LANES)].astype(jnp.float32)[row : row + 1]
    left_row = packed_ref[plane, :, tile_at(left * LANES)].astype(jnp.float32)[row : row + 1]
    return right_row, left_row


def column_coords(centroids_ref, start, store):
    for axis in range(3):
        line = centroids_ref[axis : axis + 1, tile_at(start)]
        store(axis, jnp.broadcast_to(line, (LANES, LANES)).T)


def t_kernel(
    packed_ref, centroids_ref, moments_ref, shell_ref, near_ref, out_ref, scaled_ref, column_ref, tile_ref, norm, slots
):
    q_tiles, p_tiles = shell_ref.shape
    row_count = packed_ref.shape[2] // LANES
    excitations = packed_ref.shape[1]
    kinds = moments_ref.shape[0]
    total = centroids_ref.shape[1]
    length = p_tiles * LANES
    row_start = lax.axis_index("row") * length
    col_start = lax.axis_index("col") * (q_tiles * LANES)
    low = lane_ids() < HALF

    code_right, code_left = halo_row(packed_ref, row_count, slots, 0)[0], halo_row(packed_ref, row_count, slots, 1)[1]
    near_right = jnp.where(code_right >= slots, 1.0, 0.0)
    near_left = jnp.where(code_left >= slots, 1.0, 0.0)
    slot_right = code_right - slots * near_right
    slot_left = code_left - slots * near_left

    for j in range(q_tiles):
        lanes = slice(j * LANES, (j + 1) * LANES)
        weights = [moments_ref[a : a + 1, tile_at(col_start + j * LANES)] for a in range(kinds)]
        picked = [packed_ref[s, :, lanes].astype(jnp.float32) for s in range(slots)]
        for code in (slot_right, slot_left):
            choice = jnp.broadcast_to(code[:, j : j + 1], (excitations, LANES))
            value = picked[0]
            for s in range(1, slots):
                value = jnp.where(choice == s, picked[s], value)
            picked.append(value)
        for s, value in enumerate(picked):
            for a in range(kinds):
                scaled_ref[s, a * excitations : (a + 1) * excitations, lanes] = (weights[a] * value).astype(jnp.bfloat16)

        def store(axis, value, j=j):
            column_ref[axis, j * LANES : (j + 1) * LANES, :] = value

        column_coords(centroids_ref, col_start + j * LANES, store)

    def fill(slot, line, gain_of):
        for j in range(q_tiles):
            gain = gain_of(j)
            for k in range(LANES // CHUNK):
                at = slice(j * LANES + k * CHUNK, j * LANES + (k + 1) * CHUNK)
                dx = line[0] - column_ref[0, at, :]
                dy = line[1] - column_ref[1, at, :]
                dz = line[2] - column_ref[2, at, :]
                spacing = root(dx * dx + dy * dy + dz * dz)
                tile_ref[slot, at, :] = (
                    inverse(spacing + SOFT_T) + gain * jnp.exp2(spacing * (-LOG2_E / NEAR_REACH))
                ).astype(jnp.bfloat16)

    def products(slot, lhs):
        return jnp.dot(lhs, tile_ref[slot], preferred_element_type=jnp.float32)

    def weighted(product, weights):
        field = weights[0] * product[:excitations]
        for a in range(1, kinds):
            term = weights[a] * product[a * excitations : (a + 1) * excitations]
            field = field + term if a < kinds - 1 else field - term
        return (field * norm).astype(jnp.bfloat16)

    group = max(1, 16 // q_tiles)
    while p_tiles % group:
        group -= 1

    def one_group(g, carry):
        for k in range(group):
            t = g * group + k
            start = row_start + t * LANES
            line = [centroids_ref[axis : axis + 1, tile_at(start)] for axis in range(3)]
            fill(k % 2, line, lambda j: NEAR_GAIN * near_ref[j, t].astype(jnp.float32))
            lhs = jnp.concatenate(
                [scaled_ref[shell_ref[j, t], :, j * LANES : (j + 1) * LANES] for j in range(q_tiles)], axis=1
            )
            weights = [moments_ref[a : a + 1, tile_at(start)] for a in range(kinds)]
            out_ref[:, tile_at(t * LANES)] = weighted(products(k % 2, lhs), weights)
        return carry

    lax.fori_loop(0, p_tiles // group, one_group, 0)

    right_start = lax.rem(row_start + length, total)
    left_start = lax.rem(row_start + total - LANES, total)

    def halo(ref, row):
        return jnp.where(low, ref[row : row + 1, tile_at(right_start)], ref[row : row + 1, tile_at(left_start)])

    gains = NEAR_GAIN * jnp.where(low, 1.0, 0.0), NEAR_GAIN * jnp.where(low, 0.0, 1.0)
    fill(
        0,
        [halo(centroids_ref, axis) for axis in range(3)],
        lambda j: gains[0] * near_right[:, j : j + 1] + gains[1] * near_left[:, j : j + 1],
    )
    product = jnp.where(low, products(0, scaled_ref[slots]), products(0, scaled_ref[slots + 1]))
    out_ref[:, length:] = weighted(product, [halo(moments_ref, a) for a in range(kinds)])


def s_tiles_kernel(centroids_ref, out_ref, column_ref):
    length, width = out_ref.shape
    row_start = lax.axis_index("row") * length
    col_start = lax.axis_index("col") * width

    def one_tile(t, carry):
        def store(axis, value):
            column_ref[axis] = value

        column_coords(centroids_ref, row_start + t * LANES, store)
        for k in range(width // LANES):
            line = [centroids_ref[axis : axis + 1, tile_at(col_start + k * LANES)] for axis in range(3)]
            for piece in range(LANES // CHUNK):
                at = slice(piece * CHUNK, (piece + 1) * CHUNK)
                dx = line[0] - column_ref[0, at, :]
                dy = line[1] - column_ref[1, at, :]
                dz = line[2] - column_ref[2, at, :]
                spacing = root(dx * dx + dy * dy + dz * dz)
                rows = pl.ds(pl.multiple_of(t * LANES + piece * CHUNK, CHUNK), CHUNK)
                out_ref[rows, k * LANES : (k + 1) * LANES] = inverse(spacing + SOFT_S).astype(jnp.bfloat16)
        return carry

    lax.fori_loop(0, length // LANES, one_tile, 0)


def sweep_kernel(*refs, slots, part_count):
    parts = refs[:part_count]
    packed_ref, diag_ref, off_ref, links_ref, tiles_ref, dual_moments_ref = refs[part_count:-4]
    dual_ref, out_ref, iter_ref, scaled_ref = refs[-4:]
    length = diag_ref.shape[1]
    tiles = length // LANES
    row_count = packed_ref.shape[2] // LANES
    excitations = parts[0].shape[0]
    link_count = links_ref.shape[0]
    kinds = dual_moments_ref.shape[0]
    row_start = lax.axis_index("row") * length
    col_start = lax.axis_index("col") * tiles_ref.shape[1]
    lanes = lane_ids()
    low = lanes < HALF

    def halo(plane, row):
        return jnp.where(low, *halo_row(packed_ref, row_count, plane, row))

    def sum3(plane, row):
        return halo(plane, row) + halo(plane, row + 1) + halo(plane, row + 2)

    def tile(t):
        return slice(t * LANES, (t + 1) * LANES)

    field, diag = [], []
    for t in range(tiles + 1):
        total = parts[0][:, tile(t)].astype(jnp.float32)
        for part in parts[1:]:
            total = total + part[:, tile(t)].astype(jnp.float32)
        field.append(total)
        diag.append(diag_ref[:, tile(t)] if t < tiles else sum3(slots, 2 + link_count))

    dual = [f / d for f, d in zip(field, diag)]
    for sweep_id in range(SWEEPS):
        last = sweep_id == SWEEPS - 1
        updated = []
        for t in range(tiles if last else tiles + 1):
            around = jnp.where(low, dual[(t + 1) % (tiles + 1)], dual[t - 1])
            coupled = jnp.zeros_like(field[t])
            for m in range(link_count):
                if t < tiles:
                    source = links_ref[m : m + 1, tile(t)] - (row_start + t * LANES)
                    gram = off_ref[m : m + 1, tile(t)]
                else:
                    source = halo(slots, 2 + m).astype(jnp.int32) + lanes
                    gram = sum3(slots + 1, 3 * m)
                inside = (source >= 0) & (source < LANES)
                index = jnp.broadcast_to(source & (LANES - 1), (excitations, LANES))
                here = jnp.take_along_axis(dual[t], index, axis=1)
                beside = jnp.take_along_axis(around, index, axis=1)
                coupled = coupled + gram * jnp.where(inside, here, beside)
            updated.append((field[t] - coupled) / diag[t])
        dual = updated

    for t in range(tiles):
        iter_ref[t] = dual[t]
        for a in range(kinds):
            weight = dual_moments_ref[a : a + 1, tile_at(row_start + t * LANES)]
            scaled_ref[a * excitations : (a + 1) * excitations, tile(t)] = (weight * dual[t]).astype(jnp.bfloat16)
    dual_ref[...] = iter_ref[lax.axis_index("col")]
    product = jnp.dot(scaled_ref[...], tiles_ref[...], preferred_element_type=jnp.float32)
    for k in range(out_ref.shape[0]):
        term = jnp.zeros((excitations, LANES), jnp.float32)
        for a in range(kinds):
            weight = dual_moments_ref[a : a + 1, tile_at(col_start + k * LANES)]
            term = term + weight * product[a * excitations : (a + 1) * excitations, tile(k)]
        out_ref[k] = term.astype(jnp.bfloat16)


def final_kernel(shares_ref, incident_ref, out_ref, norm):
    me = lax.axis_index("row")
    total = shares_ref[0, me].astype(jnp.float32)
    for share in range(1, shares_ref.shape[0]):
        total = total + shares_ref[share, me].astype(jnp.float32)
    out_ref[...] = incident_ref[...] - total * norm


def per_device(
    history,
    incident,
    centroids,
    moments,
    dual_moments,
    shell,
    near_mask,
    neighbours,
    gram_diag,
    gram_off,
):
    slots, excitations, shard_len = history.shape
    p_tiles, q_tiles = shell.shape
    rows_t = gram_diag.shape[0]
    cols_t = q_tiles * LANES
    norm = 1.0 / math.sqrt(centroids.shape[1])
    shell, near_mask = shell.T, near_mask.T
    gram_diag = gram_diag.reshape(1, rows_t)

    packed = pl.pallas_call(
        pack_kernel,
        out_shape=jax.ShapeDtypeStruct((slots + 2, excitations, shard_len), jnp.bfloat16),
        in_specs=[VMEM, SMEM, SMEM, VMEM, VMEM, VMEM],
        out_specs=VMEM,
        compiler_params=pltpu.CompilerParams(vmem_limit_bytes=56 * MIB),
    )(history, shell, near_mask, gram_diag, gram_off, neighbours)
    packed = lax.all_gather(packed, "row", axis=2, tiled=True)

    parts = pl.pallas_call(
        functools.partial(t_kernel, norm=norm, slots=slots),
        out_shape=jax.ShapeDtypeStruct((excitations, rows_t + LANES), jnp.bfloat16),
        in_specs=[VMEM, VMEM, VMEM, SMEM, SMEM],
        out_specs=VMEM,
        scratch_shapes=[
            pltpu.VMEM((slots + 2, moments.shape[0] * excitations, cols_t), jnp.bfloat16),
            pltpu.VMEM((3, cols_t, LANES), jnp.float32),
            pltpu.VMEM((2, cols_t, LANES), jnp.bfloat16),
        ],
        compiler_params=grant((excitations, rows_t), (slots + 2, moments.shape[0] * excitations, cols_t), (5, cols_t, LANES), moments.shape, centroids.shape),
    )(packed, centroids, moments, shell, near_mask)
    parts, late_centroids = lax.optimization_barrier((parts, centroids))
    parts = lax.psum(parts, "col")

    entries = rows_t * cols_t
    s_tiles = pl.pallas_call(
        s_tiles_kernel,
        out_shape=jax.ShapeDtypeStruct((rows_t, cols_t), jnp.bfloat16),
        in_specs=[VMEM],
        out_specs=VMEM,
        scratch_shapes=[pltpu.VMEM((3, LANES, LANES), jnp.float32)],
        compiler_params=grant((rows_t, cols_t // 2), centroids.shape),
        cost_estimate=pl.CostEstimate(flops=12 * entries, bytes_accessed=2 * entries, transcendentals=2 * entries),
    )(late_centroids)

    own_dual, potential = pl.pallas_call(
        functools.partial(sweep_kernel, slots=slots, part_count=1),
        out_shape=(
            jax.ShapeDtypeStruct((excitations, shard_len), jnp.float32),
            jax.ShapeDtypeStruct((q_tiles, excitations, LANES), jnp.bfloat16),
        ),
        in_specs=[VMEM] * 7,
        out_specs=(VMEM, VMEM),
        scratch_shapes=[
            pltpu.VMEM((p_tiles, excitations, LANES), jnp.float32),
            pltpu.VMEM((dual_moments.shape[0] * excitations, rows_t), jnp.bfloat16),
        ],
        compiler_params=grant((excitations, rows_t), (rows_t, cols_t // 2), (excitations, 8 * rows_t)),
    )(parts, packed, gram_diag, gram_off, neighbours, s_tiles, dual_moments)
    shares = lax.all_gather(potential, "row")
    march_rhs = pl.pallas_call(
        functools.partial(final_kernel, norm=norm),
        out_shape=jax.ShapeDtypeStruct(incident.shape, jnp.float32),
        in_specs=[VMEM, VMEM],
        out_specs=VMEM,
        compiler_params=grant(shares.shape),
    )(shares, incident)
    return (march_rhs, own_dual)


def solution(mesh):
    placed = (
        P(None, None, ("col", "row")),
        P(None, ("col", "row")),
        P(),
        P(),
        P(),
        P("row", "col"),
        P("row", "col"),
        P(None, "row"),
        P("row"),
        P(None, "row"),
    )
    return jax.shard_map(
        per_device,
        mesh=mesh,
        in_specs=placed,
        out_specs=(P(None, ("col", "row")), P(None, ("row", "col"))),
        check_vma=False,
    )
```

```python
import functools
import math

import jax
import jax.numpy as jnp
from jax import lax
from jax.experimental import pallas as pl
from jax.experimental.pallas import tpu as pltpu
from jax.sharding import PartitionSpec as P

SWEEPS = 2

SOFT_T = 0.05
SOFT_S = 0.1
NEAR_GAIN = 2.0
NEAR_REACH = 0.5

LANES = 128
HALF = LANES // 2
CHUNK = 64

VMEM = pl.BlockSpec(memory_space=pltpu.VMEM)
SMEM = pl.BlockSpec(memory_space=pltpu.SMEM)
LOG2_E = 1.4426950408889634
TINY = 1e-30
MIB = 1024 * 1024


def grant(*shapes):
    total = 0
    for shape in shapes:
        size = 4
        for extent in shape[:-2] + (-(-shape[-2] // 8) * 8, shape[-1]):
            size *= extent
        total += size
    return pltpu.CompilerParams(vmem_limit_bytes=min(56 * MIB, 2 * total + 2 * MIB))


def root(square):
    square = jnp.maximum(square, TINY)
    return square * lax.rsqrt(square)


def inverse(value):
    return pl.reciprocal(value, approx=True)


def lane_ids(rows=1):
    return lax.broadcasted_iota(jnp.int32, (rows, LANES), 1)


def tile_at(start):
    return pl.ds(pl.multiple_of(start, LANES), LANES)


def edges(ref, row, length):
    first = ref[row : row + 1, :LANES]
    last = ref[row : row + 1, length - LANES :]
    return jnp.where(lane_ids() < HALF, first, last)


def split3(value):
    high = value.astype(jnp.bfloat16).astype(jnp.float32)
    rest = value - high
    middle = rest.astype(jnp.bfloat16).astype(jnp.float32)
    return [high, middle, rest - middle]


def stack_rows(rows, height):
    row_ids = lax.broadcasted_iota(jnp.int32, (height, LANES), 0)
    out = jnp.zeros((height, LANES), jnp.float32)
    for position, row in enumerate(rows):
        out = jnp.where(row_ids == position, row, out)
    return out


def pack_kernel(history_ref, shell_ref, near_ref, diag_ref, off_ref, links_ref, out_ref):
    slots, excitations = history_ref.shape[:2]
    length = diag_ref.shape[1]
    tiles = shell_ref.shape[1]
    lanes = lane_ids()
    rows = []
    for tile in (0, tiles - 1):
        code = jnp.zeros((1, LANES), jnp.float32)
        for j in range(shell_ref.shape[0]):
            value = (shell_ref[j, tile] + slots * near_ref[j, tile]).astype(jnp.float32)
            code = jnp.where(lanes == j, value, code)
        rows.append(code)
    here = lax.axis_index("row") * length + jnp.where(lanes < HALF, lanes, length - LANES + lanes)
    for m in range(links_ref.shape[0]):
        rows.append((edges(links_ref, m, length) - here).astype(jnp.float32))
    rows += split3(edges(diag_ref, 0, length))
    coupling = []
    for m in range(off_ref.shape[0]):
        coupling += split3(edges(off_ref, m, length))
    out_ref[:slots] = history_ref[...]
    out_ref[slots] = stack_rows(rows, excitations).astype(jnp.bfloat16)
    out_ref[slots + 1] = stack_rows(coupling, excitations).astype(jnp.bfloat16)


def halo_row(packed_ref, row_count, plane, row):
    me = lax.axis_index("row")
    right = lax.rem(me + 1, row_count)
    left = lax.rem(me + row_count - 1, row_count)
    right_row = packed_ref[plane, :, tile_at(right * LANES)].astype(jnp.float32)[row : row + 1]
    left_row = packed_ref[plane, :, tile_at(left * LANES)].astype(jnp.float32)[row : row + 1]
    return right_row, left_row


def column_coords(centroids_ref, start, store):
    for axis in range(3):
        line = centroids_ref[axis : axis + 1, tile_at(start)]
        store(axis, jnp.broadcast_to(line, (LANES, LANES)).T)


def t_kernel(
    packed_ref, centroids_ref, moments_ref, shell_ref, near_ref, out_ref, scaled_ref, column_ref, tile_ref, norm, slots
):
    q_tiles, p_tiles = shell_ref.shape
    row_count = packed_ref.shape[2] // LANES
    excitations = packed_ref.shape[1]
    kinds = moments_ref.shape[0]
    total = centroids_ref.shape[1]
    length = p_tiles * LANES
    row_start = lax.axis_index("row") * length
    col_start = lax.axis_index("col") * (q_tiles * LANES)
    low = lane_ids() < HALF

    code_right, code_left = halo_row(packed_ref, row_count, slots, 0)[0], halo_row(packed_ref, row_count, slots, 1)[1]
    near_right = jnp.where(code_right >= slots, 1.0, 0.0)
    near_left = jnp.where(code_left >= slots, 1.0, 0.0)
    slot_right = code_right - slots * near_right
    slot_left = code_left - slots * near_left

    for j in range(q_tiles):
        lanes = slice(j * LANES, (j + 1) * LANES)
        weights = [moments_ref[a : a + 1, tile_at(col_start + j * LANES)] for a in range(kinds)]
        picked = [packed_ref[s, :, lanes].astype(jnp.float32) for s in range(slots)]
        for code in (slot_right, slot_left):
            choice = jnp.broadcast_to(code[:, j : j + 1], (excitations, LANES))
            value = picked[0]
            for s in range(1, slots):
                value = jnp.where(choice == s, picked[s], value)
            picked.append(value)
        for s, value in enumerate(picked):
            for a in range(kinds):
                scaled_ref[s, a * excitations : (a + 1) * excitations, lanes] = (weights[a] * value).astype(jnp.bfloat16)

        def store(axis, value, j=j):
            column_ref[axis, j * LANES : (j + 1) * LANES, :] = value

        column_coords(centroids_ref, col_start + j * LANES, store)

    def fill(slot, line, gain_of):
        for j in range(q_tiles):
            gain = gain_of(j)
            for k in range(LANES // CHUNK):
                at = slice(j * LANES + k * CHUNK, j * LANES + (k + 1) * CHUNK)
                dx = line[0] - column_ref[0, at, :]
                dy = line[1] - column_ref[1, at, :]
                dz = line[2] - column_ref[2, at, :]
                spacing = root(dx * dx + dy * dy + dz * dz)
                tile_ref[slot, at, :] = (
                    inverse(spacing + SOFT_T) + gain * jnp.exp2(spacing * (-LOG2_E / NEAR_REACH))
                ).astype(jnp.bfloat16)

    def products(slot, lhs):
        return jnp.dot(lhs, tile_ref[slot], preferred_element_type=jnp.float32)

    def weighted(product, weights):
        field = weights[0] * product[:excitations]
        for a in range(1, kinds):
            term = weights[a] * product[a * excitations : (a + 1) * excitations]
            field = field + term if a < kinds - 1 else field - term
        return (field * norm).astype(jnp.bfloat16)

    group = max(1, 16 // q_tiles)
    while p_tiles % group:
        group -= 1

    def one_group(g, carry):
        for k in range(group):
            t = g * group + k
            start = row_start + t * LANES
            line = [centroids_ref[axis : axis + 1, tile_at(start)] for axis in range(3)]
            fill(k % 2, line, lambda j: NEAR_GAIN * near_ref[j, t].astype(jnp.float32))
            lhs = jnp.concatenate(
                [scaled_ref[shell_ref[j, t], :, j * LANES : (j + 1) * LANES] for j in range(q_tiles)], axis=1
            )
            weights = [moments_ref[a : a + 1, tile_at(start)] for a in range(kinds)]
            out_ref[:, tile_at(t * LANES)] = weighted(products(k % 2, lhs), weights)
        return carry

    lax.fori_loop(0, p_tiles // group, one_group, 0)

    right_start = lax.rem(row_start + length, total)
    left_start = lax.rem(row_start + total - LANES, total)

    def halo(ref, row):
        return jnp.where(low, ref[row : row + 1, tile_at(right_start)], ref[row : row + 1, tile_at(left_start)])

    gains = NEAR_GAIN * jnp.where(low, 1.0, 0.0), NEAR_GAIN * jnp.where(low, 0.0, 1.0)
    fill(
        0,
        [halo(centroids_ref, axis) for axis in range(3)],
        lambda j: gains[0] * near_right[:, j : j + 1] + gains[1] * near_left[:, j : j + 1],
    )
    product = jnp.where(low, products(0, scaled_ref[slots]), products(0, scaled_ref[slots + 1]))
    out_ref[:, length:] = weighted(product, [halo(moments_ref, a) for a in range(kinds)])


def s_tiles_kernel(centroids_ref, out_ref, column_ref):
    length, width = out_ref.shape
    row_start = lax.axis_index("row") * length
    col_start = lax.axis_index("col") * width

    def one_tile(t, carry):
        def store(axis, value):
            column_ref[axis] = value

        column_coords(centroids_ref, row_start + t * LANES, store)
        for k in range(width // LANES):
            line = [centroids_ref[axis : axis + 1, tile_at(col_start + k * LANES)] for axis in range(3)]
            for piece in range(LANES // CHUNK):
                at = slice(piece * CHUNK, (piece + 1) * CHUNK)
                dx = line[0] - column_ref[0, at, :]
                dy = line[1] - column_ref[1, at, :]
                dz = line[2] - column_ref[2, at, :]
                spacing = root(dx * dx + dy * dy + dz * dz)
                rows = pl.ds(pl.multiple_of(t * LANES + piece * CHUNK, CHUNK), CHUNK)
                out_ref[rows, k * LANES : (k + 1) * LANES] = inverse(spacing + SOFT_S).astype(jnp.bfloat16)
        return carry

    lax.fori_loop(0, length // LANES, one_tile, 0)


def sweep_kernel(*refs, slots, part_count):
    parts = refs[:part_count]
    packed_ref, diag_ref, off_ref, links_ref, tiles_ref, dual_moments_ref = refs[part_count:-4]
    dual_ref, out_ref, iter_ref, scaled_ref = refs[-4:]
    length = diag_ref.shape[1]
    tiles = length // LANES
    row_count = packed_ref.shape[2] // LANES
    excitations = parts[0].shape[0]
    link_count = links_ref.shape[0]
    kinds = dual_moments_ref.shape[0]
    row_start = lax.axis_index("row") * length
    col_start = lax.axis_index("col") * tiles_ref.shape[1]
    lanes = lane_ids()
    low = lanes < HALF

    def halo(plane, row):
        return jnp.where(low, *halo_row(packed_ref, row_count, plane, row))

    def sum3(plane, row):
        return halo(plane, row) + halo(plane, row + 1) + halo(plane, row + 2)

    def tile(t):
        return slice(t * LANES, (t + 1) * LANES)

    field, diag = [], []
    for t in range(tiles + 1):
        total = parts[0][:, tile(t)].astype(jnp.float32)
        for part in parts[1:]:
            total = total + part[:, tile(t)].astype(jnp.float32)
        field.append(total)
        diag.append(diag_ref[:, tile(t)] if t < tiles else sum3(slots, 2 + link_count))

    dual = [f / d for f, d in zip(field, diag)]
    for sweep_id in range(SWEEPS):
        last = sweep_id == SWEEPS - 1
        updated = []
        for t in range(tiles if last else tiles + 1):
            around = jnp.where(low, dual[(t + 1) % (tiles + 1)], dual[t - 1])
            coupled = jnp.zeros_like(field[t])
            for m in range(link_count):
                if t < tiles:
                    source = links_ref[m : m + 1, tile(t)] - (row_start + t * LANES)
                    gram = off_ref[m : m + 1, tile(t)]
                else:
                    source = halo(slots, 2 + m).astype(jnp.int32) + lanes
                    gram = sum3(slots + 1, 3 * m)
                inside = (source >= 0) & (source < LANES)
                index = jnp.broadcast_to(source & (LANES - 1), (excitations, LANES))
                here = jnp.take_along_axis(dual[t], index, axis=1)
                beside = jnp.take_along_axis(around, index, axis=1)
                coupled = coupled + gram * jnp.where(inside, here, beside)
            updated.append((field[t] - coupled) / diag[t])
        dual = updated

    for t in range(tiles):
        iter_ref[t] = dual[t]
        for a in range(kinds):
            weight = dual_moments_ref[a : a + 1, tile_at(row_start + t * LANES)]
            scaled_ref[a * excitations : (a + 1) * excitations, tile(t)] = (weight * dual[t]).astype(jnp.bfloat16)
    dual_ref[...] = iter_ref[lax.axis_index("col")]
    product = jnp.dot(scaled_ref[...], tiles_ref[...], preferred_element_type=jnp.float32)
    for k in range(out_ref.shape[0]):
        term = jnp.zeros((excitations, LANES), jnp.float32)
        for a in range(kinds):
            weight = dual_moments_ref[a : a + 1, tile_at(col_start + k * LANES)]
            term = term + weight * product[a * excitations : (a + 1) * excitations, tile(k)]
        out_ref[k] = term.astype(jnp.bfloat16)


def final_kernel(shares_ref, incident_ref, out_ref, norm):
    me = lax.axis_index("row")
    total = shares_ref[0, me].astype(jnp.float32)
    for share in range(1, shares_ref.shape[0]):
        total = total + shares_ref[share, me].astype(jnp.float32)
    out_ref[...] = incident_ref[...] - total * norm


def swap(value, axis, step):
    count = lax.axis_size(axis)
    if count & (count - 1) == 0:
        pairs = [(i, i ^ step) for i in range(count)]
    else:
        pairs = [(i, (i + step) % count) for i in range(count)]
    return lax.ppermute(value, axis, pairs)


def exchange(value, axis):
    count = lax.axis_size(axis)
    stride = 1
    if count > 2 and count & (count - 1) == 0:
        other = swap(value, axis, 1)
        value = (value.astype(jnp.float32) + other.astype(jnp.float32)).astype(value.dtype)
        stride = 2
    return [value] + [swap(value, axis, step) for step in range(count - stride, 0, -stride)]


def per_device(
    history,
    incident,
    centroids,
    moments,
    dual_moments,
    shell,
    near_mask,
    neighbours,
    gram_diag,
    gram_off,
):
    col_devices = lax.axis_size("col")
    slots, excitations, shard_len = history.shape
    p_tiles, q_tiles = shell.shape
    rows_t = gram_diag.shape[0]
    cols_t = q_tiles * LANES
    norm = 1.0 / math.sqrt(centroids.shape[1])
    shell, near_mask = shell.T, near_mask.T
    gram_diag = gram_diag.reshape(1, rows_t)

    packed = pl.pallas_call(
        pack_kernel,
        out_shape=jax.ShapeDtypeStruct((slots + 2, excitations, shard_len), jnp.bfloat16),
        in_specs=[VMEM, SMEM, SMEM, VMEM, VMEM, VMEM],
        out_specs=VMEM,
        compiler_params=pltpu.CompilerParams(vmem_limit_bytes=56 * MIB),
    )(history, shell, near_mask, gram_diag, gram_off, neighbours)
    packed = lax.all_gather(packed, "row", axis=2, tiled=True)

    parts = pl.pallas_call(
        functools.partial(t_kernel, norm=norm, slots=slots),
        out_shape=jax.ShapeDtypeStruct((excitations, rows_t + LANES), jnp.bfloat16),
        in_specs=[VMEM, VMEM, VMEM, SMEM, SMEM],
        out_specs=VMEM,
        scratch_shapes=[
            pltpu.VMEM((slots + 2, moments.shape[0] * excitations, cols_t), jnp.bfloat16),
            pltpu.VMEM((3, cols_t, LANES), jnp.float32),
            pltpu.VMEM((2, cols_t, LANES), jnp.bfloat16),
        ],
        compiler_params=grant((excitations, rows_t), (slots + 2, moments.shape[0] * excitations, cols_t), (5, cols_t, LANES), moments.shape, centroids.shape),
    )(packed, centroids, moments, shell, near_mask)
    parts, late_centroids = lax.optimization_barrier((parts, centroids))
    parts = exchange(parts, "col")

    entries = rows_t * cols_t
    s_tiles = pl.pallas_call(
        s_tiles_kernel,
        out_shape=jax.ShapeDtypeStruct((rows_t, cols_t), jnp.bfloat16),
        in_specs=[VMEM],
        out_specs=VMEM,
        scratch_shapes=[pltpu.VMEM((3, LANES, LANES), jnp.float32)],
        compiler_params=grant((rows_t, cols_t // 2), centroids.shape),
        cost_estimate=pl.CostEstimate(flops=12 * entries, bytes_accessed=2 * entries, transcendentals=2 * entries),
    )(late_centroids)

    own_dual, potential = pl.pallas_call(
        functools.partial(sweep_kernel, slots=slots, part_count=len(parts)),
        out_shape=(
            jax.ShapeDtypeStruct((excitations, shard_len), jnp.float32),
            jax.ShapeDtypeStruct((q_tiles, excitations, LANES), jnp.bfloat16),
        ),
        in_specs=[VMEM] * (len(parts) + 6),
        out_specs=(VMEM, VMEM),
        scratch_shapes=[
            pltpu.VMEM((p_tiles, excitations, LANES), jnp.float32),
            pltpu.VMEM((dual_moments.shape[0] * excitations, rows_t), jnp.bfloat16),
        ],
        compiler_params=grant((col_devices, excitations, rows_t), (rows_t, cols_t // 2), (excitations, 8 * rows_t)),
    )(*parts, packed, gram_diag, gram_off, neighbours, s_tiles, dual_moments)
    shares = lax.all_gather(potential, "row")
    march_rhs = pl.pallas_call(
        functools.partial(final_kernel, norm=norm),
        out_shape=jax.ShapeDtypeStruct(incident.shape, jnp.float32),
        in_specs=[VMEM, VMEM],
        out_specs=VMEM,
        compiler_params=grant(shares.shape),
    )(shares, incident)
    return (march_rhs, own_dual)


def solution(mesh):
    placed = (
        P(None, None, ("col", "row")),
        P(None, ("col", "row")),
        P(),
        P(),
        P(),
        P("row", "col"),
        P("row", "col"),
        P(None, "row"),
        P("row"),
        P(None, "row"),
    )
    return jax.shard_map(
        per_device,
        mesh=mesh,
        in_specs=placed,
        out_specs=(P(None, ("col", "row")), P(None, ("row", "col"))),
        check_vma=False,
    )
```

```python
import functools
import math

import jax
import jax.numpy as jnp
from jax import lax
from jax.experimental import pallas as pl
from jax.experimental.pallas import tpu as pltpu
from jax.sharding import PartitionSpec as P

SWEEPS = 2

SOFT_T = 0.05
SOFT_S = 0.1
NEAR_GAIN = 2.0
NEAR_REACH = 0.5

LANES = 128
HALF = LANES // 2
CHUNK = 64

VMEM = pl.BlockSpec(memory_space=pltpu.VMEM)
SMEM = pl.BlockSpec(memory_space=pltpu.SMEM)
LOG2_E = 1.4426950408889634
TINY = 1e-30
MIB = 1024 * 1024


def grant(*shapes):
    total = 0
    for shape in shapes:
        size = 4
        for extent in shape[:-2] + (-(-shape[-2] // 8) * 8, shape[-1]):
            size *= extent
        total += size
    return pltpu.CompilerParams(vmem_limit_bytes=min(56 * MIB, 2 * total + 2 * MIB))


def root(square):
    square = jnp.maximum(square, TINY)
    return square * lax.rsqrt(square)


def inverse(value):
    return pl.reciprocal(value, approx=True)


def lane_ids(rows=1):
    return lax.broadcasted_iota(jnp.int32, (rows, LANES), 1)


def tile_at(start):
    return pl.ds(pl.multiple_of(start, LANES), LANES)


def edges(ref, row, length):
    first = ref[row : row + 1, :LANES]
    last = ref[row : row + 1, length - LANES :]
    return jnp.where(lane_ids() < HALF, first, last)


def split3(value):
    high = value.astype(jnp.bfloat16).astype(jnp.float32)
    rest = value - high
    middle = rest.astype(jnp.bfloat16).astype(jnp.float32)
    return [high, middle, rest - middle]


def stack_rows(rows, height):
    row_ids = lax.broadcasted_iota(jnp.int32, (height, LANES), 0)
    out = jnp.zeros((height, LANES), jnp.float32)
    for position, row in enumerate(rows):
        out = jnp.where(row_ids == position, row, out)
    return out


def pack_kernel(history_ref, shell_ref, near_ref, diag_ref, off_ref, links_ref, out_ref):
    slots, excitations = history_ref.shape[:2]
    length = diag_ref.shape[1]
    tiles = shell_ref.shape[1]
    lanes = lane_ids()
    rows = []
    for tile in (0, tiles - 1):
        code = jnp.zeros((1, LANES), jnp.float32)
        for j in range(shell_ref.shape[0]):
            value = (shell_ref[j, tile] + slots * near_ref[j, tile]).astype(jnp.float32)
            code = jnp.where(lanes == j, value, code)
        rows.append(code)
    here = lax.axis_index("row") * length + jnp.where(lanes < HALF, lanes, length - LANES + lanes)
    for m in range(links_ref.shape[0]):
        rows.append((edges(links_ref, m, length) - here).astype(jnp.float32))
    rows += split3(edges(diag_ref, 0, length))
    coupling = []
    for m in range(off_ref.shape[0]):
        coupling += split3(edges(off_ref, m, length))
    out_ref[:slots] = history_ref[...]
    out_ref[slots] = stack_rows(rows, excitations).astype(jnp.bfloat16)
    out_ref[slots + 1] = stack_rows(coupling, excitations).astype(jnp.bfloat16)


def halo_row(packed_ref, row_count, plane, row):
    me = lax.axis_index("row")
    right = lax.rem(me + 1, row_count)
    left = lax.rem(me + row_count - 1, row_count)
    right_row = packed_ref[plane, :, tile_at(right * LANES)].astype(jnp.float32)[row : row + 1]
    left_row = packed_ref[plane, :, tile_at(left * LANES)].astype(jnp.float32)[row : row + 1]
    return right_row, left_row


def column_coords(centroids_ref, start, store):
    for axis in range(3):
        line = centroids_ref[axis : axis + 1, tile_at(start)]
        store(axis, jnp.broadcast_to(line, (LANES, LANES)).T)


def t_kernel(
    packed_ref, centroids_ref, moments_ref, shell_ref, near_ref, out_ref, scaled_ref, column_ref, tile_ref, norm, slots
):
    q_tiles, p_tiles = shell_ref.shape
    row_count = packed_ref.shape[2] // LANES
    excitations = packed_ref.shape[1]
    kinds = moments_ref.shape[0]
    total = centroids_ref.shape[1]
    length = p_tiles * LANES
    row_start = lax.axis_index("row") * length
    col_start = lax.axis_index("col") * (q_tiles * LANES)
    low = lane_ids() < HALF

    code_right, code_left = halo_row(packed_ref, row_count, slots, 0)[0], halo_row(packed_ref, row_count, slots, 1)[1]
    near_right = jnp.where(code_right >= slots, 1.0, 0.0)
    near_left = jnp.where(code_left >= slots, 1.0, 0.0)
    slot_right = code_right - slots * near_right
    slot_left = code_left - slots * near_left

    for j in range(q_tiles):
        lanes = slice(j * LANES, (j + 1) * LANES)
        weights = [moments_ref[a : a + 1, tile_at(col_start + j * LANES)] for a in range(kinds)]
        picked = [packed_ref[s, :, lanes].astype(jnp.float32) for s in range(slots)]
        for code in (slot_right, slot_left):
            choice = jnp.broadcast_to(code[:, j : j + 1], (excitations, LANES))
            value = picked[0]
            for s in range(1, slots):
                value = jnp.where(choice == s, picked[s], value)
            picked.append(value)
        for s, value in enumerate(picked):
            for a in range(kinds):
                scaled_ref[s, a * excitations : (a + 1) * excitations, lanes] = (weights[a] * value).astype(jnp.bfloat16)

        def store(axis, value, j=j):
            column_ref[axis, j * LANES : (j + 1) * LANES, :] = value

        column_coords(centroids_ref, col_start + j * LANES, store)

    def fill(slot, line, gain_of):
        for j in range(q_tiles):
            gain = gain_of(j)
            for k in range(LANES // CHUNK):
                at = slice(j * LANES + k * CHUNK, j * LANES + (k + 1) * CHUNK)
                dx = line[0] - column_ref[0, at, :]
                dy = line[1] - column_ref[1, at, :]
                dz = line[2] - column_ref[2, at, :]
                spacing = root(dx * dx + dy * dy + dz * dz)
                tile_ref[slot, at, :] = (
                    inverse(spacing + SOFT_T) + gain * jnp.exp2(spacing * (-LOG2_E / NEAR_REACH))
                ).astype(jnp.bfloat16)

    def products(slot, lhs):
        return jnp.dot(lhs, tile_ref[slot], preferred_element_type=jnp.float32)

    def weighted(product, weights):
        field = weights[0] * product[:excitations]
        for a in range(1, kinds):
            term = weights[a] * product[a * excitations : (a + 1) * excitations]
            field = field + term if a < kinds - 1 else field - term
        return (field * norm).astype(jnp.bfloat16)

    group = max(1, 16 // q_tiles)
    while p_tiles % group:
        group -= 1

    def one_group(g, carry):
        for k in range(group):
            t = g * group + k
            start = row_start + t * LANES
            line = [centroids_ref[axis : axis + 1, tile_at(start)] for axis in range(3)]
            fill(k % 2, line, lambda j: NEAR_GAIN * near_ref[j, t].astype(jnp.float32))
            lhs = jnp.concatenate(
                [scaled_ref[shell_ref[j, t], :, j * LANES : (j + 1) * LANES] for j in range(q_tiles)], axis=1
            )
            weights = [moments_ref[a : a + 1, tile_at(start)] for a in range(kinds)]
            out_ref[:, tile_at(t * LANES)] = weighted(products(k % 2, lhs), weights)
        return carry

    lax.fori_loop(0, p_tiles // group, one_group, 0)

    right_start = lax.rem(row_start + length, total)
    left_start = lax.rem(row_start + total - LANES, total)

    def halo(ref, row):
        return jnp.where(low, ref[row : row + 1, tile_at(right_start)], ref[row : row + 1, tile_at(left_start)])

    gains = NEAR_GAIN * jnp.where(low, 1.0, 0.0), NEAR_GAIN * jnp.where(low, 0.0, 1.0)
    fill(
        0,
        [halo(centroids_ref, axis) for axis in range(3)],
        lambda j: gains[0] * near_right[:, j : j + 1] + gains[1] * near_left[:, j : j + 1],
    )
    product = jnp.where(low, products(0, scaled_ref[slots]), products(0, scaled_ref[slots + 1]))
    out_ref[:, length:] = weighted(product, [halo(moments_ref, a) for a in range(kinds)])


def s_tiles_kernel(centroids_ref, out_ref, column_ref):
    length, width = out_ref.shape
    row_start = lax.axis_index("row") * length
    col_start = lax.axis_index("col") * width

    def one_tile(t, carry):
        def store(axis, value):
            column_ref[axis] = value

        column_coords(centroids_ref, row_start + t * LANES, store)
        for k in range(width // LANES):
            line = [centroids_ref[axis : axis + 1, tile_at(col_start + k * LANES)] for axis in range(3)]
            for piece in range(LANES // CHUNK):
                at = slice(piece * CHUNK, (piece + 1) * CHUNK)
                dx = line[0] - column_ref[0, at, :]
                dy = line[1] - column_ref[1, at, :]
                dz = line[2] - column_ref[2, at, :]
                spacing = root(dx * dx + dy * dy + dz * dz)
                rows = pl.ds(pl.multiple_of(t * LANES + piece * CHUNK, CHUNK), CHUNK)
                out_ref[rows, k * LANES : (k + 1) * LANES] = inverse(spacing + SOFT_S).astype(jnp.bfloat16)
        return carry

    lax.fori_loop(0, length // LANES, one_tile, 0)


def sweep_kernel(*refs, slots, part_count):
    parts = refs[:part_count]
    packed_ref, diag_ref, off_ref, links_ref, tiles_ref, dual_moments_ref = refs[part_count:-4]
    dual_ref, out_ref, iter_ref, scaled_ref = refs[-4:]
    length = diag_ref.shape[1]
    tiles = length // LANES
    row_count = packed_ref.shape[2] // LANES
    excitations = parts[0].shape[0]
    link_count = links_ref.shape[0]
    kinds = dual_moments_ref.shape[0]
    row_start = lax.axis_index("row") * length
    col_start = lax.axis_index("col") * tiles_ref.shape[1]
    lanes = lane_ids()
    low = lanes < HALF

    def halo(plane, row):
        return jnp.where(low, *halo_row(packed_ref, row_count, plane, row))

    def sum3(plane, row):
        return halo(plane, row) + halo(plane, row + 1) + halo(plane, row + 2)

    def tile(t):
        return slice(t * LANES, (t + 1) * LANES)

    field, diag = [], []
    for t in range(tiles + 1):
        total = parts[0][:, tile(t)].astype(jnp.float32)
        for part in parts[1:]:
            total = total + part[:, tile(t)].astype(jnp.float32)
        field.append(total)
        diag.append(diag_ref[:, tile(t)] if t < tiles else sum3(slots, 2 + link_count))

    dual = [f / d for f, d in zip(field, diag)]
    for sweep_id in range(SWEEPS):
        last = sweep_id == SWEEPS - 1
        updated = []
        for t in range(tiles if last else tiles + 1):
            around = jnp.where(low, dual[(t + 1) % (tiles + 1)], dual[t - 1])
            coupled = jnp.zeros_like(field[t])
            for m in range(link_count):
                if t < tiles:
                    source = links_ref[m : m + 1, tile(t)] - (row_start + t * LANES)
                    gram = off_ref[m : m + 1, tile(t)]
                else:
                    source = halo(slots, 2 + m).astype(jnp.int32) + lanes
                    gram = sum3(slots + 1, 3 * m)
                inside = (source >= 0) & (source < LANES)
                index = jnp.broadcast_to(source & (LANES - 1), (excitations, LANES))
                here = jnp.take_along_axis(dual[t], index, axis=1)
                beside = jnp.take_along_axis(around, index, axis=1)
                coupled = coupled + gram * jnp.where(inside, here, beside)
            updated.append((field[t] - coupled) / diag[t])
        dual = updated

    for t in range(tiles):
        iter_ref[t] = dual[t]
        for a in range(kinds):
            weight = dual_moments_ref[a : a + 1, tile_at(row_start + t * LANES)]
            scaled_ref[a * excitations : (a + 1) * excitations, tile(t)] = (weight * dual[t]).astype(jnp.bfloat16)
    dual_ref[...] = iter_ref[lax.axis_index("col")]
    product = jnp.dot(scaled_ref[...], tiles_ref[...], preferred_element_type=jnp.float32)
    for k in range(out_ref.shape[0]):
        term = jnp.zeros((excitations, LANES), jnp.float32)
        for a in range(kinds):
            weight = dual_moments_ref[a : a + 1, tile_at(col_start + k * LANES)]
            term = term + weight * product[a * excitations : (a + 1) * excitations, tile(k)]
        out_ref[k] = term.astype(jnp.bfloat16)


def final_kernel(shares_ref, incident_ref, out_ref, norm):
    me = lax.axis_index("row")
    total = shares_ref[0, me].astype(jnp.float32)
    for share in range(1, shares_ref.shape[0]):
        total = total + shares_ref[share, me].astype(jnp.float32)
    out_ref[...] = incident_ref[...] - total * norm


def swap(value, axis, step):
    count = lax.axis_size(axis)
    if count & (count - 1) == 0:
        pairs = [(i, i ^ step) for i in range(count)]
    else:
        pairs = [(i, (i + step) % count) for i in range(count)]
    return lax.ppermute(value, axis, pairs)


def exchange(value, axis):
    count = lax.axis_size(axis)
    if count & (count - 1):
        return [value] + [swap(value, axis, step) for step in range(1, count)]
    step = 1
    while 2 * step < count:
        other = swap(value, axis, step)
        value = (value.astype(jnp.float32) + other.astype(jnp.float32)).astype(value.dtype)
        step *= 2
    return [value, swap(value, axis, step)] if count > 1 else [value]


def per_device(
    history,
    incident,
    centroids,
    moments,
    dual_moments,
    shell,
    near_mask,
    neighbours,
    gram_diag,
    gram_off,
):
    col_devices = lax.axis_size("col")
    slots, excitations, shard_len = history.shape
    p_tiles, q_tiles = shell.shape
    rows_t = gram_diag.shape[0]
    cols_t = q_tiles * LANES
    norm = 1.0 / math.sqrt(centroids.shape[1])
    shell, near_mask = shell.T, near_mask.T
    gram_diag = gram_diag.reshape(1, rows_t)

    packed = pl.pallas_call(
        pack_kernel,
        out_shape=jax.ShapeDtypeStruct((slots + 2, excitations, shard_len), jnp.bfloat16),
        in_specs=[VMEM, SMEM, SMEM, VMEM, VMEM, VMEM],
        out_specs=VMEM,
        compiler_params=pltpu.CompilerParams(vmem_limit_bytes=56 * MIB),
    )(history, shell, near_mask, gram_diag, gram_off, neighbours)
    packed = lax.all_gather(packed, "row", axis=2, tiled=True)

    parts = pl.pallas_call(
        functools.partial(t_kernel, norm=norm, slots=slots),
        out_shape=jax.ShapeDtypeStruct((excitations, rows_t + LANES), jnp.bfloat16),
        in_specs=[VMEM, VMEM, VMEM, SMEM, SMEM],
        out_specs=VMEM,
        scratch_shapes=[
            pltpu.VMEM((slots + 2, moments.shape[0] * excitations, cols_t), jnp.bfloat16),
            pltpu.VMEM((3, cols_t, LANES), jnp.float32),
            pltpu.VMEM((2, cols_t, LANES), jnp.bfloat16),
        ],
        compiler_params=grant((excitations, rows_t), (slots + 2, moments.shape[0] * excitations, cols_t), (5, cols_t, LANES), moments.shape, centroids.shape),
    )(packed, centroids, moments, shell, near_mask)
    parts = exchange(parts, "col")
    last_share, late_centroids = lax.optimization_barrier((parts[0], centroids))

    entries = rows_t * cols_t
    s_tiles = pl.pallas_call(
        s_tiles_kernel,
        out_shape=jax.ShapeDtypeStruct((rows_t, cols_t), jnp.bfloat16),
        in_specs=[VMEM],
        out_specs=VMEM,
        scratch_shapes=[pltpu.VMEM((3, LANES, LANES), jnp.float32)],
        compiler_params=grant((rows_t, cols_t // 2), centroids.shape),
        cost_estimate=pl.CostEstimate(flops=12 * entries, bytes_accessed=2 * entries, transcendentals=2 * entries),
    )(late_centroids)

    own_dual, potential = pl.pallas_call(
        functools.partial(sweep_kernel, slots=slots, part_count=len(parts)),
        out_shape=(
            jax.ShapeDtypeStruct((excitations, shard_len), jnp.float32),
            jax.ShapeDtypeStruct((q_tiles, excitations, LANES), jnp.bfloat16),
        ),
        in_specs=[VMEM] * (len(parts) + 6),
        out_specs=(VMEM, VMEM),
        scratch_shapes=[
            pltpu.VMEM((p_tiles, excitations, LANES), jnp.float32),
            pltpu.VMEM((dual_moments.shape[0] * excitations, rows_t), jnp.bfloat16),
        ],
        compiler_params=grant((col_devices, excitations, rows_t), (rows_t, cols_t // 2), (excitations, 8 * rows_t)),
    )(last_share, *parts[1:], packed, gram_diag, gram_off, neighbours, s_tiles, dual_moments)
    shares = lax.all_gather(potential, "row")
    march_rhs = pl.pallas_call(
        functools.partial(final_kernel, norm=norm),
        out_shape=jax.ShapeDtypeStruct(incident.shape, jnp.float32),
        in_specs=[VMEM, VMEM],
        out_specs=VMEM,
        compiler_params=grant(shares.shape),
    )(shares, incident)
    return (march_rhs, own_dual)


def solution(mesh):
    placed = (
        P(None, None, ("col", "row")),
        P(None, ("col", "row")),
        P(),
        P(),
        P(),
        P("row", "col"),
        P("row", "col"),
        P(None, "row"),
        P("row"),
        P(None, "row"),
    )
    return jax.shard_map(
        per_device,
        mesh=mesh,
        in_specs=placed,
        out_specs=(P(None, ("col", "row")), P(None, ("row", "col"))),
        check_vma=False,
    )
```

```python
import functools
import math

import jax
import jax.numpy as jnp
from jax import lax
from jax.experimental import pallas as pl
from jax.experimental.pallas import tpu as pltpu
from jax.sharding import PartitionSpec as P

SWEEPS = 2

SOFT_T = 0.05
SOFT_S = 0.1
NEAR_GAIN = 2.0
NEAR_REACH = 0.5

LANES = 128
HALF = LANES // 2
CHUNK = 64

VMEM = pl.BlockSpec(memory_space=pltpu.VMEM)
SMEM = pl.BlockSpec(memory_space=pltpu.SMEM)
LOG2_E = 1.4426950408889634
TINY = 1e-30
MIB = 1024 * 1024


def grant(*shapes):
    total = 0
    for shape in shapes:
        size = 4
        for extent in shape[:-2] + (-(-shape[-2] // 8) * 8, shape[-1]):
            size *= extent
        total += size
    return pltpu.CompilerParams(vmem_limit_bytes=min(56 * MIB, 2 * total + 2 * MIB))


def root(square):
    square = jnp.maximum(square, TINY)
    return square * lax.rsqrt(square)


def inverse(value):
    return pl.reciprocal(value, approx=True)


def lane_ids(rows=1):
    return lax.broadcasted_iota(jnp.int32, (rows, LANES), 1)


def tile_at(start):
    return pl.ds(pl.multiple_of(start, LANES), LANES)


def edges(ref, row, length):
    first = ref[row : row + 1, :LANES]
    last = ref[row : row + 1, length - LANES :]
    return jnp.where(lane_ids() < HALF, first, last)


def split3(value):
    high = value.astype(jnp.bfloat16).astype(jnp.float32)
    rest = value - high
    middle = rest.astype(jnp.bfloat16).astype(jnp.float32)
    return [high, middle, rest - middle]


def stack_rows(rows, height):
    row_ids = lax.broadcasted_iota(jnp.int32, (height, LANES), 0)
    out = jnp.zeros((height, LANES), jnp.float32)
    for position, row in enumerate(rows):
        out = jnp.where(row_ids == position, row, out)
    return out


def pack_kernel(history_ref, shell_ref, near_ref, diag_ref, off_ref, links_ref, out_ref):
    slots, excitations = history_ref.shape[:2]
    length = diag_ref.shape[1]
    tiles = shell_ref.shape[1]
    lanes = lane_ids()
    rows = []
    for tile in (0, tiles - 1):
        code = jnp.zeros((1, LANES), jnp.float32)
        for j in range(shell_ref.shape[0]):
            value = (shell_ref[j, tile] + slots * near_ref[j, tile]).astype(jnp.float32)
            code = jnp.where(lanes == j, value, code)
        rows.append(code)
    here = lax.axis_index("row") * length + jnp.where(lanes < HALF, lanes, length - LANES + lanes)
    for m in range(links_ref.shape[0]):
        rows.append((edges(links_ref, m, length) - here).astype(jnp.float32))
    rows += split3(edges(diag_ref, 0, length))
    coupling = []
    for m in range(off_ref.shape[0]):
        coupling += split3(edges(off_ref, m, length))
    out_ref[:slots] = history_ref[...]
    out_ref[slots] = stack_rows(rows, excitations).astype(jnp.bfloat16)
    out_ref[slots + 1] = stack_rows(coupling, excitations).astype(jnp.bfloat16)


def target_of(me, step, count):
    return me ^ step if count & (count - 1) == 0 else lax.rem(me + step, count)


def source_of(me, step, count):
    return me ^ step if count & (count - 1) == 0 else lax.rem(me + count - step, count)


def step_from(me, source, count):
    return me ^ source if count & (count - 1) == 0 else lax.rem(me + count - source, count)


def entries_t(line, column, gains):
    dx, dy, dz = [line[axis] - column[axis] for axis in range(3)]
    spacing = root(dx * dx + dy * dy + dz * dz)
    far, near = inverse(spacing + SOFT_T), jnp.exp2(spacing * (-LOG2_E / NEAR_REACH))
    return [(far + gain * near).astype(jnp.bfloat16) if gain is not None else far.astype(jnp.bfloat16) for gain in gains]


def column_coords(centroids_ref, start, store):
    for axis in range(3):
        line = centroids_ref[axis : axis + 1, tile_at(start)]
        store(axis, jnp.broadcast_to(line, (LANES, LANES)).T)


def halo_line(ref, row, row_start, length):
    total = ref.shape[1]
    right_start = lax.rem(row_start + length, total)
    left_start = lax.rem(row_start + total - LANES, total)
    return jnp.where(
        lane_ids() < HALF, ref[row : row + 1, tile_at(right_start)], ref[row : row + 1, tile_at(left_start)]
    )


def t_tiles_kernel(centroids_ref, near_ref, out_ref, column_ref):
    q_tiles, p_tiles = near_ref.shape
    me = lax.axis_index("row")
    length = p_tiles * LANES
    row_start = me * length
    col_start = lax.axis_index("col") * (q_tiles * LANES)
    sources = [source_of(me, i, q_tiles) for i in range(q_tiles)]
    for i in range(q_tiles):

        def store(axis, value, i=i):
            column_ref[axis, i * LANES : (i + 1) * LANES, :] = value

        column_coords(centroids_ref, col_start + sources[i] * LANES, store)

    def fill(first, line, gains_of):
        for i in range(q_tiles):
            gains = gains_of(sources[i])
            for k in range(LANES // CHUNK):
                at = slice(i * LANES + k * CHUNK, i * LANES + (k + 1) * CHUNK)
                for offset, tile in enumerate(entries_t(line, [column_ref[axis, at, :] for axis in range(3)], gains)):
                    out_ref[first + offset, at, :] = tile

    group = max(1, 16 // q_tiles)
    while p_tiles % group:
        group -= 1

    def one_group(g, carry):
        for k in range(group):
            t = g * group + k
            line = [centroids_ref[axis : axis + 1, tile_at(row_start + t * LANES)] for axis in range(3)]
            fill(t, line, lambda j: [NEAR_GAIN * near_ref[j, t].astype(jnp.float32)])
        return carry

    lax.fori_loop(0, p_tiles // group, one_group, 0)
    line = [halo_line(centroids_ref, axis, row_start, length) for axis in range(3)]
    fill(p_tiles, line, lambda j: [None, NEAR_GAIN])


def t_kernel(*refs, norm, slots, count):
    packed = refs[:count]
    tiles_ref, moments_ref, shell_ref = refs[count : count + 3]
    out_ref, halo_ref, scaled_ref, edge_ref = refs[count + 3 :]
    q_tiles, p_tiles = shell_ref.shape
    excitations = out_ref.shape[0]
    kinds = moments_ref.shape[0]
    me = lax.axis_index("row")
    length = p_tiles * LANES
    row_start = me * length
    col_start = lax.axis_index("col") * (q_tiles * LANES)
    low = lane_ids() < HALF

    for i in range(count):
        edge_ref[i] = packed[i][slots:].astype(jnp.float32)
    right = edge_ref[step_from(me, lax.rem(me + 1, count), count)]
    left = edge_ref[step_from(me, lax.rem(me + count - 1, count), count)]
    halo_ref[...] = jnp.where(low[None], right, left)
    codes = right[0, 0:1], left[0, 1:2]
    nears = [jnp.where(code >= slots, 1.0, 0.0) for code in codes]
    picks = [code - slots * near for code, near in zip(codes, nears)]

    sources = [source_of(me, i, count) for i in range(count)]
    lanes = lane_ids()
    halo_tiles = []
    for i in range(count):
        at = slice(i * LANES, (i + 1) * LANES)
        weights = [moments_ref[a : a + 1, tile_at(col_start + sources[i] * LANES)] for a in range(kinds)]
        values = [packed[i][s].astype(jnp.float32) for s in range(slots)]
        here = lanes == sources[i]
        for pick in picks:
            choice = jnp.sum(jnp.where(here, pick, 0.0), axis=1, keepdims=True)
            value = values[0]
            for s in range(1, slots):
                value = jnp.where(choice == s, values[s], value)
            values.append(value)
        for s, value in enumerate(values):
            for a in range(kinds):
                scaled_ref[s, a * excitations : (a + 1) * excitations, at] = (weights[a] * value).astype(jnp.bfloat16)
        near_right, near_left = [jnp.sum(jnp.where(here, near, 0.0), axis=1, keepdims=True) for near in nears]
        near = jnp.where(low, near_right, near_left)
        halo_tiles.append(
            jnp.where(near > 0.5, tiles_ref[p_tiles + 1, at].astype(jnp.float32), tiles_ref[p_tiles, at].astype(jnp.float32))
            .astype(jnp.bfloat16)
        )

    def weighted(product, weights):
        field = weights[0] * product[:excitations]
        for a in range(1, kinds):
            term = weights[a] * product[a * excitations : (a + 1) * excitations]
            field = field + term if a < kinds - 1 else field - term
        return (field * norm).astype(jnp.bfloat16)

    def one_tile(t):
        lhs = jnp.concatenate(
            [scaled_ref[shell_ref[sources[i], t], :, i * LANES : (i + 1) * LANES] for i in range(count)], axis=1
        )
        weights = [moments_ref[a : a + 1, tile_at(row_start + t * LANES)] for a in range(kinds)]
        product = jnp.dot(lhs, tiles_ref[t], preferred_element_type=jnp.float32)
        out_ref[:, tile_at(t * LANES)] = weighted(product, weights)

    group = max(1, 32 // q_tiles)
    while p_tiles % group:
        group -= 1

    def one_group(g, carry):
        for k in range(group):
            one_tile(g * group + k)
        return carry

    if group == p_tiles:
        one_group(0, 0)
    else:
        lax.fori_loop(0, p_tiles // group, one_group, 0)
    halo_tile = jnp.concatenate(halo_tiles, axis=0)
    product = jnp.where(
        low,
        jnp.dot(scaled_ref[slots], halo_tile, preferred_element_type=jnp.float32),
        jnp.dot(scaled_ref[slots + 1], halo_tile, preferred_element_type=jnp.float32),
    )
    out_ref[:, length:] = weighted(product, [halo_line(moments_ref, a, row_start, length) for a in range(kinds)])


def s_tiles_kernel(centroids_ref, out_ref, column_ref):
    length, width = out_ref.shape
    row_start = lax.axis_index("row") * length
    col_start = lax.axis_index("col") * width

    def one_tile(t, carry):
        def store(axis, value):
            column_ref[axis] = value

        column_coords(centroids_ref, row_start + t * LANES, store)
        for k in range(width // LANES):
            line = [centroids_ref[axis : axis + 1, tile_at(col_start + k * LANES)] for axis in range(3)]
            for piece in range(LANES // CHUNK):
                at = slice(piece * CHUNK, (piece + 1) * CHUNK)
                dx = line[0] - column_ref[0, at, :]
                dy = line[1] - column_ref[1, at, :]
                dz = line[2] - column_ref[2, at, :]
                spacing = root(dx * dx + dy * dy + dz * dz)
                rows = pl.ds(pl.multiple_of(t * LANES + piece * CHUNK, CHUNK), CHUNK)
                out_ref[rows, k * LANES : (k + 1) * LANES] = inverse(spacing + SOFT_S).astype(jnp.bfloat16)
        return carry

    lax.fori_loop(0, length // LANES, one_tile, 0)


def sweep_kernel(*refs, slots, part_count, count):
    parts = refs[:part_count]
    halo_ref, diag_ref, off_ref, links_ref, tiles_ref, dual_moments_ref = refs[part_count : part_count + 6]
    dual_ref, *out_refs = refs[part_count + 6 : -3]
    iter_ref, scaled_ref, share_ref = refs[-3:]
    length = diag_ref.shape[1]
    tiles = length // LANES
    excitations = parts[0].shape[0]
    link_count = links_ref.shape[0]
    kinds = dual_moments_ref.shape[0]
    row_start = lax.axis_index("row") * length
    col_start = lax.axis_index("col") * tiles_ref.shape[1]
    lanes = lane_ids()
    low = lanes < HALF

    def halo(plane, row):
        return halo_ref[plane, row : row + 1]

    def sum3(plane, row):
        return halo(plane, row) + halo(plane, row + 1) + halo(plane, row + 2)

    def tile(t):
        return slice(t * LANES, (t + 1) * LANES)

    field, diag = [], []
    for t in range(tiles + 1):
        total = parts[0][:, tile(t)].astype(jnp.float32)
        for part in parts[1:]:
            total = total + part[:, tile(t)].astype(jnp.float32)
        field.append(total)
        diag.append(diag_ref[:, tile(t)] if t < tiles else sum3(0, 2 + link_count))

    dual = [f / d for f, d in zip(field, diag)]
    for sweep_id in range(SWEEPS):
        last = sweep_id == SWEEPS - 1
        updated = []
        for t in range(tiles if last else tiles + 1):
            around = jnp.where(low, dual[(t + 1) % (tiles + 1)], dual[t - 1])
            coupled = jnp.zeros_like(field[t])
            for m in range(link_count):
                if t < tiles:
                    source = links_ref[m : m + 1, tile(t)] - (row_start + t * LANES)
                    gram = off_ref[m : m + 1, tile(t)]
                else:
                    source = halo(0, 2 + m).astype(jnp.int32) + lanes
                    gram = sum3(1, 3 * m)
                inside = (source >= 0) & (source < LANES)
                index = jnp.broadcast_to(source & (LANES - 1), (excitations, LANES))
                here = jnp.take_along_axis(dual[t], index, axis=1)
                beside = jnp.take_along_axis(around, index, axis=1)
                coupled = coupled + gram * jnp.where(inside, here, beside)
            updated.append((field[t] - coupled) / diag[t])
        dual = updated

    for t in range(tiles):
        iter_ref[t] = dual[t]
        for a in range(kinds):
            weight = dual_moments_ref[a : a + 1, tile_at(row_start + t * LANES)]
            scaled_ref[a * excitations : (a + 1) * excitations, tile(t)] = (weight * dual[t]).astype(jnp.bfloat16)
    dual_ref[...] = iter_ref[lax.axis_index("col")]
    product = jnp.dot(scaled_ref[...], tiles_ref[...], preferred_element_type=jnp.float32)
    for k in range(count):
        term = jnp.zeros((excitations, LANES), jnp.float32)
        for a in range(kinds):
            weight = dual_moments_ref[a : a + 1, tile_at(col_start + k * LANES)]
            term = term + weight * product[a * excitations : (a + 1) * excitations, tile(k)]
        share_ref[k] = term
    me = lax.axis_index("row")
    for step, out_ref in enumerate(out_refs):
        out_ref[...] = share_ref[target_of(me, step, count)].astype(out_ref.dtype)


def final_kernel(*refs, norm):
    *share_refs, incident_ref, out_ref = refs
    total = share_refs[0][...].astype(jnp.float32)
    for share_ref in share_refs[1:]:
        total = total + share_ref[...].astype(jnp.float32)
    out_ref[...] = incident_ref[...] - total * norm


def swap(value, axis, step):
    count = lax.axis_size(axis)
    if count & (count - 1) == 0:
        pairs = [(i, i ^ step) for i in range(count)]
    else:
        pairs = [(i, (i + step) % count) for i in range(count)]
    return lax.ppermute(value, axis, pairs)


def exchange(value, axis):
    count = lax.axis_size(axis)
    if count & (count - 1):
        return [value] + [swap(value, axis, step) for step in range(1, count)]
    step = 1
    while 2 * step < count:
        other = swap(value, axis, step)
        value = (value.astype(jnp.float32) + other.astype(jnp.float32)).astype(value.dtype)
        step *= 2
    return [value, swap(value, axis, step)] if count > 1 else [value]


def late(value, after):
    return lax.optimization_barrier((value, after))[0]


def per_device(
    history,
    incident,
    centroids,
    moments,
    dual_moments,
    shell,
    near_mask,
    neighbours,
    gram_diag,
    gram_off,
):
    col_devices = lax.axis_size("col")
    slots, excitations, shard_len = history.shape
    p_tiles, q_tiles = shell.shape
    rows_t = gram_diag.shape[0]
    cols_t = q_tiles * LANES
    norm = 1.0 / math.sqrt(centroids.shape[1])
    shell, near_mask = shell.T, near_mask.T
    gram_diag = gram_diag.reshape(1, rows_t)

    packed = pl.pallas_call(
        pack_kernel,
        out_shape=jax.ShapeDtypeStruct((slots + 2, excitations, shard_len), jnp.bfloat16),
        in_specs=[VMEM, SMEM, SMEM, VMEM, VMEM, VMEM],
        out_specs=VMEM,
        compiler_params=pltpu.CompilerParams(vmem_limit_bytes=56 * MIB),
    )(history, shell, near_mask, gram_diag, gram_off, neighbours)
    count = lax.axis_size("row")
    everyone = [packed] + [swap(packed, "row", step) for step in range(count - 1, 0, -1)][::-1]
    entries = rows_t * cols_t
    t_tiles = pl.pallas_call(
        t_tiles_kernel,
        out_shape=jax.ShapeDtypeStruct((p_tiles + 2, cols_t, LANES), jnp.bfloat16),
        in_specs=[VMEM, SMEM],
        out_specs=VMEM,
        scratch_shapes=[pltpu.VMEM((3, cols_t, LANES), jnp.float32)],
        compiler_params=grant((p_tiles + 8, cols_t // 2, LANES), centroids.shape),
        cost_estimate=pl.CostEstimate(flops=16 * entries, bytes_accessed=2 * entries, transcendentals=3 * entries),
    )(late(centroids, packed), near_mask)

    parts, halo = pl.pallas_call(
        functools.partial(t_kernel, norm=norm, slots=slots, count=count),
        out_shape=(
            jax.ShapeDtypeStruct((excitations, rows_t + LANES), jnp.bfloat16),
            jax.ShapeDtypeStruct((2, excitations, LANES), jnp.float32),
        ),
        in_specs=[VMEM] * (count + 2) + [SMEM],
        out_specs=(VMEM, VMEM),
        scratch_shapes=[
            pltpu.VMEM((slots + 2, moments.shape[0] * excitations, cols_t), jnp.bfloat16),
            pltpu.VMEM((count, 2, excitations, LANES), jnp.float32),
        ],
        compiler_params=grant(
            (p_tiles + 2, cols_t // 2, LANES),
            (excitations, rows_t),
            (slots + 2, moments.shape[0] * excitations, cols_t),
            moments.shape,
        ),
    )(*everyone, t_tiles, moments, shell)
    parts = exchange(parts, "col")
    s_tiles = pl.pallas_call(
        s_tiles_kernel,
        out_shape=jax.ShapeDtypeStruct((rows_t, cols_t), jnp.bfloat16),
        in_specs=[VMEM],
        out_specs=VMEM,
        scratch_shapes=[pltpu.VMEM((3, LANES, LANES), jnp.float32)],
        compiler_params=grant((rows_t, cols_t // 2), centroids.shape),
        cost_estimate=pl.CostEstimate(flops=12 * entries, bytes_accessed=2 * entries, transcendentals=2 * entries),
    )(late(centroids, parts[0]))

    own_dual, *shares = pl.pallas_call(
        functools.partial(sweep_kernel, slots=slots, part_count=len(parts), count=count),
        out_shape=[jax.ShapeDtypeStruct((excitations, shard_len), jnp.float32)] * 2
        + [jax.ShapeDtypeStruct((excitations, shard_len), jnp.bfloat16)] * (count - 1),
        in_specs=[VMEM] * (len(parts) + 6),
        out_specs=[VMEM] * (count + 1),
        scratch_shapes=[
            pltpu.VMEM((p_tiles, excitations, LANES), jnp.float32),
            pltpu.VMEM((dual_moments.shape[0] * excitations, rows_t), jnp.bfloat16),
            pltpu.VMEM((q_tiles, excitations, LANES), jnp.float32),
        ],
        compiler_params=grant((col_devices, excitations, rows_t), (rows_t, cols_t // 2), (excitations, 8 * rows_t)),
    )(*parts, halo, gram_diag, gram_off, neighbours, s_tiles, dual_moments)
    for step in range(count - 1, 0, -1):
        shares[step] = swap(shares[step], "row", step)
    march_rhs = pl.pallas_call(
        functools.partial(final_kernel, norm=norm),
        out_shape=jax.ShapeDtypeStruct(incident.shape, jnp.float32),
        in_specs=[VMEM] * (count + 1),
        out_specs=VMEM,
        compiler_params=grant((count, excitations, shard_len)),
    )(*shares, incident)
    return (march_rhs, own_dual)


def solution(mesh):
    placed = (
        P(None, None, ("col", "row")),
        P(None, ("col", "row")),
        P(),
        P(),
        P(),
        P("row", "col"),
        P("row", "col"),
        P(None, "row"),
        P("row"),
        P(None, "row"),
    )
    return jax.shard_map(
        per_device,
        mesh=mesh,
        in_specs=placed,
        out_specs=(P(None, ("col", "row")), P(None, ("row", "col"))),
        check_vma=False,
    )
```

```python
import functools
import math

import jax
import jax.numpy as jnp
from jax import lax
from jax.experimental import pallas as pl
from jax.experimental.pallas import tpu as pltpu
from jax.sharding import PartitionSpec as P

SWEEPS = 2

SOFT_T = 0.05
SOFT_S = 0.1
NEAR_GAIN = 2.0
NEAR_REACH = 0.5

LANES = 128
HALF = LANES // 2
CHUNK = 64

VMEM = pl.BlockSpec(memory_space=pltpu.VMEM)
SMEM = pl.BlockSpec(memory_space=pltpu.SMEM)
LOG2_E = 1.4426950408889634
TINY = 1e-30
MIB = 1024 * 1024


def grant(*shapes):
    total = 0
    for shape in shapes:
        size = 4
        for extent in shape[:-2] + (-(-shape[-2] // 8) * 8, shape[-1]):
            size *= extent
        total += size
    return pltpu.CompilerParams(vmem_limit_bytes=min(56 * MIB, 2 * total + 2 * MIB))


def root(square):
    square = jnp.maximum(square, TINY)
    return square * lax.rsqrt(square)


def inverse(value):
    return pl.reciprocal(value, approx=True)


def lane_ids(rows=1):
    return lax.broadcasted_iota(jnp.int32, (rows, LANES), 1)


def tile_at(start):
    return pl.ds(pl.multiple_of(start, LANES), LANES)


def edges(ref, row, length):
    first = ref[row : row + 1, :LANES]
    last = ref[row : row + 1, length - LANES :]
    return jnp.where(lane_ids() < HALF, first, last)


def split3(value):
    high = value.astype(jnp.bfloat16).astype(jnp.float32)
    rest = value - high
    middle = rest.astype(jnp.bfloat16).astype(jnp.float32)
    return [high, middle, rest - middle]


def stack_rows(rows, height):
    row_ids = lax.broadcasted_iota(jnp.int32, (height, LANES), 0)
    out = jnp.zeros((height, LANES), jnp.float32)
    for position, row in enumerate(rows):
        out = jnp.where(row_ids == position, row, out)
    return out


def pack_kernel(history_ref, shell_ref, near_ref, diag_ref, off_ref, links_ref, out_ref, token_ref):
    slots, excitations = history_ref.shape[:2]
    length = diag_ref.shape[1]
    tiles = shell_ref.shape[1]
    lanes = lane_ids()
    rows = []
    for tile in (0, tiles - 1):
        code = jnp.zeros((1, LANES), jnp.float32)
        for j in range(shell_ref.shape[0]):
            value = (shell_ref[j, tile] + slots * near_ref[j, tile]).astype(jnp.float32)
            code = jnp.where(lanes == j, value, code)
        rows.append(code)
    here = lax.axis_index("row") * length + jnp.where(lanes < HALF, lanes, length - LANES + lanes)
    for m in range(links_ref.shape[0]):
        rows.append((edges(links_ref, m, length) - here).astype(jnp.float32))
    rows += split3(edges(diag_ref, 0, length))
    coupling = []
    for m in range(off_ref.shape[0]):
        coupling += split3(edges(off_ref, m, length))
    out_ref[:slots] = history_ref[...]
    out_ref[slots] = stack_rows(rows, excitations).astype(jnp.bfloat16)
    out_ref[slots + 1] = stack_rows(coupling, excitations).astype(jnp.bfloat16)
    token_ref[...] = jnp.zeros_like(token_ref)


def target_of(me, step, count):
    return me ^ step if count & (count - 1) == 0 else lax.rem(me + step, count)


def source_of(me, step, count):
    return me ^ step if count & (count - 1) == 0 else lax.rem(me + count - step, count)


def step_from(me, source, count):
    return me ^ source if count & (count - 1) == 0 else lax.rem(me + count - source, count)


def entries_t(line, column, gains):
    dx, dy, dz = [line[axis] - column[axis] for axis in range(3)]
    spacing = root(dx * dx + dy * dy + dz * dz)
    far, near = inverse(spacing + SOFT_T), jnp.exp2(spacing * (-LOG2_E / NEAR_REACH))
    return [(far + gain * near).astype(jnp.bfloat16) if gain is not None else far.astype(jnp.bfloat16) for gain in gains]


def column_coords(centroids_ref, start, store):
    for axis in range(3):
        line = centroids_ref[axis : axis + 1, tile_at(start)]
        store(axis, jnp.broadcast_to(line, (LANES, LANES)).T)


def halo_line(ref, row, row_start, length):
    total = ref.shape[1]
    right_start = lax.rem(row_start + length, total)
    left_start = lax.rem(row_start + total - LANES, total)
    return jnp.where(
        lane_ids() < HALF, ref[row : row + 1, tile_at(right_start)], ref[row : row + 1, tile_at(left_start)]
    )


def t_tiles_kernel(token_ref, centroids_ref, near_ref, out_ref, column_ref):
    del token_ref
    q_tiles, p_tiles = near_ref.shape
    me = lax.axis_index("row")
    length = p_tiles * LANES
    row_start = me * length
    col_start = lax.axis_index("col") * (q_tiles * LANES)
    sources = [source_of(me, i, q_tiles) for i in range(q_tiles)]
    for i in range(q_tiles):

        def store(axis, value, i=i):
            column_ref[axis, i * LANES : (i + 1) * LANES, :] = value

        column_coords(centroids_ref, col_start + sources[i] * LANES, store)

    def fill(first, line, gains_of):
        for i in range(q_tiles):
            gains = gains_of(sources[i])
            for k in range(LANES // CHUNK):
                at = slice(i * LANES + k * CHUNK, i * LANES + (k + 1) * CHUNK)
                for offset, tile in enumerate(entries_t(line, [column_ref[axis, at, :] for axis in range(3)], gains)):
                    out_ref[first + offset, at, :] = tile

    group = max(1, 16 // q_tiles)
    while p_tiles % group:
        group -= 1

    def one_group(g, carry):
        for k in range(group):
            t = g * group + k
            line = [centroids_ref[axis : axis + 1, tile_at(row_start + t * LANES)] for axis in range(3)]
            fill(t, line, lambda j: [NEAR_GAIN * near_ref[j, t].astype(jnp.float32)])
        return carry

    lax.fori_loop(0, p_tiles // group, one_group, 0)
    line = [halo_line(centroids_ref, axis, row_start, length) for axis in range(3)]
    fill(p_tiles, line, lambda j: [None, NEAR_GAIN])


def t_kernel(*refs, norm, slots, count):
    packed = refs[:count]
    tiles_ref, moments_ref, shell_ref = refs[count : count + 3]
    out_ref, halo_ref, scaled_ref, edge_ref = refs[count + 3 :]
    q_tiles, p_tiles = shell_ref.shape
    excitations = out_ref.shape[0]
    kinds = moments_ref.shape[0]
    me = lax.axis_index("row")
    length = p_tiles * LANES
    row_start = me * length
    col_start = lax.axis_index("col") * (q_tiles * LANES)
    low = lane_ids() < HALF

    for i in range(count):
        edge_ref[i] = packed[i][slots:].astype(jnp.float32)
    right = edge_ref[step_from(me, lax.rem(me + 1, count), count)]
    left = edge_ref[step_from(me, lax.rem(me + count - 1, count), count)]
    halo_ref[...] = jnp.where(low[None], right, left)
    codes = right[0, 0:1], left[0, 1:2]
    nears = [jnp.where(code >= slots, 1.0, 0.0) for code in codes]
    picks = [code - slots * near for code, near in zip(codes, nears)]

    sources = [source_of(me, i, count) for i in range(count)]
    lanes = lane_ids()
    halo_tiles = []
    for i in range(count):
        at = slice(i * LANES, (i + 1) * LANES)
        weights = [moments_ref[a : a + 1, tile_at(col_start + sources[i] * LANES)] for a in range(kinds)]
        values = [packed[i][s].astype(jnp.float32) for s in range(slots)]
        here = lanes == sources[i]
        for pick in picks:
            choice = jnp.sum(jnp.where(here, pick, 0.0), axis=1, keepdims=True)
            value = values[0]
            for s in range(1, slots):
                value = jnp.where(choice == s, values[s], value)
            values.append(value)
        for s, value in enumerate(values):
            for a in range(kinds):
                scaled_ref[s, a * excitations : (a + 1) * excitations, at] = (weights[a] * value).astype(jnp.bfloat16)
        near_right, near_left = [jnp.sum(jnp.where(here, near, 0.0), axis=1, keepdims=True) for near in nears]
        near = jnp.where(low, near_right, near_left)
        halo_tiles.append(
            jnp.where(near > 0.5, tiles_ref[p_tiles + 1, at].astype(jnp.float32), tiles_ref[p_tiles, at].astype(jnp.float32))
            .astype(jnp.bfloat16)
        )

    def weighted(product, weights):
        field = weights[0] * product[:excitations]
        for a in range(1, kinds):
            term = weights[a] * product[a * excitations : (a + 1) * excitations]
            field = field + term if a < kinds - 1 else field - term
        return (field * norm).astype(jnp.bfloat16)

    def one_tile(t):
        lhs = jnp.concatenate(
            [scaled_ref[shell_ref[sources[i], t], :, i * LANES : (i + 1) * LANES] for i in range(count)], axis=1
        )
        weights = [moments_ref[a : a + 1, tile_at(row_start + t * LANES)] for a in range(kinds)]
        product = jnp.dot(lhs, tiles_ref[t], preferred_element_type=jnp.float32)
        out_ref[:, tile_at(t * LANES)] = weighted(product, weights)

    group = max(1, 32 // q_tiles)
    while p_tiles % group:
        group -= 1

    def one_group(g, carry):
        for k in range(group):
            one_tile(g * group + k)
        return carry

    if group == p_tiles:
        one_group(0, 0)
    else:
        lax.fori_loop(0, p_tiles // group, one_group, 0)
    halo_tile = jnp.concatenate(halo_tiles, axis=0)
    product = jnp.where(
        low,
        jnp.dot(scaled_ref[slots], halo_tile, preferred_element_type=jnp.float32),
        jnp.dot(scaled_ref[slots + 1], halo_tile, preferred_element_type=jnp.float32),
    )
    out_ref[:, length:] = weighted(product, [halo_line(moments_ref, a, row_start, length) for a in range(kinds)])


def s_tiles_kernel(centroids_ref, out_ref, column_ref):
    length, width = out_ref.shape
    row_start = lax.axis_index("row") * length
    col_start = lax.axis_index("col") * width

    def one_tile(t, carry):
        def store(axis, value):
            column_ref[axis] = value

        column_coords(centroids_ref, row_start + t * LANES, store)
        for k in range(width // LANES):
            line = [centroids_ref[axis : axis + 1, tile_at(col_start + k * LANES)] for axis in range(3)]
            for piece in range(LANES // CHUNK):
                at = slice(piece * CHUNK, (piece + 1) * CHUNK)
                dx = line[0] - column_ref[0, at, :]
                dy = line[1] - column_ref[1, at, :]
                dz = line[2] - column_ref[2, at, :]
                spacing = root(dx * dx + dy * dy + dz * dz)
                rows = pl.ds(pl.multiple_of(t * LANES + piece * CHUNK, CHUNK), CHUNK)
                out_ref[rows, k * LANES : (k + 1) * LANES] = inverse(spacing + SOFT_S).astype(jnp.bfloat16)
        return carry

    lax.fori_loop(0, length // LANES, one_tile, 0)


def sweep_kernel(*refs, slots, part_count, count):
    parts = refs[:part_count]
    halo_ref, diag_ref, off_ref, links_ref, tiles_ref, dual_moments_ref = refs[part_count : part_count + 6]
    dual_ref, *out_refs = refs[part_count + 6 : -3]
    iter_ref, scaled_ref, share_ref = refs[-3:]
    length = diag_ref.shape[1]
    tiles = length // LANES
    excitations = parts[0].shape[0]
    link_count = links_ref.shape[0]
    kinds = dual_moments_ref.shape[0]
    row_start = lax.axis_index("row") * length
    col_start = lax.axis_index("col") * tiles_ref.shape[1]
    lanes = lane_ids()
    low = lanes < HALF

    def halo(plane, row):
        return halo_ref[plane, row : row + 1]

    def sum3(plane, row):
        return halo(plane, row) + halo(plane, row + 1) + halo(plane, row + 2)

    def tile(t):
        return slice(t * LANES, (t + 1) * LANES)

    field, diag = [], []
    for t in range(tiles + 1):
        total = parts[0][:, tile(t)].astype(jnp.float32)
        for part in parts[1:]:
            total = total + part[:, tile(t)].astype(jnp.float32)
        field.append(total)
        diag.append(diag_ref[:, tile(t)] if t < tiles else sum3(0, 2 + link_count))

    dual = [f / d for f, d in zip(field, diag)]
    for sweep_id in range(SWEEPS):
        last = sweep_id == SWEEPS - 1
        updated = []
        for t in range(tiles if last else tiles + 1):
            around = jnp.where(low, dual[(t + 1) % (tiles + 1)], dual[t - 1])
            coupled = jnp.zeros_like(field[t])
            for m in range(link_count):
                if t < tiles:
                    source = links_ref[m : m + 1, tile(t)] - (row_start + t * LANES)
                    gram = off_ref[m : m + 1, tile(t)]
                else:
                    source = halo(0, 2 + m).astype(jnp.int32) + lanes
                    gram = sum3(1, 3 * m)
                inside = (source >= 0) & (source < LANES)
                index = jnp.broadcast_to(source & (LANES - 1), (excitations, LANES))
                here = jnp.take_along_axis(dual[t], index, axis=1)
                beside = jnp.take_along_axis(around, index, axis=1)
                coupled = coupled + gram * jnp.where(inside, here, beside)
            updated.append((field[t] - coupled) / diag[t])
        dual = updated

    for t in range(tiles):
        iter_ref[t] = dual[t]
        for a in range(kinds):
            weight = dual_moments_ref[a : a + 1, tile_at(row_start + t * LANES)]
            scaled_ref[a * excitations : (a + 1) * excitations, tile(t)] = (weight * dual[t]).astype(jnp.bfloat16)
    dual_ref[...] = iter_ref[lax.axis_index("col")]
    product = jnp.dot(scaled_ref[...], tiles_ref[...], preferred_element_type=jnp.float32)
    for k in range(count):
        term = jnp.zeros((excitations, LANES), jnp.float32)
        for a in range(kinds):
            weight = dual_moments_ref[a : a + 1, tile_at(col_start + k * LANES)]
            term = term + weight * product[a * excitations : (a + 1) * excitations, tile(k)]
        share_ref[k] = term
    me = lax.axis_index("row")
    for step, out_ref in enumerate(out_refs):
        out_ref[...] = share_ref[target_of(me, step, count)].astype(out_ref.dtype)


def final_kernel(*refs, norm):
    *share_refs, incident_ref, out_ref = refs
    total = share_refs[0][...].astype(jnp.float32)
    for share_ref in share_refs[1:]:
        total = total + share_ref[...].astype(jnp.float32)
    out_ref[...] = incident_ref[...] - total * norm


def swap(value, axis, step):
    count = lax.axis_size(axis)
    if count & (count - 1) == 0:
        pairs = [(i, i ^ step) for i in range(count)]
    else:
        pairs = [(i, (i + step) % count) for i in range(count)]
    return lax.ppermute(value, axis, pairs)


def exchange(value, axis):
    count = lax.axis_size(axis)
    if count == 1 or count & (count - 1):
        return [value] + [swap(value, axis, step) for step in range(1, count)]
    step = 1
    while step < count:
        radix = min(4, count // step)
        values = [value] + [swap(value, axis, step * k) for k in range(1, radix)]
        step *= radix
        if step < count:
            value = sum(part.astype(jnp.float32) for part in values).astype(value.dtype)
    return values


def late(value, after):
    return lax.optimization_barrier((value, after))[0]


def per_device(
    history,
    incident,
    centroids,
    moments,
    dual_moments,
    shell,
    near_mask,
    neighbours,
    gram_diag,
    gram_off,
):
    col_devices = lax.axis_size("col")
    slots, excitations, shard_len = history.shape
    p_tiles, q_tiles = shell.shape
    rows_t = gram_diag.shape[0]
    cols_t = q_tiles * LANES
    norm = 1.0 / math.sqrt(centroids.shape[1])
    shell, near_mask = shell.T, near_mask.T
    gram_diag = gram_diag.reshape(1, rows_t)

    packed, token = pl.pallas_call(
        pack_kernel,
        out_shape=(
            jax.ShapeDtypeStruct((slots + 2, excitations, shard_len), jnp.bfloat16),
            jax.ShapeDtypeStruct((8, LANES), jnp.float32),
        ),
        in_specs=[VMEM, SMEM, SMEM, VMEM, VMEM, VMEM],
        out_specs=(VMEM, VMEM),
        compiler_params=pltpu.CompilerParams(vmem_limit_bytes=56 * MIB),
    )(history, shell, near_mask, gram_diag, gram_off, neighbours)
    count = lax.axis_size("row")
    everyone = [packed] + [swap(packed, "row", step) for step in range(count - 1, 0, -1)][::-1]
    entries = rows_t * cols_t
    t_tiles = pl.pallas_call(
        t_tiles_kernel,
        out_shape=jax.ShapeDtypeStruct((p_tiles + 2, cols_t, LANES), jnp.bfloat16),
        in_specs=[pl.BlockSpec(memory_space=pl.ANY), VMEM, SMEM],
        out_specs=VMEM,
        scratch_shapes=[pltpu.VMEM((3, cols_t, LANES), jnp.float32)],
        compiler_params=grant((p_tiles + 8, cols_t // 2, LANES), centroids.shape),
        cost_estimate=pl.CostEstimate(flops=16 * entries, bytes_accessed=2 * entries, transcendentals=3 * entries),
    )(token, centroids, near_mask)

    parts, halo = pl.pallas_call(
        functools.partial(t_kernel, norm=norm, slots=slots, count=count),
        out_shape=(
            jax.ShapeDtypeStruct((excitations, rows_t + LANES), jnp.bfloat16),
            jax.ShapeDtypeStruct((2, excitations, LANES), jnp.float32),
        ),
        in_specs=[VMEM] * (count + 2) + [SMEM],
        out_specs=(VMEM, VMEM),
        scratch_shapes=[
            pltpu.VMEM((slots + 2, moments.shape[0] * excitations, cols_t), jnp.bfloat16),
            pltpu.VMEM((count, 2, excitations, LANES), jnp.float32),
        ],
        compiler_params=grant(
            (p_tiles + 2, cols_t // 2, LANES),
            (excitations, rows_t),
            (slots + 2, moments.shape[0] * excitations, cols_t),
            moments.shape,
        ),
    )(*everyone, t_tiles, moments, shell)
    parts = exchange(parts, "col")
    s_tiles = pl.pallas_call(
        s_tiles_kernel,
        out_shape=jax.ShapeDtypeStruct((rows_t, cols_t), jnp.bfloat16),
        in_specs=[VMEM],
        out_specs=VMEM,
        scratch_shapes=[pltpu.VMEM((3, LANES, LANES), jnp.float32)],
        compiler_params=grant((rows_t, cols_t // 2), centroids.shape),
        cost_estimate=pl.CostEstimate(flops=12 * entries, bytes_accessed=2 * entries, transcendentals=2 * entries),
    )(late(centroids, parts[0]))

    own_dual, *shares = pl.pallas_call(
        functools.partial(sweep_kernel, slots=slots, part_count=len(parts), count=count),
        out_shape=[jax.ShapeDtypeStruct((excitations, shard_len), jnp.float32)] * 2
        + [jax.ShapeDtypeStruct((excitations, shard_len), jnp.bfloat16)] * (count - 1),
        in_specs=[VMEM] * (len(parts) + 6),
        out_specs=[VMEM] * (count + 1),
        scratch_shapes=[
            pltpu.VMEM((p_tiles, excitations, LANES), jnp.float32),
            pltpu.VMEM((dual_moments.shape[0] * excitations, rows_t), jnp.bfloat16),
            pltpu.VMEM((q_tiles, excitations, LANES), jnp.float32),
        ],
        compiler_params=grant((col_devices, excitations, rows_t), (rows_t, cols_t // 2), (excitations, 8 * rows_t)),
    )(*parts, halo, gram_diag, gram_off, neighbours, s_tiles, dual_moments)
    for step in sorted(range(1, count), key=lambda step: (1 - step % 2, step)):
        shares[step] = swap(shares[step], "row", step)
    march_rhs = pl.pallas_call(
        functools.partial(final_kernel, norm=norm),
        out_shape=jax.ShapeDtypeStruct(incident.shape, jnp.float32),
        in_specs=[VMEM] * (count + 1),
        out_specs=VMEM,
        compiler_params=grant((count, excitations, shard_len)),
    )(*shares, incident)
    return (march_rhs, own_dual)


def solution(mesh):
    placed = (
        P(None, None, ("col", "row")),
        P(None, ("col", "row")),
        P(),
        P(),
        P(),
        P("row", "col"),
        P("row", "col"),
        P(None, "row"),
        P("row"),
        P(None, "row"),
    )
    return jax.shard_map(
        per_device,
        mesh=mesh,
        in_specs=placed,
        out_specs=(P(None, ("col", "row")), P(None, ("row", "col"))),
        check_vma=False,
    )
```

```python
import functools
import math

import jax
import jax.numpy as jnp
from jax import lax
from jax.experimental import pallas as pl
from jax.experimental.pallas import tpu as pltpu
from jax.sharding import PartitionSpec as P

SWEEPS = 2

SOFT_T = 0.05
SOFT_S = 0.1
NEAR_GAIN = 2.0
NEAR_REACH = 0.5

LANES = 128
HALF = LANES // 2
CHUNK = 64

VMEM = pl.BlockSpec(memory_space=pltpu.VMEM)
SMEM = pl.BlockSpec(memory_space=pltpu.SMEM)
LOG2_E = 1.4426950408889634
TINY = 1e-30
MIB = 1024 * 1024


def grant(*shapes):
    total = 0
    for shape in shapes:
        size = 4
        for extent in shape[:-2] + (-(-shape[-2] // 8) * 8, shape[-1]):
            size *= extent
        total += size
    return pltpu.CompilerParams(vmem_limit_bytes=min(56 * MIB, 2 * total + 2 * MIB))


def root(square):
    square = jnp.maximum(square, TINY)
    return square * lax.rsqrt(square)


def inverse(value):
    return pl.reciprocal(value, approx=True)


def lane_ids(rows=1):
    return lax.broadcasted_iota(jnp.int32, (rows, LANES), 1)


def tile_at(start):
    return pl.ds(pl.multiple_of(start, LANES), LANES)


def edges(ref, row, length):
    first = ref[row : row + 1, :LANES]
    last = ref[row : row + 1, length - LANES :]
    return jnp.where(lane_ids() < HALF, first, last)


def split3(value):
    high = value.astype(jnp.bfloat16).astype(jnp.float32)
    rest = value - high
    middle = rest.astype(jnp.bfloat16).astype(jnp.float32)
    return [high, middle, rest - middle]


def stack_rows(rows, height):
    row_ids = lax.broadcasted_iota(jnp.int32, (height, LANES), 0)
    out = jnp.zeros((height, LANES), jnp.float32)
    for position, row in enumerate(rows):
        out = jnp.where(row_ids == position, row, out)
    return out


def pack_kernel(history_ref, shell_ref, near_ref, diag_ref, off_ref, links_ref, centroids_ref, out_ref, lines_ref):
    slots, excitations = history_ref.shape[:2]
    length = diag_ref.shape[1]
    tiles = shell_ref.shape[1]
    lanes = lane_ids()
    rows = []
    for tile in (0, tiles - 1):
        code = jnp.zeros((1, LANES), jnp.float32)
        for j in range(shell_ref.shape[0]):
            value = (shell_ref[j, tile] + slots * near_ref[j, tile]).astype(jnp.float32)
            code = jnp.where(lanes == j, value, code)
        rows.append(code)
    here = lax.axis_index("row") * length + jnp.where(lanes < HALF, lanes, length - LANES + lanes)
    for m in range(links_ref.shape[0]):
        rows.append((edges(links_ref, m, length) - here).astype(jnp.float32))
    rows += split3(edges(diag_ref, 0, length))
    coupling = []
    for m in range(off_ref.shape[0]):
        coupling += split3(edges(off_ref, m, length))
    out_ref[:slots] = history_ref[...]
    out_ref[slots] = stack_rows(rows, excitations).astype(jnp.bfloat16)
    out_ref[slots + 1] = stack_rows(coupling, excitations).astype(jnp.bfloat16)
    me = lax.axis_index("row")
    row_start = me * length
    q_tiles = shell_ref.shape[0]
    col_start = lax.axis_index("col") * (q_tiles * LANES)
    sources = [source_of(me, i, q_tiles) for i in range(q_tiles)]
    for t in range(tiles):
        for axis in range(3):
            lines_ref[3 * t + axis] = centroids_ref[axis, tile_at(row_start + t * LANES)]
    row = 3 * tiles
    for axis in range(3):
        lines_ref[row + axis : row + axis + 1] = halo_line(centroids_ref, axis, row_start, length)
    row += 3
    for i in range(q_tiles):
        for axis in range(3):
            lines_ref[row + axis] = centroids_ref[axis, tile_at(col_start + sources[i] * LANES)]
        row += 3
    for t in range(tiles):
        for i in range(q_tiles):
            gain = NEAR_GAIN * near_ref[sources[i], t].astype(jnp.float32)
            lines_ref[row : row + 1] = jnp.full((1, LANES), gain, jnp.float32)
            row += 1


def target_of(me, step, count):
    return me ^ step if count & (count - 1) == 0 else lax.rem(me + step, count)


def source_of(me, step, count):
    return me ^ step if count & (count - 1) == 0 else lax.rem(me + count - step, count)


def step_from(me, source, count):
    return me ^ source if count & (count - 1) == 0 else lax.rem(me + count - source, count)


def entries_t(line, column, gains):
    dx, dy, dz = [line[axis] - column[axis] for axis in range(3)]
    spacing = root(dx * dx + dy * dy + dz * dz)
    far, near = inverse(spacing + SOFT_T), jnp.exp2(spacing * (-LOG2_E / NEAR_REACH))
    return [(far + gain * near).astype(jnp.bfloat16) if gain is not None else far.astype(jnp.bfloat16) for gain in gains]


def columns(line):
    return jnp.broadcast_to(line, (LANES, LANES)).T


def halo_line(ref, row, row_start, length):
    total = ref.shape[1]
    right_start = lax.rem(row_start + length, total)
    left_start = lax.rem(row_start + total - LANES, total)
    return jnp.where(
        lane_ids() < HALF, ref[row : row + 1, tile_at(right_start)], ref[row : row + 1, tile_at(left_start)]
    )


def t_tiles_kernel(lines_ref, out_ref, column_ref, p_tiles, q_tiles):
    first_column = 3 * (p_tiles + 1)
    first_gain = first_column + 3 * q_tiles
    for i in range(q_tiles):
        for axis in range(3):
            row = first_column + 3 * i + axis
            column_ref[axis, i * LANES : (i + 1) * LANES, :] = columns(lines_ref[row : row + 1])

    def fill(first, gains_of):
        line = [lines_ref[pl.ds(3 * first + axis, 1)] for axis in range(3)]
        for i in range(q_tiles):
            gains = gains_of(i)
            for k in range(LANES // CHUNK):
                at = slice(i * LANES + k * CHUNK, i * LANES + (k + 1) * CHUNK)
                for offset, tile in enumerate(entries_t(line, [column_ref[axis, at, :] for axis in range(3)], gains)):
                    out_ref[first + offset, at, :] = tile

    group = max(1, 16 // q_tiles)
    while p_tiles % group:
        group -= 1

    def one_group(g, carry):
        for k in range(group):
            t = g * group + k
            fill(t, lambda i: [lines_ref[pl.ds(first_gain + t * q_tiles + i, 1)]])
        return carry

    lax.fori_loop(0, p_tiles // group, one_group, 0)
    fill(p_tiles, lambda i: [None, NEAR_GAIN])


def t_kernel(*refs, norm, slots, count):
    packed = refs[:count]
    tiles_ref, moments_ref, shell_ref = refs[count : count + 3]
    out_ref, halo_ref, scaled_ref, edge_ref = refs[count + 3 :]
    q_tiles, p_tiles = shell_ref.shape
    excitations = out_ref.shape[0]
    kinds = moments_ref.shape[0]
    me = lax.axis_index("row")
    length = p_tiles * LANES
    row_start = me * length
    col_start = lax.axis_index("col") * (q_tiles * LANES)
    low = lane_ids() < HALF

    for i in range(count):
        edge_ref[i] = packed[i][slots:].astype(jnp.float32)
    right = edge_ref[step_from(me, lax.rem(me + 1, count), count)]
    left = edge_ref[step_from(me, lax.rem(me + count - 1, count), count)]
    halo_ref[...] = jnp.where(low[None], right, left)
    codes = right[0, 0:1], left[0, 1:2]
    nears = [jnp.where(code >= slots, 1.0, 0.0) for code in codes]
    picks = [code - slots * near for code, near in zip(codes, nears)]

    sources = [source_of(me, i, count) for i in range(count)]
    lanes = lane_ids()
    halo_tiles = []
    for i in range(count):
        at = slice(i * LANES, (i + 1) * LANES)
        weights = [moments_ref[a : a + 1, tile_at(col_start + sources[i] * LANES)] for a in range(kinds)]
        values = [packed[i][s].astype(jnp.float32) for s in range(slots)]
        here = lanes == sources[i]
        for pick in picks:
            choice = jnp.sum(jnp.where(here, pick, 0.0), axis=1, keepdims=True)
            value = values[0]
            for s in range(1, slots):
                value = jnp.where(choice == s, values[s], value)
            values.append(value)
        for s, value in enumerate(values):
            for a in range(kinds):
                scaled_ref[s, a * excitations : (a + 1) * excitations, at] = (weights[a] * value).astype(jnp.bfloat16)
        near_right, near_left = [jnp.sum(jnp.where(here, near, 0.0), axis=1, keepdims=True) for near in nears]
        near = jnp.where(low, near_right, near_left)
        halo_tiles.append(
            jnp.where(near > 0.5, tiles_ref[p_tiles + 1, at].astype(jnp.float32), tiles_ref[p_tiles, at].astype(jnp.float32))
            .astype(jnp.bfloat16)
        )

    def weighted(product, weights):
        field = weights[0] * product[:excitations]
        for a in range(1, kinds):
            term = weights[a] * product[a * excitations : (a + 1) * excitations]
            field = field + term if a < kinds - 1 else field - term
        return (field * norm).astype(jnp.bfloat16)

    def one_tile(t):
        lhs = jnp.concatenate(
            [scaled_ref[shell_ref[sources[i], t], :, i * LANES : (i + 1) * LANES] for i in range(count)], axis=1
        )
        weights = [moments_ref[a : a + 1, tile_at(row_start + t * LANES)] for a in range(kinds)]
        product = jnp.dot(lhs, tiles_ref[t], preferred_element_type=jnp.float32)
        out_ref[:, tile_at(t * LANES)] = weighted(product, weights)

    group = max(1, 32 // q_tiles)
    while p_tiles % group:
        group -= 1

    def one_group(g, carry):
        for k in range(group):
            one_tile(g * group + k)
        return carry

    if group == p_tiles:
        one_group(0, 0)
    else:
        lax.fori_loop(0, p_tiles // group, one_group, 0)
    halo_tile = jnp.concatenate(halo_tiles, axis=0)
    product = jnp.where(
        low,
        jnp.dot(scaled_ref[slots], halo_tile, preferred_element_type=jnp.float32),
        jnp.dot(scaled_ref[slots + 1], halo_tile, preferred_element_type=jnp.float32),
    )
    out_ref[:, length:] = weighted(product, [halo_line(moments_ref, a, row_start, length) for a in range(kinds)])


def s_tiles_kernel(centroids_ref, out_ref, column_ref):
    length, width = out_ref.shape
    row_start = lax.axis_index("row") * length
    col_start = lax.axis_index("col") * width

    def one_tile(t, carry):
        for axis in range(3):
            column_ref[axis] = columns(centroids_ref[axis : axis + 1, tile_at(row_start + t * LANES)])
        for k in range(width // LANES):
            line = [centroids_ref[axis : axis + 1, tile_at(col_start + k * LANES)] for axis in range(3)]
            for piece in range(LANES // CHUNK):
                at = slice(piece * CHUNK, (piece + 1) * CHUNK)
                dx = line[0] - column_ref[0, at, :]
                dy = line[1] - column_ref[1, at, :]
                dz = line[2] - column_ref[2, at, :]
                spacing = root(dx * dx + dy * dy + dz * dz)
                rows = pl.ds(pl.multiple_of(t * LANES + piece * CHUNK, CHUNK), CHUNK)
                out_ref[rows, k * LANES : (k + 1) * LANES] = inverse(spacing + SOFT_S).astype(jnp.bfloat16)
        return carry

    lax.fori_loop(0, length // LANES, one_tile, 0)


def sweep_kernel(*refs, slots, part_count, count):
    parts = refs[:part_count]
    halo_ref, diag_ref, off_ref, links_ref, tiles_ref, dual_moments_ref = refs[part_count : part_count + 6]
    dual_ref, *out_refs = refs[part_count + 6 : -3]
    iter_ref, scaled_ref, share_ref = refs[-3:]
    length = diag_ref.shape[1]
    tiles = length // LANES
    excitations = parts[0].shape[0]
    link_count = links_ref.shape[0]
    kinds = dual_moments_ref.shape[0]
    row_start = lax.axis_index("row") * length
    col_start = lax.axis_index("col") * tiles_ref.shape[1]
    lanes = lane_ids()
    low = lanes < HALF

    def halo(plane, row):
        return halo_ref[plane, row : row + 1]

    def sum3(plane, row):
        return halo(plane, row) + halo(plane, row + 1) + halo(plane, row + 2)

    def tile(t):
        return slice(t * LANES, (t + 1) * LANES)

    field, diag = [], []
    for t in range(tiles + 1):
        total = parts[0][:, tile(t)].astype(jnp.float32)
        for part in parts[1:]:
            total = total + part[:, tile(t)].astype(jnp.float32)
        field.append(total)
        diag.append(diag_ref[:, tile(t)] if t < tiles else sum3(0, 2 + link_count))

    dual = [f / d for f, d in zip(field, diag)]
    for sweep_id in range(SWEEPS):
        last = sweep_id == SWEEPS - 1
        updated = []
        for t in range(tiles if last else tiles + 1):
            around = jnp.where(low, dual[(t + 1) % (tiles + 1)], dual[t - 1])
            coupled = jnp.zeros_like(field[t])
            for m in range(link_count):
                if t < tiles:
                    source = links_ref[m : m + 1, tile(t)] - (row_start + t * LANES)
                    gram = off_ref[m : m + 1, tile(t)]
                else:
                    source = halo(0, 2 + m).astype(jnp.int32) + lanes
                    gram = sum3(1, 3 * m)
                inside = (source >= 0) & (source < LANES)
                index = jnp.broadcast_to(source & (LANES - 1), (excitations, LANES))
                here = jnp.take_along_axis(dual[t], index, axis=1)
                beside = jnp.take_along_axis(around, index, axis=1)
                coupled = coupled + gram * jnp.where(inside, here, beside)
            updated.append((field[t] - coupled) / diag[t])
        dual = updated

    for t in range(tiles):
        iter_ref[t] = dual[t]
        for a in range(kinds):
            weight = dual_moments_ref[a : a + 1, tile_at(row_start + t * LANES)]
            scaled_ref[a * excitations : (a + 1) * excitations, tile(t)] = (weight * dual[t]).astype(jnp.bfloat16)
    dual_ref[...] = iter_ref[lax.axis_index("col")]
    product = jnp.dot(scaled_ref[...], tiles_ref[...], preferred_element_type=jnp.float32)
    for k in range(count):
        term = jnp.zeros((excitations, LANES), jnp.float32)
        for a in range(kinds):
            weight = dual_moments_ref[a : a + 1, tile_at(col_start + k * LANES)]
            term = term + weight * product[a * excitations : (a + 1) * excitations, tile(k)]
        share_ref[k] = term
    me = lax.axis_index("row")
    for step, out_ref in enumerate(out_refs):
        out_ref[...] = share_ref[target_of(me, step, count)].astype(out_ref.dtype)


def final_kernel(*refs, norm):
    *share_refs, incident_ref, out_ref = refs
    total = share_refs[0][...].astype(jnp.float32)
    for share_ref in share_refs[1:]:
        total = total + share_ref[...].astype(jnp.float32)
    out_ref[...] = incident_ref[...] - total * norm


def swap(value, axis, step):
    count = lax.axis_size(axis)
    if count & (count - 1) == 0:
        pairs = [(i, i ^ step) for i in range(count)]
    else:
        pairs = [(i, (i + step) % count) for i in range(count)]
    return lax.ppermute(value, axis, pairs)


def exchange(value, axis):
    count = lax.axis_size(axis)
    if count == 1 or count & (count - 1):
        return [value] + [swap(value, axis, step) for step in range(1, count)]
    step = 1
    while step < count:
        radix = min(4, count // step)
        values = [value] + [swap(value, axis, step * k) for k in range(1, radix)]
        step *= radix
        if step < count:
            value = sum(part.astype(jnp.float32) for part in values[::-1]).astype(value.dtype)
    return values


def late(value, after):
    return lax.optimization_barrier((value, after))[0]


def per_device(
    history,
    incident,
    centroids,
    moments,
    dual_moments,
    shell,
    near_mask,
    neighbours,
    gram_diag,
    gram_off,
):
    col_devices = lax.axis_size("col")
    slots, excitations, shard_len = history.shape
    p_tiles, q_tiles = shell.shape
    rows_t = gram_diag.shape[0]
    cols_t = q_tiles * LANES
    norm = 1.0 / math.sqrt(centroids.shape[1])
    shell, near_mask = shell.T, near_mask.T
    gram_diag = gram_diag.reshape(1, rows_t)

    line_rows = -(-(3 * (p_tiles + 1 + q_tiles) + p_tiles * q_tiles) // 8) * 8
    packed, lines = pl.pallas_call(
        pack_kernel,
        out_shape=(
            jax.ShapeDtypeStruct((slots + 2, excitations, shard_len), jnp.bfloat16),
            jax.ShapeDtypeStruct((line_rows, LANES), jnp.float32),
        ),
        in_specs=[VMEM, SMEM, SMEM, VMEM, VMEM, VMEM, VMEM],
        out_specs=(VMEM, VMEM),
        compiler_params=pltpu.CompilerParams(vmem_limit_bytes=56 * MIB),
    )(history, shell, near_mask, gram_diag, gram_off, neighbours, centroids)
    count = lax.axis_size("row")
    everyone = [packed] + [swap(packed, "row", step) for step in range(count - 1, 0, -1)][::-1]
    entries = rows_t * cols_t
    t_tiles = pl.pallas_call(
        functools.partial(t_tiles_kernel, p_tiles=p_tiles, q_tiles=q_tiles),
        out_shape=jax.ShapeDtypeStruct((p_tiles + 2, cols_t, LANES), jnp.bfloat16),
        in_specs=[VMEM],
        out_specs=VMEM,
        scratch_shapes=[pltpu.VMEM((3, cols_t, LANES), jnp.float32)],
        compiler_params=grant((p_tiles + 8, cols_t // 2, LANES), centroids.shape),
        cost_estimate=pl.CostEstimate(flops=16 * entries, bytes_accessed=2 * entries, transcendentals=3 * entries),
    )(lines)

    parts, halo = pl.pallas_call(
        functools.partial(t_kernel, norm=norm, slots=slots, count=count),
        out_shape=(
            jax.ShapeDtypeStruct((excitations, rows_t + LANES), jnp.bfloat16),
            jax.ShapeDtypeStruct((2, excitations, LANES), jnp.float32),
        ),
        in_specs=[VMEM] * (count + 2) + [SMEM],
        out_specs=(VMEM, VMEM),
        scratch_shapes=[
            pltpu.VMEM((slots + 2, moments.shape[0] * excitations, cols_t), jnp.bfloat16),
            pltpu.VMEM((count, 2, excitations, LANES), jnp.float32),
        ],
        compiler_params=grant(
            (p_tiles + 2, cols_t // 2, LANES),
            (excitations, rows_t),
            (slots + 2, moments.shape[0] * excitations, cols_t),
            moments.shape,
        ),
    )(*everyone, t_tiles, moments, shell)
    parts = exchange(parts, "col")
    s_tiles = pl.pallas_call(
        s_tiles_kernel,
        out_shape=jax.ShapeDtypeStruct((rows_t, cols_t), jnp.bfloat16),
        in_specs=[VMEM],
        out_specs=VMEM,
        scratch_shapes=[pltpu.VMEM((3, LANES, LANES), jnp.float32)],
        compiler_params=grant((rows_t, cols_t // 2), centroids.shape),
        cost_estimate=pl.CostEstimate(flops=12 * entries, bytes_accessed=2 * entries, transcendentals=2 * entries),
    )(late(centroids, parts[0]))

    own_dual, *shares = pl.pallas_call(
        functools.partial(sweep_kernel, slots=slots, part_count=len(parts), count=count),
        out_shape=[jax.ShapeDtypeStruct((excitations, shard_len), jnp.float32)] * 2
        + [jax.ShapeDtypeStruct((excitations, shard_len), jnp.bfloat16)] * (count - 1),
        in_specs=[VMEM] * (len(parts) + 6),
        out_specs=[VMEM] * (count + 1),
        scratch_shapes=[
            pltpu.VMEM((p_tiles, excitations, LANES), jnp.float32),
            pltpu.VMEM((dual_moments.shape[0] * excitations, rows_t), jnp.bfloat16),
            pltpu.VMEM((q_tiles, excitations, LANES), jnp.float32),
        ],
        compiler_params=grant((col_devices, excitations, rows_t), (rows_t, cols_t // 2), (excitations, 8 * rows_t)),
    )(*parts, halo, gram_diag, gram_off, neighbours, s_tiles, dual_moments)
    for step in sorted(range(1, count), key=lambda step: (1 - step % 2, step)):
        shares[step] = swap(shares[step], "row", step)
    march_rhs = pl.pallas_call(
        functools.partial(final_kernel, norm=norm),
        out_shape=jax.ShapeDtypeStruct(incident.shape, jnp.float32),
        in_specs=[VMEM] * (count + 1),
        out_specs=VMEM,
        compiler_params=grant((count, excitations, shard_len)),
    )(*shares, incident)
    return (march_rhs, own_dual)


def solution(mesh):
    placed = (
        P(None, None, ("col", "row")),
        P(None, ("col", "row")),
        P(),
        P(),
        P(),
        P("row", "col"),
        P("row", "col"),
        P(None, "row"),
        P("row"),
        P(None, "row"),
    )
    return jax.shard_map(
        per_device,
        mesh=mesh,
        in_specs=placed,
        out_specs=(P(None, ("col", "row")), P(None, ("row", "col"))),
        check_vma=False,
    )
```

```python
import functools
import math

import jax
import jax.numpy as jnp
from jax import lax
from jax.experimental import pallas as pl
from jax.experimental.pallas import tpu as pltpu
from jax.sharding import PartitionSpec as P

SWEEPS = 2

SOFT_T = 0.05
SOFT_S = 0.1
NEAR_GAIN = 2.0
NEAR_REACH = 0.5

LANES = 128
HALF = LANES // 2
CHUNK = 64

VMEM = pl.BlockSpec(memory_space=pltpu.VMEM)
SMEM = pl.BlockSpec(memory_space=pltpu.SMEM)
LOG2_E = 1.4426950408889634
TINY = 1e-30
MIB = 1024 * 1024


def grant(*shapes):
    total = 0
    for shape in shapes:
        size = 4
        for extent in shape[:-2] + (-(-shape[-2] // 8) * 8, shape[-1]):
            size *= extent
        total += size
    return pltpu.CompilerParams(vmem_limit_bytes=min(56 * MIB, 2 * total + 2 * MIB))


def root(square):
    square = jnp.maximum(square, TINY)
    return square * lax.rsqrt(square)


def inverse(value):
    return pl.reciprocal(value, approx=True)


def lane_ids(rows=1):
    return lax.broadcasted_iota(jnp.int32, (rows, LANES), 1)


def tile_at(start):
    return pl.ds(pl.multiple_of(start, LANES), LANES)


def edges(ref, row, length):
    first = ref[row : row + 1, :LANES]
    last = ref[row : row + 1, length - LANES :]
    return jnp.where(lane_ids() < HALF, first, last)


def split3(value):
    high = value.astype(jnp.bfloat16).astype(jnp.float32)
    rest = value - high
    middle = rest.astype(jnp.bfloat16).astype(jnp.float32)
    return [high, middle, rest - middle]


def stack_rows(rows, height):
    row_ids = lax.broadcasted_iota(jnp.int32, (height, LANES), 0)
    out = jnp.zeros((height, LANES), jnp.float32)
    for position, row in enumerate(rows):
        out = jnp.where(row_ids == position, row, out)
    return out


def pack_kernel(history_ref, shell_ref, near_ref, diag_ref, off_ref, links_ref, centroids_ref, out_ref, lines_ref):
    slots, excitations = history_ref.shape[:2]
    length = diag_ref.shape[1]
    tiles = shell_ref.shape[1]
    lanes = lane_ids()
    rows = []
    for tile in (0, tiles - 1):
        code = jnp.zeros((1, LANES), jnp.float32)
        for j in range(shell_ref.shape[0]):
            value = (shell_ref[j, tile] + slots * near_ref[j, tile]).astype(jnp.float32)
            code = jnp.where(lanes == j, value, code)
        rows.append(code)
    here = lax.axis_index("row") * length + jnp.where(lanes < HALF, lanes, length - LANES + lanes)
    for m in range(links_ref.shape[0]):
        rows.append((edges(links_ref, m, length) - here).astype(jnp.float32))
    rows += split3(edges(diag_ref, 0, length))
    coupling = []
    for m in range(off_ref.shape[0]):
        coupling += split3(edges(off_ref, m, length))
    out_ref[:slots] = history_ref[...]
    out_ref[slots] = stack_rows(rows, excitations).astype(jnp.bfloat16)
    out_ref[slots + 1] = stack_rows(coupling, excitations).astype(jnp.bfloat16)
    me = lax.axis_index("row")
    row_start = me * length
    q_tiles = shell_ref.shape[0]
    col_start = lax.axis_index("col") * (q_tiles * LANES)
    sources = [source_of(me, i, q_tiles) for i in range(q_tiles)]
    for t in range(tiles):
        for axis in range(3):
            lines_ref[3 * t + axis] = centroids_ref[axis, tile_at(row_start + t * LANES)]
    row = 3 * tiles
    for axis in range(3):
        lines_ref[row + axis : row + axis + 1] = halo_line(centroids_ref, axis, row_start, length)
    row += 3
    for i in range(q_tiles):
        for axis in range(3):
            lines_ref[row + axis] = centroids_ref[axis, tile_at(col_start + sources[i] * LANES)]
        row += 3
    for t in range(tiles):
        for i in range(q_tiles):
            gain = NEAR_GAIN * near_ref[sources[i], t].astype(jnp.float32)
            lines_ref[row : row + 1] = jnp.full((1, LANES), gain, jnp.float32)
            row += 1


def target_of(me, step, count):
    return me ^ step if count & (count - 1) == 0 else lax.rem(me + step, count)


def source_of(me, step, count):
    return me ^ step if count & (count - 1) == 0 else lax.rem(me + count - step, count)


def step_from(me, source, count):
    return me ^ source if count & (count - 1) == 0 else lax.rem(me + count - source, count)


def entries_t(line, column, gains):
    dx, dy, dz = [line[axis] - column[axis] for axis in range(3)]
    spacing = root(dx * dx + dy * dy + dz * dz)
    far, near = inverse(spacing + SOFT_T), jnp.exp2(spacing * (-LOG2_E / NEAR_REACH))
    return [(far + gain * near).astype(jnp.bfloat16) if gain is not None else far.astype(jnp.bfloat16) for gain in gains]


def columns(line):
    return jnp.broadcast_to(line, (LANES, LANES)).T


def halo_line(ref, row, row_start, length):
    total = ref.shape[1]
    right_start = lax.rem(row_start + length, total)
    left_start = lax.rem(row_start + total - LANES, total)
    return jnp.where(
        lane_ids() < HALF, ref[row : row + 1, tile_at(right_start)], ref[row : row + 1, tile_at(left_start)]
    )


def t_tiles_kernel(lines_ref, out_ref, column_ref, p_tiles, q_tiles):
    first_column = 3 * (p_tiles + 1)
    first_gain = first_column + 3 * q_tiles
    for i in range(q_tiles):
        for axis in range(3):
            row = first_column + 3 * i + axis
            column_ref[axis, i * LANES : (i + 1) * LANES, :] = columns(lines_ref[row : row + 1])

    def fill(first, gains_of):
        line = [lines_ref[pl.ds(3 * first + axis, 1)] for axis in range(3)]
        for i in range(q_tiles):
            gains = gains_of(i)
            for k in range(LANES // CHUNK):
                at = slice(i * LANES + k * CHUNK, i * LANES + (k + 1) * CHUNK)
                for offset, tile in enumerate(entries_t(line, [column_ref[axis, at, :] for axis in range(3)], gains)):
                    out_ref[first + offset, at, :] = tile

    group = max(1, 16 // q_tiles)
    while p_tiles % group:
        group -= 1

    def one_group(g, carry):
        for k in range(group):
            t = g * group + k
            fill(t, lambda i: [lines_ref[pl.ds(first_gain + t * q_tiles + i, 1)]])
        return carry

    lax.fori_loop(0, p_tiles // group, one_group, 0)
    fill(p_tiles, lambda i: [None, NEAR_GAIN])


def t_kernel(*refs, norm, slots, count):
    packed = [refs[order_of(count).index(step)] for step in range(count)]
    tiles_ref, moments_ref, shell_ref = refs[count : count + 3]
    out_ref, halo_ref, scaled_ref, edge_ref = refs[count + 3 :]
    q_tiles, p_tiles = shell_ref.shape
    excitations = out_ref.shape[0]
    kinds = moments_ref.shape[0]
    me = lax.axis_index("row")
    length = p_tiles * LANES
    row_start = me * length
    col_start = lax.axis_index("col") * (q_tiles * LANES)
    low = lane_ids() < HALF

    for i in range(count):
        edge_ref[i] = packed[i][slots:].astype(jnp.float32)
    right = edge_ref[step_from(me, lax.rem(me + 1, count), count)]
    left = edge_ref[step_from(me, lax.rem(me + count - 1, count), count)]
    halo_ref[...] = jnp.where(low[None], right, left)
    codes = right[0, 0:1], left[0, 1:2]
    nears = [jnp.where(code >= slots, 1.0, 0.0) for code in codes]
    picks = [code - slots * near for code, near in zip(codes, nears)]

    sources = [source_of(me, i, count) for i in range(count)]
    lanes = lane_ids()
    halo_tiles = []
    for i in range(count):
        at = slice(i * LANES, (i + 1) * LANES)
        weights = [moments_ref[a : a + 1, tile_at(col_start + sources[i] * LANES)] for a in range(kinds)]
        values = [packed[i][s].astype(jnp.float32) for s in range(slots)]
        here = lanes == sources[i]
        for pick in picks:
            choice = jnp.sum(jnp.where(here, pick, 0.0), axis=1, keepdims=True)
            value = values[0]
            for s in range(1, slots):
                value = jnp.where(choice == s, values[s], value)
            values.append(value)
        for s, value in enumerate(values):
            for a in range(kinds):
                scaled_ref[s, a * excitations : (a + 1) * excitations, at] = (weights[a] * value).astype(jnp.bfloat16)
        near_right, near_left = [jnp.sum(jnp.where(here, near, 0.0), axis=1, keepdims=True) for near in nears]
        near = jnp.where(low, near_right, near_left)
        halo_tiles.append(
            jnp.where(near > 0.5, tiles_ref[p_tiles + 1, at].astype(jnp.float32), tiles_ref[p_tiles, at].astype(jnp.float32))
            .astype(jnp.bfloat16)
        )

    def weighted(product, weights):
        field = weights[0] * product[:excitations]
        for a in range(1, kinds):
            term = weights[a] * product[a * excitations : (a + 1) * excitations]
            field = field + term if a < kinds - 1 else field - term
        return (field * norm).astype(jnp.bfloat16)

    def one_tile(t):
        lhs = jnp.concatenate(
            [scaled_ref[shell_ref[sources[i], t], :, i * LANES : (i + 1) * LANES] for i in range(count)], axis=1
        )
        weights = [moments_ref[a : a + 1, tile_at(row_start + t * LANES)] for a in range(kinds)]
        product = jnp.dot(lhs, tiles_ref[t], preferred_element_type=jnp.float32)
        out_ref[:, tile_at(t * LANES)] = weighted(product, weights)

    group = max(1, 32 // q_tiles)
    while p_tiles % group:
        group -= 1

    def one_group(g, carry):
        for k in range(group):
            one_tile(g * group + k)
        return carry

    if group == p_tiles:
        one_group(0, 0)
    else:
        lax.fori_loop(0, p_tiles // group, one_group, 0)
    halo_tile = jnp.concatenate(halo_tiles, axis=0)
    product = jnp.where(
        low,
        jnp.dot(scaled_ref[slots], halo_tile, preferred_element_type=jnp.float32),
        jnp.dot(scaled_ref[slots + 1], halo_tile, preferred_element_type=jnp.float32),
    )
    out_ref[:, length:] = weighted(product, [halo_line(moments_ref, a, row_start, length) for a in range(kinds)])


def s_tiles_kernel(centroids_ref, out_ref, column_ref):
    length, width = out_ref.shape
    row_start = lax.axis_index("row") * length
    col_start = lax.axis_index("col") * width

    def one_tile(t, carry):
        for axis in range(3):
            column_ref[axis] = columns(centroids_ref[axis : axis + 1, tile_at(row_start + t * LANES)])
        for k in range(width // LANES):
            line = [centroids_ref[axis : axis + 1, tile_at(col_start + k * LANES)] for axis in range(3)]
            for piece in range(LANES // CHUNK):
                at = slice(piece * CHUNK, (piece + 1) * CHUNK)
                dx = line[0] - column_ref[0, at, :]
                dy = line[1] - column_ref[1, at, :]
                dz = line[2] - column_ref[2, at, :]
                spacing = root(dx * dx + dy * dy + dz * dz)
                rows = pl.ds(pl.multiple_of(t * LANES + piece * CHUNK, CHUNK), CHUNK)
                out_ref[rows, k * LANES : (k + 1) * LANES] = inverse(spacing + SOFT_S).astype(jnp.bfloat16)
        return carry

    lax.fori_loop(0, length // LANES, one_tile, 0)


def sweep_kernel(*refs, slots, part_count, count):
    parts = refs[:part_count]
    halo_ref, diag_ref, off_ref, links_ref, tiles_ref, dual_moments_ref = refs[part_count : part_count + 6]
    dual_ref, *out_refs = refs[part_count + 6 : -3]
    iter_ref, scaled_ref, share_ref = refs[-3:]
    length = diag_ref.shape[1]
    tiles = length // LANES
    excitations = parts[0].shape[0]
    link_count = links_ref.shape[0]
    kinds = dual_moments_ref.shape[0]
    row_start = lax.axis_index("row") * length
    col_start = lax.axis_index("col") * tiles_ref.shape[1]
    lanes = lane_ids()
    low = lanes < HALF

    def halo(plane, row):
        return halo_ref[plane, row : row + 1]

    def sum3(plane, row):
        return halo(plane, row) + halo(plane, row + 1) + halo(plane, row + 2)

    def tile(t):
        return slice(t * LANES, (t + 1) * LANES)

    field, diag = [], []
    for t in range(tiles + 1):
        total = parts[0][:, tile(t)].astype(jnp.float32)
        for part in parts[1:]:
            total = total + part[:, tile(t)].astype(jnp.float32)
        field.append(total)
        diag.append(diag_ref[:, tile(t)] if t < tiles else sum3(0, 2 + link_count))

    dual = [f / d for f, d in zip(field, diag)]
    for sweep_id in range(SWEEPS):
        last = sweep_id == SWEEPS - 1
        updated = []
        for t in range(tiles if last else tiles + 1):
            around = jnp.where(low, dual[(t + 1) % (tiles + 1)], dual[t - 1])
            coupled = jnp.zeros_like(field[t])
            for m in range(link_count):
                if t < tiles:
                    source = links_ref[m : m + 1, tile(t)] - (row_start + t * LANES)
                    gram = off_ref[m : m + 1, tile(t)]
                else:
                    source = halo(0, 2 + m).astype(jnp.int32) + lanes
                    gram = sum3(1, 3 * m)
                inside = (source >= 0) & (source < LANES)
                index = jnp.broadcast_to(source & (LANES - 1), (excitations, LANES))
                here = jnp.take_along_axis(dual[t], index, axis=1)
                beside = jnp.take_along_axis(around, index, axis=1)
                coupled = coupled + gram * jnp.where(inside, here, beside)
            updated.append((field[t] - coupled) / diag[t])
        dual = updated

    for t in range(tiles):
        iter_ref[t] = dual[t]
        for a in range(kinds):
            weight = dual_moments_ref[a : a + 1, tile_at(row_start + t * LANES)]
            scaled_ref[a * excitations : (a + 1) * excitations, tile(t)] = (weight * dual[t]).astype(jnp.bfloat16)
    dual_ref[...] = iter_ref[lax.axis_index("col")]
    product = jnp.dot(scaled_ref[...], tiles_ref[...], preferred_element_type=jnp.float32)
    for k in range(count):
        term = jnp.zeros((excitations, LANES), jnp.float32)
        for a in range(kinds):
            weight = dual_moments_ref[a : a + 1, tile_at(col_start + k * LANES)]
            term = term + weight * product[a * excitations : (a + 1) * excitations, tile(k)]
        share_ref[k] = term
    me = lax.axis_index("row")
    for step, out_ref in enumerate(out_refs):
        out_ref[...] = share_ref[target_of(me, step, count)].astype(out_ref.dtype)


def final_kernel(*refs, norm):
    *share_refs, incident_ref, out_ref = refs
    total = share_refs[0][...].astype(jnp.float32)
    for share_ref in share_refs[1:]:
        total = total + share_ref[...].astype(jnp.float32)
    out_ref[...] = incident_ref[...] - total * norm


def swap(value, axis, step):
    count = lax.axis_size(axis)
    if count & (count - 1) == 0:
        pairs = [(i, i ^ step) for i in range(count)]
    else:
        pairs = [(i, (i + step) % count) for i in range(count)]
    return lax.ppermute(value, axis, pairs)


def order_of(count):
    return (0, 1, 3, 2) if count == 4 else tuple(range(count))


def exchange(value, axis):
    count = lax.axis_size(axis)
    if count == 1 or count & (count - 1):
        return [value] + [swap(value, axis, step) for step in range(1, count)]
    step = 1
    while step < count:
        radix = min(4, count // step)
        values = [value] + [swap(value, axis, step * k) for k in range(1, radix)]
        step *= radix
        if step < count:
            value = sum(values[k].astype(jnp.float32) for k in order_of(radix)).astype(value.dtype)
    return values


def late(value, after):
    return lax.optimization_barrier((value, after))[0]


def per_device(
    history,
    incident,
    centroids,
    moments,
    dual_moments,
    shell,
    near_mask,
    neighbours,
    gram_diag,
    gram_off,
):
    col_devices = lax.axis_size("col")
    slots, excitations, shard_len = history.shape
    p_tiles, q_tiles = shell.shape
    rows_t = gram_diag.shape[0]
    cols_t = q_tiles * LANES
    norm = 1.0 / math.sqrt(centroids.shape[1])
    shell, near_mask = shell.T, near_mask.T
    gram_diag = gram_diag.reshape(1, rows_t)

    line_rows = -(-(3 * (p_tiles + 1 + q_tiles) + p_tiles * q_tiles) // 8) * 8
    packed, lines = pl.pallas_call(
        pack_kernel,
        out_shape=(
            jax.ShapeDtypeStruct((slots + 2, excitations, shard_len), jnp.bfloat16),
            jax.ShapeDtypeStruct((line_rows, LANES), jnp.float32),
        ),
        in_specs=[VMEM, SMEM, SMEM, VMEM, VMEM, VMEM, VMEM],
        out_specs=(VMEM, VMEM),
        compiler_params=pltpu.CompilerParams(vmem_limit_bytes=56 * MIB),
    )(history, shell, near_mask, gram_diag, gram_off, neighbours, centroids)
    count = lax.axis_size("row")
    everyone = [packed] + [swap(packed, "row", step) for step in range(count - 1, 0, -1)][::-1]
    entries = rows_t * cols_t
    t_tiles = pl.pallas_call(
        functools.partial(t_tiles_kernel, p_tiles=p_tiles, q_tiles=q_tiles),
        out_shape=jax.ShapeDtypeStruct((p_tiles + 2, cols_t, LANES), jnp.bfloat16),
        in_specs=[VMEM],
        out_specs=VMEM,
        scratch_shapes=[pltpu.VMEM((3, cols_t, LANES), jnp.float32)],
        compiler_params=grant((p_tiles + 8, cols_t // 2, LANES), centroids.shape),
        cost_estimate=pl.CostEstimate(flops=16 * entries, bytes_accessed=2 * entries, transcendentals=3 * entries),
    )(lines)

    parts, halo = pl.pallas_call(
        functools.partial(t_kernel, norm=norm, slots=slots, count=count),
        out_shape=(
            jax.ShapeDtypeStruct((excitations, rows_t + LANES), jnp.bfloat16),
            jax.ShapeDtypeStruct((2, excitations, LANES), jnp.float32),
        ),
        in_specs=[VMEM] * (count + 2) + [SMEM],
        out_specs=(VMEM, VMEM),
        scratch_shapes=[
            pltpu.VMEM((slots + 2, moments.shape[0] * excitations, cols_t), jnp.bfloat16),
            pltpu.VMEM((count, 2, excitations, LANES), jnp.float32),
        ],
        compiler_params=grant(
            (p_tiles + 2, cols_t // 2, LANES),
            (excitations, rows_t),
            (slots + 2, moments.shape[0] * excitations, cols_t),
            moments.shape,
        ),
    )(*[everyone[step] for step in order_of(count)], t_tiles, moments, shell)
    parts = exchange(parts, "col")
    s_tiles = pl.pallas_call(
        s_tiles_kernel,
        out_shape=jax.ShapeDtypeStruct((rows_t, cols_t), jnp.bfloat16),
        in_specs=[VMEM],
        out_specs=VMEM,
        scratch_shapes=[pltpu.VMEM((3, LANES, LANES), jnp.float32)],
        compiler_params=grant((rows_t, cols_t // 2), centroids.shape),
        cost_estimate=pl.CostEstimate(flops=12 * entries, bytes_accessed=2 * entries, transcendentals=2 * entries),
    )(late(centroids, parts[0]))

    own_dual, *shares = pl.pallas_call(
        functools.partial(sweep_kernel, slots=slots, part_count=len(parts), count=count),
        out_shape=[jax.ShapeDtypeStruct((excitations, shard_len), jnp.float32)] * 2
        + [jax.ShapeDtypeStruct((excitations, shard_len), jnp.bfloat16)] * (count - 1),
        in_specs=[VMEM] * (len(parts) + 6),
        out_specs=[VMEM] * (count + 1),
        scratch_shapes=[
            pltpu.VMEM((p_tiles, excitations, LANES), jnp.float32),
            pltpu.VMEM((dual_moments.shape[0] * excitations, rows_t), jnp.bfloat16),
            pltpu.VMEM((q_tiles, excitations, LANES), jnp.float32),
        ],
        compiler_params=grant((col_devices, excitations, rows_t), (rows_t, cols_t // 2), (excitations, 8 * rows_t)),
    )(*parts, halo, gram_diag, gram_off, neighbours, s_tiles, dual_moments)
    for step in sorted(range(1, count), key=lambda step: (1 - step % 2, step)):
        shares[step] = swap(shares[step], "row", step)
    march_rhs = pl.pallas_call(
        functools.partial(final_kernel, norm=norm),
        out_shape=jax.ShapeDtypeStruct(incident.shape, jnp.float32),
        in_specs=[VMEM] * (count + 1),
        out_specs=VMEM,
        compiler_params=grant((count, excitations, shard_len)),
    )(*shares, incident)
    return (march_rhs, own_dual)


def solution(mesh):
    placed = (
        P(None, None, ("col", "row")),
        P(None, ("col", "row")),
        P(),
        P(),
        P(),
        P("row", "col"),
        P("row", "col"),
        P(None, "row"),
        P("row"),
        P(None, "row"),
    )
    return jax.shard_map(
        per_device,
        mesh=mesh,
        in_specs=placed,
        out_specs=(P(None, ("col", "row")), P(None, ("row", "col"))),
        check_vma=False,
    )
```

```python
import functools
import math

import jax
import jax.numpy as jnp
from jax import lax
from jax.experimental import pallas as pl
from jax.experimental.pallas import tpu as pltpu
from jax.sharding import PartitionSpec as P

SWEEPS = 2

SOFT_T = 0.05
SOFT_S = 0.1
NEAR_GAIN = 2.0
NEAR_REACH = 0.5

LANES = 128
HALF = LANES // 2
CHUNK = 64

VMEM = pl.BlockSpec(memory_space=pltpu.VMEM)
SMEM = pl.BlockSpec(memory_space=pltpu.SMEM)
LOG2_E = 1.4426950408889634
TINY = 1e-30
MIB = 1024 * 1024


def grant(*shapes):
    total = 0
    for shape in shapes:
        size = 4
        for extent in shape[:-2] + (-(-shape[-2] // 8) * 8, shape[-1]):
            size *= extent
        total += size
    return pltpu.CompilerParams(vmem_limit_bytes=min(56 * MIB, 2 * total + 2 * MIB))


def root(square):
    square = jnp.maximum(square, TINY)
    return square * lax.rsqrt(square)


def inverse(value):
    return pl.reciprocal(value, approx=True)


def lane_ids(rows=1):
    return lax.broadcasted_iota(jnp.int32, (rows, LANES), 1)


def tile_at(start):
    return pl.ds(pl.multiple_of(start, LANES), LANES)


def edges(ref, row, length):
    first = ref[row : row + 1, :LANES]
    last = ref[row : row + 1, length - LANES :]
    return jnp.where(lane_ids() < HALF, first, last)


def split3(value):
    high = value.astype(jnp.bfloat16).astype(jnp.float32)
    rest = value - high
    middle = rest.astype(jnp.bfloat16).astype(jnp.float32)
    return [high, middle, rest - middle]


def stack_rows(rows, height):
    row_ids = lax.broadcasted_iota(jnp.int32, (height, LANES), 0)
    out = jnp.zeros((height, LANES), jnp.float32)
    for position, row in enumerate(rows):
        out = jnp.where(row_ids == position, row, out)
    return out


def pack_kernel(history_ref, shell_ref, near_ref, diag_ref, off_ref, links_ref, centroids_ref, out_ref, lines_ref):
    slots, excitations = history_ref.shape[:2]
    length = diag_ref.shape[1]
    tiles = shell_ref.shape[1]
    lanes = lane_ids()
    rows = []
    for tile in (0, tiles - 1):
        code = jnp.zeros((1, LANES), jnp.float32)
        for j in range(shell_ref.shape[0]):
            value = (shell_ref[j, tile] + slots * near_ref[j, tile]).astype(jnp.float32)
            code = jnp.where(lanes == j, value, code)
        rows.append(code)
    here = lax.axis_index("row") * length + jnp.where(lanes < HALF, lanes, length - LANES + lanes)
    for m in range(links_ref.shape[0]):
        rows.append((edges(links_ref, m, length) - here).astype(jnp.float32))
    rows += split3(edges(diag_ref, 0, length))
    coupling = []
    for m in range(off_ref.shape[0]):
        coupling += split3(edges(off_ref, m, length))
    out_ref[:slots] = history_ref[...]
    out_ref[slots] = stack_rows(rows, excitations).astype(jnp.bfloat16)
    out_ref[slots + 1] = stack_rows(coupling, excitations).astype(jnp.bfloat16)
    me = lax.axis_index("row")
    row_start = me * length
    q_tiles = shell_ref.shape[0]
    col_start = lax.axis_index("col") * (q_tiles * LANES)
    sources = [source_of(me, i, q_tiles) for i in range(q_tiles)]
    for t in range(tiles):
        for axis in range(3):
            lines_ref[3 * t + axis] = centroids_ref[axis, tile_at(row_start + t * LANES)]
    row = 3 * tiles
    for axis in range(3):
        lines_ref[row + axis : row + axis + 1] = halo_line(centroids_ref, axis, row_start, length)
    row += 3
    for i in range(q_tiles):
        for axis in range(3):
            lines_ref[row + axis] = centroids_ref[axis, tile_at(col_start + sources[i] * LANES)]
        row += 3
    for t in range(tiles):
        for i in range(q_tiles):
            gain = NEAR_GAIN * near_ref[sources[i], t].astype(jnp.float32)
            lines_ref[row : row + 1] = jnp.full((1, LANES), gain, jnp.float32)
            row += 1


def target_of(me, step, count):
    return me ^ step if count & (count - 1) == 0 else lax.rem(me + step, count)


def source_of(me, step, count):
    return me ^ step if count & (count - 1) == 0 else lax.rem(me + count - step, count)


def step_from(me, source, count):
    return me ^ source if count & (count - 1) == 0 else lax.rem(me + count - source, count)


def entries_t(line, column, gains):
    dx, dy, dz = [line[axis] - column[axis] for axis in range(3)]
    spacing = root(dx * dx + dy * dy + dz * dz)
    far, near = inverse(spacing + SOFT_T), jnp.exp2(spacing * (-LOG2_E / NEAR_REACH))
    return [(far + gain * near).astype(jnp.bfloat16) if gain is not None else far.astype(jnp.bfloat16) for gain in gains]


def columns(line):
    return jnp.broadcast_to(line, (LANES, LANES)).T


def halo_line(ref, row, row_start, length):
    total = ref.shape[1]
    right_start = lax.rem(row_start + length, total)
    left_start = lax.rem(row_start + total - LANES, total)
    return jnp.where(
        lane_ids() < HALF, ref[row : row + 1, tile_at(right_start)], ref[row : row + 1, tile_at(left_start)]
    )


def t_tiles_kernel(lines_ref, out_ref, column_ref, p_tiles, q_tiles):
    first_column = 3 * (p_tiles + 1)
    first_gain = first_column + 3 * q_tiles
    for i in range(q_tiles):
        for axis in range(3):
            row = first_column + 3 * i + axis
            column_ref[axis, i * LANES : (i + 1) * LANES, :] = columns(lines_ref[row : row + 1])

    def fill(first, gains_of):
        line = [lines_ref[pl.ds(3 * first + axis, 1)] for axis in range(3)]
        for i in range(q_tiles):
            gains = gains_of(i)
            for k in range(LANES // CHUNK):
                at = slice(i * LANES + k * CHUNK, i * LANES + (k + 1) * CHUNK)
                for offset, tile in enumerate(entries_t(line, [column_ref[axis, at, :] for axis in range(3)], gains)):
                    out_ref[first + offset, at, :] = tile

    group = max(1, 16 // q_tiles)
    while p_tiles % group:
        group -= 1

    def one_group(g, carry):
        for k in range(group):
            t = g * group + k
            fill(t, lambda i: [lines_ref[pl.ds(first_gain + t * q_tiles + i, 1)]])
        return carry

    lax.fori_loop(0, p_tiles // group, one_group, 0)
    fill(p_tiles, lambda i: [None, NEAR_GAIN])


def t_kernel(*refs, norm, slots, count):
    packed = [refs[order_of(count).index(step)] for step in range(count)]
    tiles_ref, moments_ref, shell_ref = refs[count : count + 3]
    out_ref, halo_ref, scaled_ref, edge_ref = refs[count + 3 :]
    q_tiles, p_tiles = shell_ref.shape
    excitations = out_ref.shape[0]
    kinds = moments_ref.shape[0]
    me = lax.axis_index("row")
    length = p_tiles * LANES
    row_start = me * length
    col_start = lax.axis_index("col") * (q_tiles * LANES)
    low = lane_ids() < HALF

    for i in range(count):
        edge_ref[i] = packed[i][slots:].astype(jnp.float32)
    right = edge_ref[step_from(me, lax.rem(me + 1, count), count)]
    left = edge_ref[step_from(me, lax.rem(me + count - 1, count), count)]
    halo_ref[...] = jnp.where(low[None], right, left)
    codes = right[0, 0:1], left[0, 1:2]
    nears = [jnp.where(code >= slots, 1.0, 0.0) for code in codes]
    picks = [code - slots * near for code, near in zip(codes, nears)]

    sources = [source_of(me, i, count) for i in range(count)]
    lanes = lane_ids()
    halo_tiles = []
    for i in range(count):
        at = slice(i * LANES, (i + 1) * LANES)
        weights = [moments_ref[a : a + 1, tile_at(col_start + sources[i] * LANES)] for a in range(kinds)]
        values = [packed[i][s].astype(jnp.float32) for s in range(slots)]
        here = lanes == sources[i]
        for pick in picks:
            choice = jnp.sum(jnp.where(here, pick, 0.0), axis=1, keepdims=True)
            value = values[0]
            for s in range(1, slots):
                value = jnp.where(choice == s, values[s], value)
            values.append(value)
        for s, value in enumerate(values):
            for a in range(kinds):
                scaled_ref[s, a * excitations : (a + 1) * excitations, at] = (weights[a] * value).astype(jnp.bfloat16)
        near_right, near_left = [jnp.sum(jnp.where(here, near, 0.0), axis=1, keepdims=True) for near in nears]
        near = jnp.where(low, near_right, near_left)
        halo_tiles.append(
            jnp.where(near > 0.5, tiles_ref[p_tiles + 1, at].astype(jnp.float32), tiles_ref[p_tiles, at].astype(jnp.float32))
            .astype(jnp.bfloat16)
        )

    def weighted(product, weights):
        field = weights[0] * product[:excitations]
        for a in range(1, kinds):
            term = weights[a] * product[a * excitations : (a + 1) * excitations]
            field = field + term if a < kinds - 1 else field - term
        return (field * norm).astype(jnp.bfloat16)

    def one_tile(t):
        lhs = jnp.concatenate(
            [scaled_ref[shell_ref[sources[i], t], :, i * LANES : (i + 1) * LANES] for i in range(count)], axis=1
        )
        weights = [moments_ref[a : a + 1, tile_at(row_start + t * LANES)] for a in range(kinds)]
        product = jnp.dot(lhs, tiles_ref[t], preferred_element_type=jnp.float32)
        out_ref[:, tile_at(t * LANES)] = weighted(product, weights)

    group = max(1, 32 // q_tiles)
    while p_tiles % group:
        group -= 1

    def one_group(g, carry):
        for k in range(group):
            one_tile(g * group + k)
        return carry

    if group == p_tiles:
        one_group(0, 0)
    else:
        lax.fori_loop(0, p_tiles // group, one_group, 0)
    halo_tile = jnp.concatenate(halo_tiles, axis=0)
    product = jnp.where(
        low,
        jnp.dot(scaled_ref[slots], halo_tile, preferred_element_type=jnp.float32),
        jnp.dot(scaled_ref[slots + 1], halo_tile, preferred_element_type=jnp.float32),
    )
    out_ref[:, length:] = weighted(product, [halo_line(moments_ref, a, row_start, length) for a in range(kinds)])


def s_tiles_kernel(centroids_ref, out_ref, column_ref):
    length, width = out_ref.shape
    row_start = lax.axis_index("row") * length
    col_start = lax.axis_index("col") * width

    def one_tile(t, carry):
        for axis in range(3):
            column_ref[axis] = columns(centroids_ref[axis : axis + 1, tile_at(row_start + t * LANES)])
        for k in range(width // LANES):
            line = [centroids_ref[axis : axis + 1, tile_at(col_start + k * LANES)] for axis in range(3)]
            for piece in range(LANES // CHUNK):
                at = slice(piece * CHUNK, (piece + 1) * CHUNK)
                dx = line[0] - column_ref[0, at, :]
                dy = line[1] - column_ref[1, at, :]
                dz = line[2] - column_ref[2, at, :]
                spacing = root(dx * dx + dy * dy + dz * dz)
                rows = pl.ds(pl.multiple_of(t * LANES + piece * CHUNK, CHUNK), CHUNK)
                out_ref[rows, k * LANES : (k + 1) * LANES] = inverse(spacing + SOFT_S).astype(jnp.bfloat16)
        return carry

    lax.fori_loop(0, length // LANES, one_tile, 0)


def sweep_kernel(*refs, slots, part_count, count):
    parts = refs[:part_count]
    halo_ref, diag_ref, off_ref, links_ref, tiles_ref, dual_moments_ref = refs[part_count : part_count + 6]
    dual_ref, *out_refs = refs[part_count + 6 : -3]
    iter_ref, scaled_ref, share_ref = refs[-3:]
    length = diag_ref.shape[1]
    tiles = length // LANES
    excitations = parts[0].shape[0]
    link_count = links_ref.shape[0]
    kinds = dual_moments_ref.shape[0]
    row_start = lax.axis_index("row") * length
    col_start = lax.axis_index("col") * tiles_ref.shape[1]
    lanes = lane_ids()
    low = lanes < HALF

    def halo(plane, row):
        return halo_ref[plane, row : row + 1]

    def sum3(plane, row):
        return halo(plane, row) + halo(plane, row + 1) + halo(plane, row + 2)

    def tile(t):
        return slice(t * LANES, (t + 1) * LANES)

    field, diag = [], []
    for t in range(tiles + 1):
        total = parts[0][:, tile(t)].astype(jnp.float32)
        for part in parts[1:]:
            total = total + part[:, tile(t)].astype(jnp.float32)
        field.append(total)
        diag.append(diag_ref[:, tile(t)] if t < tiles else sum3(0, 2 + link_count))

    dual = [f / d for f, d in zip(field, diag)]
    for sweep_id in range(SWEEPS):
        last = sweep_id == SWEEPS - 1
        updated = []
        for t in range(tiles if last else tiles + 1):
            around = jnp.where(low, dual[(t + 1) % (tiles + 1)], dual[t - 1])
            coupled = jnp.zeros_like(field[t])
            for m in range(link_count):
                if t < tiles:
                    source = links_ref[m : m + 1, tile(t)] - (row_start + t * LANES)
                    gram = off_ref[m : m + 1, tile(t)]
                else:
                    source = halo(0, 2 + m).astype(jnp.int32) + lanes
                    gram = sum3(1, 3 * m)
                inside = (source >= 0) & (source < LANES)
                index = jnp.broadcast_to(source & (LANES - 1), (excitations, LANES))
                here = jnp.take_along_axis(dual[t], index, axis=1)
                beside = jnp.take_along_axis(around, index, axis=1)
                coupled = coupled + gram * jnp.where(inside, here, beside)
            updated.append((field[t] - coupled) / diag[t])
        dual = updated

    for t in range(tiles):
        iter_ref[t] = dual[t]
        for a in range(kinds):
            weight = dual_moments_ref[a : a + 1, tile_at(row_start + t * LANES)]
            scaled_ref[a * excitations : (a + 1) * excitations, tile(t)] = (weight * dual[t]).astype(jnp.bfloat16)
    dual_ref[...] = iter_ref[lax.axis_index("col")]
    product = jnp.dot(scaled_ref[...], tiles_ref[...], preferred_element_type=jnp.float32)
    for k in range(count):
        term = jnp.zeros((excitations, LANES), jnp.float32)
        for a in range(kinds):
            weight = dual_moments_ref[a : a + 1, tile_at(col_start + k * LANES)]
            term = term + weight * product[a * excitations : (a + 1) * excitations, tile(k)]
        share_ref[k] = term
    me = lax.axis_index("row")
    for step, out_ref in zip(last_steps(count), out_refs):
        out_ref[...] = share_ref[target_of(me, step, count)].astype(out_ref.dtype)


def final_kernel(*refs, norm):
    *share_refs, incident_ref, out_ref = refs
    total = share_refs[0][...].astype(jnp.float32)
    for share_ref in share_refs[1:]:
        total = total + share_ref[...].astype(jnp.float32)
    out_ref[...] = incident_ref[...] - total * norm


def swap(value, axis, step):
    count = lax.axis_size(axis)
    if count & (count - 1) == 0:
        pairs = [(i, i ^ step) for i in range(count)]
    else:
        pairs = [(i, (i + step) % count) for i in range(count)]
    return lax.ppermute(value, axis, pairs)


def order_of(count):
    return (0, 1, 3, 2) if count == 4 else tuple(range(count))


def last_steps(count):
    return (0,) + tuple(range(count - 1, 0, -1))


def exchange(value, axis):
    count = lax.axis_size(axis)
    if count == 1 or count & (count - 1):
        return [value] + [swap(value, axis, step) for step in range(1, count)]
    step = 1
    while step < count:
        radix = min(4, count // step)
        values = [value] + [swap(value, axis, step * k) for k in range(1, radix)]
        step *= radix
        if step < count:
            value = sum(values[k].astype(jnp.float32) for k in order_of(radix)).astype(value.dtype)
    return values


def late(value, after):
    return lax.optimization_barrier((value, after))[0]


def per_device(
    history,
    incident,
    centroids,
    moments,
    dual_moments,
    shell,
    near_mask,
    neighbours,
    gram_diag,
    gram_off,
):
    col_devices = lax.axis_size("col")
    slots, excitations, shard_len = history.shape
    p_tiles, q_tiles = shell.shape
    rows_t = gram_diag.shape[0]
    cols_t = q_tiles * LANES
    norm = 1.0 / math.sqrt(centroids.shape[1])
    shell, near_mask = shell.T, near_mask.T
    gram_diag = gram_diag.reshape(1, rows_t)

    line_rows = -(-(3 * (p_tiles + 1 + q_tiles) + p_tiles * q_tiles) // 8) * 8
    packed, lines = pl.pallas_call(
        pack_kernel,
        out_shape=(
            jax.ShapeDtypeStruct((slots + 2, excitations, shard_len), jnp.bfloat16),
            jax.ShapeDtypeStruct((line_rows, LANES), jnp.float32),
        ),
        in_specs=[VMEM, SMEM, SMEM, VMEM, VMEM, VMEM, VMEM],
        out_specs=(VMEM, VMEM),
        compiler_params=pltpu.CompilerParams(vmem_limit_bytes=56 * MIB),
    )(history, shell, near_mask, gram_diag, gram_off, neighbours, centroids)
    count = lax.axis_size("row")
    everyone = [packed] + [swap(packed, "row", step) for step in range(count - 1, 0, -1)][::-1]
    entries = rows_t * cols_t
    t_tiles = pl.pallas_call(
        functools.partial(t_tiles_kernel, p_tiles=p_tiles, q_tiles=q_tiles),
        out_shape=jax.ShapeDtypeStruct((p_tiles + 2, cols_t, LANES), jnp.bfloat16),
        in_specs=[VMEM],
        out_specs=VMEM,
        scratch_shapes=[pltpu.VMEM((3, cols_t, LANES), jnp.float32)],
        compiler_params=grant((p_tiles + 8, cols_t // 2, LANES), centroids.shape),
        cost_estimate=pl.CostEstimate(flops=16 * entries, bytes_accessed=2 * entries, transcendentals=3 * entries),
    )(lines)

    parts, halo = pl.pallas_call(
        functools.partial(t_kernel, norm=norm, slots=slots, count=count),
        out_shape=(
            jax.ShapeDtypeStruct((excitations, rows_t + LANES), jnp.bfloat16),
            jax.ShapeDtypeStruct((2, excitations, LANES), jnp.float32),
        ),
        in_specs=[VMEM] * (count + 2) + [SMEM],
        out_specs=(VMEM, VMEM),
        scratch_shapes=[
            pltpu.VMEM((slots + 2, moments.shape[0] * excitations, cols_t), jnp.bfloat16),
            pltpu.VMEM((count, 2, excitations, LANES), jnp.float32),
        ],
        compiler_params=grant(
            (p_tiles + 2, cols_t // 2, LANES),
            (excitations, rows_t),
            (slots + 2, moments.shape[0] * excitations, cols_t),
            moments.shape,
        ),
    )(*[everyone[step] for step in order_of(count)], t_tiles, moments, shell)
    parts = exchange(parts, "col")
    s_tiles = pl.pallas_call(
        s_tiles_kernel,
        out_shape=jax.ShapeDtypeStruct((rows_t, cols_t), jnp.bfloat16),
        in_specs=[VMEM],
        out_specs=VMEM,
        scratch_shapes=[pltpu.VMEM((3, LANES, LANES), jnp.float32)],
        compiler_params=grant((rows_t, cols_t // 2), centroids.shape),
        cost_estimate=pl.CostEstimate(flops=12 * entries, bytes_accessed=2 * entries, transcendentals=2 * entries),
    )(late(centroids, parts[0]))

    own_dual, *shares = pl.pallas_call(
        functools.partial(sweep_kernel, slots=slots, part_count=len(parts), count=count),
        out_shape=[jax.ShapeDtypeStruct((excitations, shard_len), jnp.float32)] * 2
        + [jax.ShapeDtypeStruct((excitations, shard_len), jnp.bfloat16)] * (count - 1),
        in_specs=[VMEM] * (len(parts) + 6),
        out_specs=[VMEM] * (count + 1),
        scratch_shapes=[
            pltpu.VMEM((p_tiles, excitations, LANES), jnp.float32),
            pltpu.VMEM((dual_moments.shape[0] * excitations, rows_t), jnp.bfloat16),
            pltpu.VMEM((q_tiles, excitations, LANES), jnp.float32),
        ],
        compiler_params=grant((col_devices, excitations, rows_t), (rows_t, cols_t // 2), (excitations, 8 * rows_t)),
    )(*parts, halo, gram_diag, gram_off, neighbours, s_tiles, dual_moments)
    shares = shares[:1] + [swap(share, "row", step) for step, share in zip(last_steps(count)[1:], shares[1:])]
    march_rhs = pl.pallas_call(
        functools.partial(final_kernel, norm=norm),
        out_shape=jax.ShapeDtypeStruct(incident.shape, jnp.float32),
        in_specs=[VMEM] * (count + 1),
        out_specs=VMEM,
        compiler_params=grant((count, excitations, shard_len)),
    )(*shares, incident)
    return (march_rhs, own_dual)


def solution(mesh):
    placed = (
        P(None, None, ("col", "row")),
        P(None, ("col", "row")),
        P(),
        P(),
        P(),
        P("row", "col"),
        P("row", "col"),
        P(None, "row"),
        P("row"),
        P(None, "row"),
    )
    return jax.shard_map(
        per_device,
        mesh=mesh,
        in_specs=placed,
        out_specs=(P(None, ("col", "row")), P(None, ("row", "col"))),
        check_vma=False,
    )
```

```python
import functools
import math

import jax
import jax.numpy as jnp
from jax import lax
from jax.experimental import pallas as pl
from jax.experimental.pallas import tpu as pltpu
from jax.sharding import PartitionSpec as P

SWEEPS = 2

SOFT_T = 0.05
SOFT_S = 0.1
NEAR_GAIN = 2.0
NEAR_REACH = 0.5

LANES = 128
HALF = LANES // 2
CHUNK = 64

VMEM = pl.BlockSpec(memory_space=pltpu.VMEM)
SMEM = pl.BlockSpec(memory_space=pltpu.SMEM)
ANY = pl.BlockSpec(memory_space=pl.ANY)
LOG2_E = 1.4426950408889634
TINY = 1e-30
MIB = 1024 * 1024


def grant(*shapes):
    total = 0
    for shape in shapes:
        size = 4
        for extent in shape[:-2] + (-(-shape[-2] // 8) * 8, shape[-1]):
            size *= extent
        total += size
    return pltpu.CompilerParams(vmem_limit_bytes=min(56 * MIB, 2 * total + 2 * MIB))


def root(square):
    square = jnp.maximum(square, TINY)
    return square * lax.rsqrt(square)


def inverse(value):
    return pl.reciprocal(value, approx=True)


def lane_ids(rows=1):
    return lax.broadcasted_iota(jnp.int32, (rows, LANES), 1)


def tile_at(start):
    return pl.ds(pl.multiple_of(start, LANES), LANES)


def edges(ref, row, length):
    first = ref[row : row + 1, :LANES]
    last = ref[row : row + 1, length - LANES :]
    return jnp.where(lane_ids() < HALF, first, last)


def split2(value):
    high = value.astype(jnp.bfloat16).astype(jnp.float32)
    return [high, value - high]


def stack_rows(rows, height):
    row_ids = lax.broadcasted_iota(jnp.int32, (height, LANES), 0)
    out = jnp.zeros((height, LANES), jnp.float32)
    for position, row in enumerate(rows):
        out = jnp.where(row_ids == position, row, out)
    return out


def pack_kernel(
    history_in, shell_in, near_in, diag_in, off_in, links_in, centroids_in, out_any, lines_any,
    shell_ref, near_ref, diag_ref, off_ref, links_ref, centroids_ref, edge_ref, lines_ref, sems,
):
    slots, excitations = history_in.shape[:2]
    pairs = (
        (centroids_in, centroids_ref),
        (near_in, near_ref),
        (shell_in, shell_ref),
        (links_in, links_ref),
        (diag_in, diag_ref),
        (off_in, off_ref),
        (history_in, out_any.at[pl.ds(0, slots)]),
        (edge_ref, out_any.at[pl.ds(slots, 1)]),
        (lines_ref, lines_any),
    )
    *reads, history_copy, edge_copy, lines_copy = [
        pltpu.make_async_copy(source, target, sems.at[k]) for k, (source, target) in enumerate(pairs)
    ]
    for read in reads:
        read.start()
    history_copy.start()
    for read in reads:
        read.wait()
    length = diag_ref.shape[1]
    tiles = shell_ref.shape[1]
    lanes = lane_ids()
    rows = []
    for tile in (0, tiles - 1):
        code = jnp.zeros((1, LANES), jnp.float32)
        for j in range(shell_ref.shape[0]):
            value = (shell_ref[j, tile] + slots * near_ref[j, tile]).astype(jnp.float32)
            code = jnp.where(lanes == j, value, code)
        rows.append(code)
    here = lax.axis_index("row") * length + jnp.where(lanes < HALF, lanes, length - LANES + lanes)
    for m in range(links_ref.shape[0]):
        rows.append((edges(links_ref, m, length) - here).astype(jnp.float32))
    rows += split2(edges(diag_ref, 0, length))
    for m in range(off_ref.shape[0]):
        rows += split2(edges(off_ref, m, length))
    edge_ref[0] = stack_rows(rows, excitations).astype(jnp.bfloat16)
    edge_copy.start()
    me = lax.axis_index("row")
    row_start = me * length
    q_tiles = shell_ref.shape[0]
    col_start = lax.axis_index("col") * (q_tiles * LANES)
    sources = [source_of(me, i, q_tiles) for i in range(q_tiles)]
    for t in range(tiles):
        for axis in range(3):
            lines_ref[3 * t + axis] = centroids_ref[axis, tile_at(row_start + t * LANES)]
    row = 3 * tiles
    for axis in range(3):
        lines_ref[row + axis : row + axis + 1] = halo_line(centroids_ref, axis, row_start, length)
    row += 3
    for i in range(q_tiles):
        for axis in range(3):
            lines_ref[row + axis] = centroids_ref[axis, tile_at(col_start + sources[i] * LANES)]
        row += 3
    for t in range(tiles):
        for i in range(q_tiles):
            gain = NEAR_GAIN * near_ref[sources[i], t].astype(jnp.float32)
            lines_ref[row : row + 1] = jnp.full((1, LANES), gain, jnp.float32)
            row += 1
    lines_copy.start()
    history_copy.wait()
    edge_copy.wait()
    lines_copy.wait()


def target_of(me, step, count):
    return me ^ step if count & (count - 1) == 0 else lax.rem(me + step, count)


def source_of(me, step, count):
    return me ^ step if count & (count - 1) == 0 else lax.rem(me + count - step, count)


def step_from(me, source, count):
    return me ^ source if count & (count - 1) == 0 else lax.rem(me + count - source, count)


def entries_t(line, column, gains):
    dx, dy, dz = [line[axis] - column[axis] for axis in range(3)]
    spacing = root(dx * dx + dy * dy + dz * dz)
    far, near = inverse(spacing + SOFT_T), jnp.exp2(spacing * (-LOG2_E / NEAR_REACH))
    return [(far + gain * near).astype(jnp.bfloat16) if gain is not None else far.astype(jnp.bfloat16) for gain in gains]


def columns(line):
    return jnp.broadcast_to(line, (LANES, LANES)).T


def halo_line(ref, row, row_start, length):
    total = ref.shape[1]
    right_start = lax.rem(row_start + length, total)
    left_start = lax.rem(row_start + total - LANES, total)
    return jnp.where(
        lane_ids() < HALF, ref[row : row + 1, tile_at(right_start)], ref[row : row + 1, tile_at(left_start)]
    )


def t_tiles_kernel(lines_ref, out_ref, column_ref, p_tiles, q_tiles):
    first_column = 3 * (p_tiles + 1)
    first_gain = first_column + 3 * q_tiles
    for i in range(q_tiles):
        for axis in range(3):
            row = first_column + 3 * i + axis
            column_ref[axis, i * LANES : (i + 1) * LANES, :] = columns(lines_ref[row : row + 1])

    def fill(first, gains_of):
        line = [lines_ref[pl.ds(3 * first + axis, 1)] for axis in range(3)]
        for i in range(q_tiles):
            gains = gains_of(i)
            for k in range(LANES // CHUNK):
                at = slice(i * LANES + k * CHUNK, i * LANES + (k + 1) * CHUNK)
                for offset, tile in enumerate(entries_t(line, [column_ref[axis, at, :] for axis in range(3)], gains)):
                    out_ref[first + offset, at, :] = tile

    group = max(1, 16 // q_tiles)
    while p_tiles % group:
        group -= 1

    def one_group(g, carry):
        for k in range(group):
            t = g * group + k
            fill(t, lambda i: [lines_ref[pl.ds(first_gain + t * q_tiles + i, 1)]])
        return carry

    lax.fori_loop(0, p_tiles // group, one_group, 0)
    fill(p_tiles, lambda i: [None, NEAR_GAIN])


def t_kernel(*refs, norm, slots, count):
    packed = [refs[order_of(count).index(step)] for step in range(count)]
    tiles_ref, moments_ref, shell_ref = refs[count : count + 3]
    out_ref, halo_ref, scaled_ref, edge_ref = refs[count + 3 :]
    q_tiles, p_tiles = shell_ref.shape
    excitations = out_ref.shape[0]
    kinds = moments_ref.shape[0]
    me = lax.axis_index("row")
    length = p_tiles * LANES
    row_start = me * length
    col_start = lax.axis_index("col") * (q_tiles * LANES)
    low = lane_ids() < HALF

    for i in range(count):
        edge_ref[i] = packed[i][slots:].astype(jnp.float32)
    right = edge_ref[step_from(me, lax.rem(me + 1, count), count)]
    left = edge_ref[step_from(me, lax.rem(me + count - 1, count), count)]
    halo_ref[...] = jnp.where(low[None], right, left)
    codes = right[0, 0:1], left[0, 1:2]
    nears = [jnp.where(code >= slots, 1.0, 0.0) for code in codes]
    picks = [code - slots * near for code, near in zip(codes, nears)]

    sources = [source_of(me, i, count) for i in range(count)]
    lanes = lane_ids()
    halo_tiles = []
    for i in range(count):
        at = slice(i * LANES, (i + 1) * LANES)
        weights = [moments_ref[a : a + 1, tile_at(col_start + sources[i] * LANES)] for a in range(kinds)]
        values = [packed[i][s].astype(jnp.float32) for s in range(slots)]
        here = lanes == sources[i]
        for pick in picks:
            choice = jnp.sum(jnp.where(here, pick, 0.0), axis=1, keepdims=True)
            value = values[0]
            for s in range(1, slots):
                value = jnp.where(choice == s, values[s], value)
            values.append(value)
        for s, value in enumerate(values):
            for a in range(kinds):
                scaled_ref[s, a * excitations : (a + 1) * excitations, at] = (weights[a] * value).astype(jnp.bfloat16)
        near_right, near_left = [jnp.sum(jnp.where(here, near, 0.0), axis=1, keepdims=True) for near in nears]
        near = jnp.where(low, near_right, near_left)
        halo_tiles.append(
            jnp.where(near > 0.5, tiles_ref[p_tiles + 1, at].astype(jnp.float32), tiles_ref[p_tiles, at].astype(jnp.float32))
            .astype(jnp.bfloat16)
        )

    def weighted(product, weights):
        field = weights[0] * product[:excitations]
        for a in range(1, kinds):
            term = weights[a] * product[a * excitations : (a + 1) * excitations]
            field = field + term if a < kinds - 1 else field - term
        return (field * norm).astype(jnp.bfloat16)

    def one_tile(t):
        lhs = jnp.concatenate(
            [scaled_ref[shell_ref[sources[i], t], :, i * LANES : (i + 1) * LANES] for i in range(count)], axis=1
        )
        weights = [moments_ref[a : a + 1, tile_at(row_start + t * LANES)] for a in range(kinds)]
        product = jnp.dot(lhs, tiles_ref[t], preferred_element_type=jnp.float32)
        out_ref[:, tile_at(t * LANES)] = weighted(product, weights)

    group = max(1, 32 // q_tiles)
    while p_tiles % group:
        group -= 1

    def one_group(g, carry):
        for k in range(group):
            one_tile(g * group + k)
        return carry

    if group == p_tiles:
        one_group(0, 0)
    else:
        lax.fori_loop(0, p_tiles // group, one_group, 0)
    halo_tile = jnp.concatenate(halo_tiles, axis=0)
    product = jnp.where(
        low,
        jnp.dot(scaled_ref[slots], halo_tile, preferred_element_type=jnp.float32),
        jnp.dot(scaled_ref[slots + 1], halo_tile, preferred_element_type=jnp.float32),
    )
    out_ref[:, length:] = weighted(product, [halo_line(moments_ref, a, row_start, length) for a in range(kinds)])


def s_tiles_kernel(centroids_ref, out_ref, column_ref):
    length, width = out_ref.shape
    row_start = lax.axis_index("row") * length
    col_start = lax.axis_index("col") * width

    def one_tile(t, carry):
        for axis in range(3):
            column_ref[axis] = columns(centroids_ref[axis : axis + 1, tile_at(row_start + t * LANES)])
        for k in range(width // LANES):
            line = [centroids_ref[axis : axis + 1, tile_at(col_start + k * LANES)] for axis in range(3)]
            for piece in range(LANES // CHUNK):
                at = slice(piece * CHUNK, (piece + 1) * CHUNK)
                dx = line[0] - column_ref[0, at, :]
                dy = line[1] - column_ref[1, at, :]
                dz = line[2] - column_ref[2, at, :]
                spacing = root(dx * dx + dy * dy + dz * dz)
                rows = pl.ds(pl.multiple_of(t * LANES + piece * CHUNK, CHUNK), CHUNK)
                out_ref[rows, k * LANES : (k + 1) * LANES] = inverse(spacing + SOFT_S).astype(jnp.bfloat16)
        return carry

    lax.fori_loop(0, length // LANES, one_tile, 0)


def sweep_kernel(*refs, slots, part_count, count):
    parts = refs[:part_count]
    halo_ref, diag_ref, off_ref, links_ref, tiles_ref, dual_moments_ref = refs[part_count : part_count + 6]
    dual_ref, *out_refs = refs[part_count + 6 : -3]
    iter_ref, scaled_ref, share_ref = refs[-3:]
    length = diag_ref.shape[1]
    tiles = length // LANES
    excitations = parts[0].shape[0]
    link_count = links_ref.shape[0]
    kinds = dual_moments_ref.shape[0]
    row_start = lax.axis_index("row") * length
    col_start = lax.axis_index("col") * tiles_ref.shape[1]
    lanes = lane_ids()
    low = lanes < HALF

    def halo(row):
        return halo_ref[0, row : row + 1]

    def sum2(row):
        return halo(row) + halo(row + 1)

    def tile(t):
        return slice(t * LANES, (t + 1) * LANES)

    field, diag = [], []
    for t in range(tiles + 1):
        total = parts[0][:, tile(t)].astype(jnp.float32)
        for part in parts[1:]:
            total = total + part[:, tile(t)].astype(jnp.float32)
        field.append(total)
        diag.append(diag_ref[:, tile(t)] if t < tiles else sum2(2 + link_count))

    dual = [f / d for f, d in zip(field, diag)]
    for sweep_id in range(SWEEPS):
        last = sweep_id == SWEEPS - 1
        updated = []
        for t in range(tiles if last else tiles + 1):
            around = jnp.where(low, dual[(t + 1) % (tiles + 1)], dual[t - 1])
            coupled = jnp.zeros_like(field[t])
            for m in range(link_count):
                if t < tiles:
                    source = links_ref[m : m + 1, tile(t)] - (row_start + t * LANES)
                    gram = off_ref[m : m + 1, tile(t)]
                else:
                    source = halo(2 + m).astype(jnp.int32) + lanes
                    gram = sum2(4 + link_count + 2 * m)
                inside = (source >= 0) & (source < LANES)
                index = jnp.broadcast_to(source & (LANES - 1), (excitations, LANES))
                here = jnp.take_along_axis(dual[t], index, axis=1)
                beside = jnp.take_along_axis(around, index, axis=1)
                coupled = coupled + gram * jnp.where(inside, here, beside)
            updated.append((field[t] - coupled) / diag[t])
        dual = updated

    for t in range(tiles):
        iter_ref[t] = dual[t]
        for a in range(kinds):
            weight = dual_moments_ref[a : a + 1, tile_at(row_start + t * LANES)]
            scaled_ref[a * excitations : (a + 1) * excitations, tile(t)] = (weight * dual[t]).astype(jnp.bfloat16)
    dual_ref[...] = iter_ref[lax.axis_index("col")]
    product = jnp.dot(scaled_ref[...], tiles_ref[...], preferred_element_type=jnp.float32)
    for k in range(count):
        term = jnp.zeros((excitations, LANES), jnp.float32)
        for a in range(kinds):
            weight = dual_moments_ref[a : a + 1, tile_at(col_start + k * LANES)]
            term = term + weight * product[a * excitations : (a + 1) * excitations, tile(k)]
        share_ref[k] = term
    me = lax.axis_index("row")
    for step, out_ref in zip(last_steps(count), out_refs):
        out_ref[...] = share_ref[target_of(me, step, count)].astype(out_ref.dtype)


def final_kernel(*refs, norm):
    *share_refs, incident_ref, out_ref = refs
    total = share_refs[0][...].astype(jnp.float32)
    for share_ref in share_refs[1:]:
        total = total + share_ref[...].astype(jnp.float32)
    out_ref[...] = incident_ref[...] - total * norm


def swap(value, axis, step):
    count = lax.axis_size(axis)
    if count & (count - 1) == 0:
        pairs = [(i, i ^ step) for i in range(count)]
    else:
        pairs = [(i, (i + step) % count) for i in range(count)]
    return lax.ppermute(value, axis, pairs)


def order_of(count):
    return (0, 1, 3, 2) if count == 4 else tuple(range(count))


def last_steps(count):
    return (0,) + tuple(range(count - 1, 0, -1))


def exchange(value, axis):
    count = lax.axis_size(axis)
    if count == 1 or count & (count - 1):
        return [value] + [swap(value, axis, step) for step in range(1, count)]
    step = 1
    while step < count:
        radix = min(4, count // step)
        values = [value] + [swap(value, axis, step * k) for k in range(1, radix)]
        step *= radix
        if step < count:
            value = sum(values[k].astype(jnp.float32) for k in order_of(radix)).astype(value.dtype)
    return values


def late(value, after):
    return lax.optimization_barrier((value, after))[0]


def per_device(
    history,
    incident,
    centroids,
    moments,
    dual_moments,
    shell,
    near_mask,
    neighbours,
    gram_diag,
    gram_off,
):
    col_devices = lax.axis_size("col")
    slots, excitations, shard_len = history.shape
    p_tiles, q_tiles = shell.shape
    rows_t = gram_diag.shape[0]
    cols_t = q_tiles * LANES
    norm = 1.0 / math.sqrt(centroids.shape[1])
    shell, near_mask = shell.T, near_mask.T
    gram_diag = gram_diag.reshape(1, rows_t)

    line_rows = -(-(3 * (p_tiles + 1 + q_tiles) + p_tiles * q_tiles) // 8) * 8
    packed, lines = pl.pallas_call(
        pack_kernel,
        out_shape=(
            jax.ShapeDtypeStruct((slots + 1, excitations, shard_len), jnp.bfloat16),
            jax.ShapeDtypeStruct((line_rows, LANES), jnp.float32),
        ),
        in_specs=[ANY] * 7,
        out_specs=(ANY, ANY),
        scratch_shapes=[
            pltpu.SMEM(shell.shape, jnp.int32),
            pltpu.SMEM(shell.shape, jnp.int32),
            pltpu.VMEM(gram_diag.shape, jnp.float32),
            pltpu.VMEM(gram_off.shape, jnp.float32),
            pltpu.VMEM(neighbours.shape, jnp.int32),
            pltpu.VMEM(centroids.shape, jnp.float32),
            pltpu.VMEM((1, excitations, LANES), jnp.bfloat16),
            pltpu.VMEM((line_rows, LANES), jnp.float32),
            pltpu.SemaphoreType.DMA((9,)),
        ],
        compiler_params=pltpu.CompilerParams(vmem_limit_bytes=56 * MIB),
    )(history, shell, near_mask, gram_diag, gram_off, neighbours, centroids)
    count = lax.axis_size("row")
    everyone = [packed] + [swap(packed, "row", step) for step in range(count - 1, 0, -1)][::-1]
    entries = rows_t * cols_t
    t_tiles = pl.pallas_call(
        functools.partial(t_tiles_kernel, p_tiles=p_tiles, q_tiles=q_tiles),
        out_shape=jax.ShapeDtypeStruct((p_tiles + 2, cols_t, LANES), jnp.bfloat16),
        in_specs=[VMEM],
        out_specs=VMEM,
        scratch_shapes=[pltpu.VMEM((3, cols_t, LANES), jnp.float32)],
        compiler_params=grant((p_tiles + 8, cols_t // 2, LANES), centroids.shape),
        cost_estimate=pl.CostEstimate(flops=16 * entries, bytes_accessed=2 * entries, transcendentals=3 * entries),
    )(lines)

    parts, halo = pl.pallas_call(
        functools.partial(t_kernel, norm=norm, slots=slots, count=count),
        out_shape=(
            jax.ShapeDtypeStruct((excitations, rows_t + LANES), jnp.bfloat16),
            jax.ShapeDtypeStruct((1, excitations, LANES), jnp.float32),
        ),
        in_specs=[VMEM] * (count + 2) + [SMEM],
        out_specs=(VMEM, VMEM),
        scratch_shapes=[
            pltpu.VMEM((slots + 2, moments.shape[0] * excitations, cols_t), jnp.bfloat16),
            pltpu.VMEM((count, 1, excitations, LANES), jnp.float32),
        ],
        compiler_params=grant(
            (p_tiles + 2, cols_t // 2, LANES),
            (excitations, rows_t),
            (slots + 2, moments.shape[0] * excitations, cols_t),
            moments.shape,
        ),
    )(*[everyone[step] for step in order_of(count)], t_tiles, moments, shell)
    parts = exchange(parts, "col")
    s_tiles = pl.pallas_call(
        s_tiles_kernel,
        out_shape=jax.ShapeDtypeStruct((rows_t, cols_t), jnp.bfloat16),
        in_specs=[VMEM],
        out_specs=VMEM,
        scratch_shapes=[pltpu.VMEM((3, LANES, LANES), jnp.float32)],
        compiler_params=grant((rows_t, cols_t // 2), centroids.shape),
        cost_estimate=pl.CostEstimate(flops=12 * entries, bytes_accessed=2 * entries, transcendentals=2 * entries),
    )(late(centroids, parts[0]))

    own_dual, *shares = pl.pallas_call(
        functools.partial(sweep_kernel, slots=slots, part_count=len(parts), count=count),
        out_shape=[jax.ShapeDtypeStruct((excitations, shard_len), jnp.float32)] * 2
        + [jax.ShapeDtypeStruct((excitations, shard_len), jnp.bfloat16)] * (count - 1),
        in_specs=[VMEM] * (len(parts) + 6),
        out_specs=[VMEM] * (count + 1),
        scratch_shapes=[
            pltpu.VMEM((p_tiles, excitations, LANES), jnp.float32),
            pltpu.VMEM((dual_moments.shape[0] * excitations, rows_t), jnp.bfloat16),
            pltpu.VMEM((q_tiles, excitations, LANES), jnp.float32),
        ],
        compiler_params=grant((col_devices, excitations, rows_t), (rows_t, cols_t // 2), (excitations, 8 * rows_t)),
    )(*parts, halo, gram_diag, gram_off, neighbours, s_tiles, dual_moments)
    shares = shares[:1] + [swap(share, "row", step) for step, share in zip(last_steps(count)[1:], shares[1:])]
    march_rhs = pl.pallas_call(
        functools.partial(final_kernel, norm=norm),
        out_shape=jax.ShapeDtypeStruct(incident.shape, jnp.float32),
        in_specs=[VMEM] * (count + 1),
        out_specs=VMEM,
        compiler_params=grant((count, excitations, shard_len)),
    )(*shares, incident)
    return (march_rhs, own_dual)


def solution(mesh):
    placed = (
        P(None, None, ("col", "row")),
        P(None, ("col", "row")),
        P(),
        P(),
        P(),
        P("row", "col"),
        P("row", "col"),
        P(None, "row"),
        P("row"),
        P(None, "row"),
    )
    return jax.shard_map(
        per_device,
        mesh=mesh,
        in_specs=placed,
        out_specs=(P(None, ("col", "row")), P(None, ("row", "col"))),
        check_vma=False,
    )
```

```python
import functools
import math

import jax
import jax.numpy as jnp
from jax import lax
from jax.experimental import pallas as pl
from jax.experimental.pallas import tpu as pltpu
from jax.sharding import PartitionSpec as P

SWEEPS = 2

SOFT_T = 0.05
SOFT_S = 0.1
NEAR_GAIN = 2.0
NEAR_REACH = 0.5

LANES = 128
HALF = LANES // 2
CHUNK = 64

VMEM = pl.BlockSpec(memory_space=pltpu.VMEM)
SMEM = pl.BlockSpec(memory_space=pltpu.SMEM)
LOG2_E = 1.4426950408889634
TINY = 1e-30
MIB = 1024 * 1024


def grant(*shapes):
    total = 0
    for shape in shapes:
        size = 4
        for extent in shape[:-2] + (-(-shape[-2] // 8) * 8, shape[-1]):
            size *= extent
        total += size
    return pltpu.CompilerParams(vmem_limit_bytes=min(56 * MIB, 2 * total + 2 * MIB))


def root(square):
    square = jnp.maximum(square, TINY)
    return square * lax.rsqrt(square)


def inverse(value):
    return pl.reciprocal(value, approx=True)


def lane_ids(rows=1):
    return lax.broadcasted_iota(jnp.int32, (rows, LANES), 1)


def tile_at(start):
    return pl.ds(pl.multiple_of(start, LANES), LANES)


def edges(ref, row, length):
    first = ref[row : row + 1, :LANES]
    last = ref[row : row + 1, length - LANES :]
    return jnp.where(lane_ids() < HALF, first, last)


def split2(value):
    high = value.astype(jnp.bfloat16).astype(jnp.float32)
    return [high, value - high]


def stack_rows(rows, height):
    row_ids = lax.broadcasted_iota(jnp.int32, (height, LANES), 0)
    out = jnp.zeros((height, LANES), jnp.float32)
    for position, row in enumerate(rows):
        out = jnp.where(row_ids == position, row, out)
    return out


def pack_kernel(history_ref, shell_ref, near_ref, diag_ref, off_ref, links_ref, centroids_ref, out_ref, lines_ref):
    slots, excitations = history_ref.shape[:2]
    length = diag_ref.shape[1]
    tiles = shell_ref.shape[1]
    lanes = lane_ids()
    rows = []
    for tile in (0, tiles - 1):
        code = jnp.zeros((1, LANES), jnp.float32)
        for j in range(shell_ref.shape[0]):
            value = (shell_ref[j, tile] + slots * near_ref[j, tile]).astype(jnp.float32)
            code = jnp.where(lanes == j, value, code)
        rows.append(code)
    here = lax.axis_index("row") * length + jnp.where(lanes < HALF, lanes, length - LANES + lanes)
    for m in range(links_ref.shape[0]):
        rows.append((edges(links_ref, m, length) - here).astype(jnp.float32))
    rows += split2(edges(diag_ref, 0, length))
    for m in range(off_ref.shape[0]):
        rows += split2(edges(off_ref, m, length))
    out_ref[:slots] = history_ref[...]
    out_ref[slots] = stack_rows(rows, excitations).astype(jnp.bfloat16)
    me = lax.axis_index("row")
    row_start = me * length
    q_tiles = shell_ref.shape[0]
    col_start = lax.axis_index("col") * (q_tiles * LANES)
    sources = [source_of(me, i, q_tiles) for i in range(q_tiles)]
    for t in range(tiles):
        for axis in range(3):
            lines_ref[3 * t + axis] = centroids_ref[axis, tile_at(row_start + t * LANES)]
    row = 3 * tiles
    for axis in range(3):
        lines_ref[row + axis : row + axis + 1] = halo_line(centroids_ref, axis, row_start, length)
    row += 3
    for i in range(q_tiles):
        for axis in range(3):
            lines_ref[row + axis] = centroids_ref[axis, tile_at(col_start + sources[i] * LANES)]
        row += 3
    for t in range(tiles):
        for i in range(q_tiles):
            gain = NEAR_GAIN * near_ref[sources[i], t].astype(jnp.float32)
            lines_ref[row : row + 1] = jnp.full((1, LANES), gain, jnp.float32)
            row += 1


def target_of(me, step, count):
    return me ^ step if count & (count - 1) == 0 else lax.rem(me + step, count)


def source_of(me, step, count):
    return me ^ step if count & (count - 1) == 0 else lax.rem(me + count - step, count)


def step_from(me, source, count):
    return me ^ source if count & (count - 1) == 0 else lax.rem(me + count - source, count)


def entries_t(line, column, gains):
    dx, dy, dz = [line[axis] - column[axis] for axis in range(3)]
    spacing = root(dx * dx + dy * dy + dz * dz)
    far, near = inverse(spacing + SOFT_T), jnp.exp2(spacing * (-LOG2_E / NEAR_REACH))
    return [(far + gain * near).astype(jnp.bfloat16) if gain is not None else far.astype(jnp.bfloat16) for gain in gains]


def columns(line):
    return jnp.broadcast_to(line, (LANES, LANES)).T


def halo_line(ref, row, row_start, length):
    total = ref.shape[1]
    right_start = lax.rem(row_start + length, total)
    left_start = lax.rem(row_start + total - LANES, total)
    return jnp.where(
        lane_ids() < HALF, ref[row : row + 1, tile_at(right_start)], ref[row : row + 1, tile_at(left_start)]
    )


def t_tiles_kernel(lines_ref, out_ref, column_ref, p_tiles, q_tiles):
    first_column = 3 * (p_tiles + 1)
    first_gain = first_column + 3 * q_tiles
    for i in range(q_tiles):
        for axis in range(3):
            row = first_column + 3 * i + axis
            column_ref[axis, i * LANES : (i + 1) * LANES, :] = columns(lines_ref[row : row + 1])

    def fill(first, gains_of):
        line = [lines_ref[pl.ds(3 * first + axis, 1)] for axis in range(3)]
        for i in range(q_tiles):
            gains = gains_of(i)
            for k in range(LANES // CHUNK):
                at = slice(i * LANES + k * CHUNK, i * LANES + (k + 1) * CHUNK)
                for offset, tile in enumerate(entries_t(line, [column_ref[axis, at, :] for axis in range(3)], gains)):
                    out_ref[first + offset, at, :] = tile

    group = max(1, 16 // q_tiles)
    while p_tiles % group:
        group -= 1

    def one_group(g, carry):
        for k in range(group):
            t = g * group + k
            fill(t, lambda i: [lines_ref[pl.ds(first_gain + t * q_tiles + i, 1)]])
        return carry

    lax.fori_loop(0, p_tiles // group, one_group, 0)
    fill(p_tiles, lambda i: [None, NEAR_GAIN])


def t_kernel(*refs, norm, slots, count):
    packed = [refs[order_of(count).index(step)] for step in range(count)]
    tiles_ref, moments_ref, shell_ref = refs[count : count + 3]
    out_ref, halo_ref, scaled_ref, edge_ref = refs[count + 3 :]
    q_tiles, p_tiles = shell_ref.shape
    excitations = out_ref.shape[0]
    kinds = moments_ref.shape[0]
    me = lax.axis_index("row")
    length = p_tiles * LANES
    row_start = me * length
    col_start = lax.axis_index("col") * (q_tiles * LANES)
    low = lane_ids() < HALF

    for i in range(count):
        edge_ref[i] = packed[i][slots:].astype(jnp.float32)
    right = edge_ref[step_from(me, lax.rem(me + 1, count), count)]
    left = edge_ref[step_from(me, lax.rem(me + count - 1, count), count)]
    halo_ref[...] = jnp.where(low[None], right, left)
    codes = right[0, 0:1], left[0, 1:2]
    nears = [jnp.where(code >= slots, 1.0, 0.0) for code in codes]
    picks = [code - slots * near for code, near in zip(codes, nears)]

    sources = [source_of(me, i, count) for i in range(count)]
    lanes = lane_ids()
    halo_tiles = []
    for i in range(count):
        at = slice(i * LANES, (i + 1) * LANES)
        weights = [moments_ref[a : a + 1, tile_at(col_start + sources[i] * LANES)] for a in range(kinds)]
        values = [packed[i][s].astype(jnp.float32) for s in range(slots)]
        here = lanes == sources[i]
        for pick in picks:
            choice = jnp.sum(jnp.where(here, pick, 0.0), axis=1, keepdims=True)
            value = values[0]
            for s in range(1, slots):
                value = jnp.where(choice == s, values[s], value)
            values.append(value)
        for s, value in enumerate(values):
            for a in range(kinds):
                scaled_ref[s, a * excitations : (a + 1) * excitations, at] = (weights[a] * value).astype(jnp.bfloat16)
        near_right, near_left = [jnp.sum(jnp.where(here, near, 0.0), axis=1, keepdims=True) for near in nears]
        near = jnp.where(low, near_right, near_left)
        halo_tiles.append(
            jnp.where(near > 0.5, tiles_ref[p_tiles + 1, at].astype(jnp.float32), tiles_ref[p_tiles, at].astype(jnp.float32))
            .astype(jnp.bfloat16)
        )

    def weighted(product, weights):
        field = weights[0] * product[:excitations]
        for a in range(1, kinds):
            term = weights[a] * product[a * excitations : (a + 1) * excitations]
            field = field + term if a < kinds - 1 else field - term
        return (field * norm).astype(jnp.bfloat16)

    def one_tile(t):
        lhs = jnp.concatenate(
            [scaled_ref[shell_ref[sources[i], t], :, i * LANES : (i + 1) * LANES] for i in range(count)], axis=1
        )
        weights = [moments_ref[a : a + 1, tile_at(row_start + t * LANES)] for a in range(kinds)]
        product = jnp.dot(lhs, tiles_ref[t], preferred_element_type=jnp.float32)
        out_ref[:, tile_at(t * LANES)] = weighted(product, weights)

    group = max(1, 32 // q_tiles)
    while p_tiles % group:
        group -= 1

    def one_group(g, carry):
        for k in range(group):
            one_tile(g * group + k)
        return carry

    if group == p_tiles:
        one_group(0, 0)
    else:
        lax.fori_loop(0, p_tiles // group, one_group, 0)
    halo_tile = jnp.concatenate(halo_tiles, axis=0)
    product = jnp.where(
        low,
        jnp.dot(scaled_ref[slots], halo_tile, preferred_element_type=jnp.float32),
        jnp.dot(scaled_ref[slots + 1], halo_tile, preferred_element_type=jnp.float32),
    )
    out_ref[:, length:] = weighted(product, [halo_line(moments_ref, a, row_start, length) for a in range(kinds)])


def s_tiles_kernel(centroids_ref, out_ref, column_ref):
    length, width = out_ref.shape
    row_start = lax.axis_index("row") * length
    col_start = lax.axis_index("col") * width

    def one_tile(t, carry):
        for axis in range(3):
            column_ref[axis] = columns(centroids_ref[axis : axis + 1, tile_at(row_start + t * LANES)])
        for k in range(width // LANES):
            line = [centroids_ref[axis : axis + 1, tile_at(col_start + k * LANES)] for axis in range(3)]
            for piece in range(LANES // CHUNK):
                at = slice(piece * CHUNK, (piece + 1) * CHUNK)
                dx = line[0] - column_ref[0, at, :]
                dy = line[1] - column_ref[1, at, :]
                dz = line[2] - column_ref[2, at, :]
                spacing = root(dx * dx + dy * dy + dz * dz)
                rows = pl.ds(pl.multiple_of(t * LANES + piece * CHUNK, CHUNK), CHUNK)
                out_ref[rows, k * LANES : (k + 1) * LANES] = inverse(spacing + SOFT_S).astype(jnp.bfloat16)
        return carry

    lax.fori_loop(0, length // LANES, one_tile, 0)


def sweep_kernel(*refs, slots, part_count, count):
    parts = refs[:part_count]
    halo_ref, diag_ref, off_ref, links_ref, tiles_ref, dual_moments_ref = refs[part_count : part_count + 6]
    dual_ref, *out_refs = refs[part_count + 6 : -3]
    iter_ref, scaled_ref, share_ref = refs[-3:]
    length = diag_ref.shape[1]
    tiles = length // LANES
    excitations = parts[0].shape[0]
    link_count = links_ref.shape[0]
    kinds = dual_moments_ref.shape[0]
    row_start = lax.axis_index("row") * length
    col_start = lax.axis_index("col") * tiles_ref.shape[1]
    lanes = lane_ids()
    low = lanes < HALF

    def halo(row):
        return halo_ref[0, row : row + 1]

    def sum2(row):
        return halo(row) + halo(row + 1)

    def tile(t):
        return slice(t * LANES, (t + 1) * LANES)

    field, diag = [], []
    for t in range(tiles + 1):
        total = parts[0][:, tile(t)].astype(jnp.float32)
        for part in parts[1:]:
            total = total + part[:, tile(t)].astype(jnp.float32)
        field.append(total)
        diag.append(diag_ref[:, tile(t)] if t < tiles else sum2(2 + link_count))

    dual = [f / d for f, d in zip(field, diag)]
    for sweep_id in range(SWEEPS):
        last = sweep_id == SWEEPS - 1
        updated = []
        for t in range(tiles if last else tiles + 1):
            around = jnp.where(low, dual[(t + 1) % (tiles + 1)], dual[t - 1])
            coupled = jnp.zeros_like(field[t])
            for m in range(link_count):
                if t < tiles:
                    source = links_ref[m : m + 1, tile(t)] - (row_start + t * LANES)
                    gram = off_ref[m : m + 1, tile(t)]
                else:
                    source = halo(2 + m).astype(jnp.int32) + lanes
                    gram = sum2(4 + link_count + 2 * m)
                inside = (source >= 0) & (source < LANES)
                index = jnp.broadcast_to(source & (LANES - 1), (excitations, LANES))
                here = jnp.take_along_axis(dual[t], index, axis=1)
                beside = jnp.take_along_axis(around, index, axis=1)
                coupled = coupled + gram * jnp.where(inside, here, beside)
            updated.append((field[t] - coupled) / diag[t])
        dual = updated

    for t in range(tiles):
        iter_ref[t] = dual[t]
        for a in range(kinds):
            weight = dual_moments_ref[a : a + 1, tile_at(row_start + t * LANES)]
            scaled_ref[a * excitations : (a + 1) * excitations, tile(t)] = (weight * dual[t]).astype(jnp.bfloat16)
    dual_ref[...] = iter_ref[lax.axis_index("col")]
    product = jnp.dot(scaled_ref[...], tiles_ref[...], preferred_element_type=jnp.float32)
    for k in range(count):
        term = jnp.zeros((excitations, LANES), jnp.float32)
        for a in range(kinds):
            weight = dual_moments_ref[a : a + 1, tile_at(col_start + k * LANES)]
            term = term + weight * product[a * excitations : (a + 1) * excitations, tile(k)]
        share_ref[k] = term
    me = lax.axis_index("row")
    for step, out_ref in zip(last_steps(count), out_refs):
        out_ref[...] = share_ref[target_of(me, step, count)].astype(out_ref.dtype)


def final_kernel(*refs, norm):
    *share_refs, dual_in_ref, incident_ref, out_ref, dual_ref = refs
    total = share_refs[0][...].astype(jnp.float32)
    for share_ref in share_refs[1:]:
        total = total + share_ref[...].astype(jnp.float32)
    out_ref[...] = incident_ref[...] - total * norm
    dual_ref[...] = dual_in_ref[...]


def swap(value, axis, step):
    count = lax.axis_size(axis)
    if count & (count - 1) == 0:
        pairs = [(i, i ^ step) for i in range(count)]
    else:
        pairs = [(i, (i + step) % count) for i in range(count)]
    return lax.ppermute(value, axis, pairs)


def order_of(count):
    return (0, 1, 3, 2) if count == 4 else tuple(range(count))


def last_steps(count):
    return (0,) + tuple(range(count - 1, 0, -1))


def exchange(value, axis):
    count = lax.axis_size(axis)
    if count == 1 or count & (count - 1):
        return [value] + [swap(value, axis, step) for step in range(1, count)]
    step = 1
    while step < count:
        radix = min(4, count // step)
        values = [value] + [swap(value, axis, step * k) for k in range(1, radix)]
        step *= radix
        if step < count:
            value = sum(values[k].astype(jnp.float32) for k in order_of(radix)).astype(value.dtype)
    return values


def late(value, after):
    return lax.optimization_barrier((value, after))[0]


def per_device(
    history,
    incident,
    centroids,
    moments,
    dual_moments,
    shell,
    near_mask,
    neighbours,
    gram_diag,
    gram_off,
):
    col_devices = lax.axis_size("col")
    slots, excitations, shard_len = history.shape
    p_tiles, q_tiles = shell.shape
    rows_t = gram_diag.shape[0]
    cols_t = q_tiles * LANES
    norm = 1.0 / math.sqrt(centroids.shape[1])
    shell, near_mask = shell.T, near_mask.T
    gram_diag = gram_diag.reshape(1, rows_t)

    line_rows = -(-(3 * (p_tiles + 1 + q_tiles) + p_tiles * q_tiles) // 8) * 8
    packed, lines = pl.pallas_call(
        pack_kernel,
        out_shape=(
            jax.ShapeDtypeStruct((slots + 1, excitations, shard_len), jnp.bfloat16),
            jax.ShapeDtypeStruct((line_rows, LANES), jnp.float32),
        ),
        in_specs=[VMEM, SMEM, SMEM, VMEM, VMEM, VMEM, VMEM],
        out_specs=(VMEM, VMEM),
        compiler_params=pltpu.CompilerParams(vmem_limit_bytes=56 * MIB),
    )(history, shell, near_mask, gram_diag, gram_off, neighbours, centroids)
    count = lax.axis_size("row")
    everyone = [packed] + [swap(packed, "row", step) for step in range(count - 1, 0, -1)][::-1]
    entries = rows_t * cols_t
    t_tiles = pl.pallas_call(
        functools.partial(t_tiles_kernel, p_tiles=p_tiles, q_tiles=q_tiles),
        out_shape=jax.ShapeDtypeStruct((p_tiles + 2, cols_t, LANES), jnp.bfloat16),
        in_specs=[VMEM],
        out_specs=VMEM,
        scratch_shapes=[pltpu.VMEM((3, cols_t, LANES), jnp.float32)],
        compiler_params=grant((p_tiles + 8, cols_t // 2, LANES), centroids.shape),
        cost_estimate=pl.CostEstimate(flops=16 * entries, bytes_accessed=2 * entries, transcendentals=3 * entries),
    )(lines)

    parts, halo = pl.pallas_call(
        functools.partial(t_kernel, norm=norm, slots=slots, count=count),
        out_shape=(
            jax.ShapeDtypeStruct((excitations, rows_t + LANES), jnp.bfloat16),
            jax.ShapeDtypeStruct((1, excitations, LANES), jnp.float32),
        ),
        in_specs=[VMEM] * (count + 2) + [SMEM],
        out_specs=(VMEM, VMEM),
        scratch_shapes=[
            pltpu.VMEM((slots + 2, moments.shape[0] * excitations, cols_t), jnp.bfloat16),
            pltpu.VMEM((count, 1, excitations, LANES), jnp.float32),
        ],
        compiler_params=grant(
            (p_tiles + 2, cols_t // 2, LANES),
            (excitations, rows_t),
            (slots + 2, moments.shape[0] * excitations, cols_t),
            moments.shape,
        ),
    )(*[everyone[step] for step in order_of(count)], t_tiles, moments, shell)
    parts = exchange(parts, "col")
    s_tiles = pl.pallas_call(
        s_tiles_kernel,
        out_shape=jax.ShapeDtypeStruct((rows_t, cols_t), jnp.bfloat16),
        in_specs=[VMEM],
        out_specs=VMEM,
        scratch_shapes=[pltpu.VMEM((3, LANES, LANES), jnp.float32)],
        compiler_params=grant((rows_t, cols_t // 2), centroids.shape),
        cost_estimate=pl.CostEstimate(flops=12 * entries, bytes_accessed=2 * entries, transcendentals=2 * entries),
    )(late(centroids, parts[0]))

    own_dual, *shares = pl.pallas_call(
        functools.partial(sweep_kernel, slots=slots, part_count=len(parts), count=count),
        out_shape=[jax.ShapeDtypeStruct((excitations, shard_len), jnp.float32)] * 2
        + [jax.ShapeDtypeStruct((excitations, shard_len), jnp.bfloat16)] * (count - 1),
        in_specs=[VMEM] * (len(parts) + 6),
        out_specs=[VMEM] * (count + 1),
        scratch_shapes=[
            pltpu.VMEM((p_tiles, excitations, LANES), jnp.float32),
            pltpu.VMEM((dual_moments.shape[0] * excitations, rows_t), jnp.bfloat16),
            pltpu.VMEM((q_tiles, excitations, LANES), jnp.float32),
        ],
        compiler_params=grant((col_devices, excitations, rows_t), (rows_t, cols_t // 2), (excitations, 8 * rows_t)),
    )(*parts, halo, gram_diag, gram_off, neighbours, s_tiles, dual_moments)
    shares = shares[:1] + [swap(share, "row", step) for step, share in zip(last_steps(count)[1:], shares[1:])]
    march_rhs, own_dual = pl.pallas_call(
        functools.partial(final_kernel, norm=norm),
        out_shape=[jax.ShapeDtypeStruct(incident.shape, jnp.float32)] * 2,
        in_specs=[VMEM] * (count + 2),
        out_specs=[VMEM, VMEM],
        compiler_params=grant((count, excitations, shard_len)),
    )(*shares, own_dual, incident)
    return (march_rhs, own_dual)


def solution(mesh):
    placed = (
        P(None, None, ("col", "row")),
        P(None, ("col", "row")),
        P(),
        P(),
        P(),
        P("row", "col"),
        P("row", "col"),
        P(None, "row"),
        P("row"),
        P(None, "row"),
    )
    return jax.shard_map(
        per_device,
        mesh=mesh,
        in_specs=placed,
        out_specs=(P(None, ("col", "row")), P(None, ("row", "col"))),
        check_vma=False,
    )
```

```python
import functools
import math

import jax
import jax.numpy as jnp
from jax import lax
from jax.experimental import pallas as pl
from jax.experimental.pallas import tpu as pltpu
from jax.sharding import PartitionSpec as P

SWEEPS = 2

SOFT_T = 0.05
SOFT_S = 0.1
NEAR_GAIN = 2.0
NEAR_REACH = 0.5

LANES = 128
HALF = LANES // 2
CHUNK = 64

VMEM = pl.BlockSpec(memory_space=pltpu.VMEM)
SMEM = pl.BlockSpec(memory_space=pltpu.SMEM)
LOG2_E = 1.4426950408889634
TINY = 1e-30
MIB = 1024 * 1024


def grant(*shapes):
    total = 0
    for shape in shapes:
        size = 4
        for extent in shape[:-2] + (-(-shape[-2] // 8) * 8, shape[-1]):
            size *= extent
        total += size
    return pltpu.CompilerParams(vmem_limit_bytes=min(56 * MIB, 2 * total + 2 * MIB))


def root(square):
    square = jnp.maximum(square, TINY)
    return square * lax.rsqrt(square)


def inverse(value):
    return pl.reciprocal(value, approx=True)


def lane_ids(rows=1):
    return lax.broadcasted_iota(jnp.int32, (rows, LANES), 1)


def tile_at(start):
    return pl.ds(pl.multiple_of(start, LANES), LANES)


def edges(ref, row, length):
    first = ref[row : row + 1, :LANES]
    last = ref[row : row + 1, length - LANES :]
    return jnp.where(lane_ids() < HALF, first, last)


def split2(value):
    high = value.astype(jnp.bfloat16).astype(jnp.float32)
    return [high, value - high]


def stack_rows(rows, height):
    row_ids = lax.broadcasted_iota(jnp.int32, (height, LANES), 0)
    out = jnp.zeros((height, LANES), jnp.float32)
    for position, row in enumerate(rows):
        out = jnp.where(row_ids == position, row, out)
    return out


def pack_kernel(history_ref, shell_ref, near_ref, diag_ref, off_ref, links_ref, centroids_ref, out_ref, lines_ref):
    slots, excitations = history_ref.shape[:2]
    length = diag_ref.shape[1]
    tiles = shell_ref.shape[1]
    lanes = lane_ids()
    rows = []
    for tile in (0, tiles - 1):
        code = jnp.zeros((1, LANES), jnp.float32)
        for j in range(shell_ref.shape[0]):
            value = (shell_ref[j, tile] + slots * near_ref[j, tile]).astype(jnp.float32)
            code = jnp.where(lanes == j, value, code)
        rows.append(code)
    here = lax.axis_index("row") * length + jnp.where(lanes < HALF, lanes, length - LANES + lanes)
    for m in range(links_ref.shape[0]):
        rows.append((edges(links_ref, m, length) - here).astype(jnp.float32))
    rows += split2(edges(diag_ref, 0, length))
    for m in range(off_ref.shape[0]):
        rows += split2(edges(off_ref, m, length))
    out_ref[:slots] = history_ref[...]
    out_ref[slots] = stack_rows(rows, excitations).astype(jnp.bfloat16)
    me = lax.axis_index("row")
    row_start = me * length
    q_tiles = shell_ref.shape[0]
    col_start = lax.axis_index("col") * (q_tiles * LANES)
    sources = [source_of(me, i, q_tiles) for i in range(q_tiles)]
    for t in range(tiles):
        for axis in range(3):
            lines_ref[3 * t + axis] = centroids_ref[axis, tile_at(row_start + t * LANES)]
    row = 3 * tiles
    for axis in range(3):
        lines_ref[row + axis : row + axis + 1] = halo_line(centroids_ref, axis, row_start, length)
    row += 3
    for i in range(q_tiles):
        for axis in range(3):
            lines_ref[row + axis] = centroids_ref[axis, tile_at(col_start + sources[i] * LANES)]
        row += 3
    for t in range(tiles):
        for i in range(q_tiles):
            gain = NEAR_GAIN * near_ref[sources[i], t].astype(jnp.float32)
            lines_ref[row : row + 1] = jnp.full((1, LANES), gain, jnp.float32)
            row += 1


def target_of(me, step, count):
    return me ^ step if count & (count - 1) == 0 else lax.rem(me + step, count)


def source_of(me, step, count):
    return me ^ step if count & (count - 1) == 0 else lax.rem(me + count - step, count)


def step_from(me, source, count):
    return me ^ source if count & (count - 1) == 0 else lax.rem(me + count - source, count)


def entries_t(line, column, gains):
    dx, dy, dz = [line[axis] - column[axis] for axis in range(3)]
    spacing = root(dx * dx + dy * dy + dz * dz)
    far, near = inverse(spacing + SOFT_T), jnp.exp2(spacing * (-LOG2_E / NEAR_REACH))
    return [(far + gain * near).astype(jnp.bfloat16) if gain is not None else far.astype(jnp.bfloat16) for gain in gains]


def columns(line):
    return jnp.broadcast_to(line, (LANES, LANES)).T


def halo_line(ref, row, row_start, length):
    total = ref.shape[1]
    right_start = lax.rem(row_start + length, total)
    left_start = lax.rem(row_start + total - LANES, total)
    return jnp.where(
        lane_ids() < HALF, ref[row : row + 1, tile_at(right_start)], ref[row : row + 1, tile_at(left_start)]
    )


def t_tiles_kernel(lines_ref, out_ref, column_ref, p_tiles, q_tiles):
    first_column = 3 * (p_tiles + 1)
    first_gain = first_column + 3 * q_tiles
    for i in range(q_tiles):
        for axis in range(3):
            row = first_column + 3 * i + axis
            column_ref[axis, i * LANES : (i + 1) * LANES, :] = columns(lines_ref[row : row + 1])

    def fill(first, gains_of):
        line = [lines_ref[pl.ds(3 * first + axis, 1)] for axis in range(3)]
        for i in range(q_tiles):
            gains = gains_of(i)
            for k in range(LANES // CHUNK):
                at = slice(i * LANES + k * CHUNK, i * LANES + (k + 1) * CHUNK)
                for offset, tile in enumerate(entries_t(line, [column_ref[axis, at, :] for axis in range(3)], gains)):
                    out_ref[first + offset, at, :] = tile

    group = max(1, 16 // q_tiles)
    while p_tiles % group:
        group -= 1

    def one_group(g, carry):
        for k in range(group):
            t = g * group + k
            fill(t, lambda i: [lines_ref[pl.ds(first_gain + t * q_tiles + i, 1)]])
        return carry

    lax.fori_loop(0, p_tiles // group, one_group, 0)
    fill(p_tiles, lambda i: [None, NEAR_GAIN])


def t_kernel(*refs, norm, slots, count):
    packed = [refs[order_of(count).index(step)] for step in range(count)]
    tiles_ref, moments_ref, shell_in = refs[count : count + 3]
    out_ref, halo_ref, scaled_ref, edge_ref, shell_ref, sem = refs[count + 3 :]
    shell_copy = pltpu.make_async_copy(shell_in, shell_ref, sem)
    shell_copy.start()
    q_tiles, p_tiles = shell_ref.shape
    excitations = out_ref.shape[0]
    kinds = moments_ref.shape[0]
    me = lax.axis_index("row")
    length = p_tiles * LANES
    row_start = me * length
    col_start = lax.axis_index("col") * (q_tiles * LANES)
    low = lane_ids() < HALF

    for i in range(count):
        edge_ref[i] = packed[i][slots:].astype(jnp.float32)
    right = edge_ref[step_from(me, lax.rem(me + 1, count), count)]
    left = edge_ref[step_from(me, lax.rem(me + count - 1, count), count)]
    halo_ref[...] = jnp.where(low[None], right, left)
    codes = right[0, 0:1], left[0, 1:2]
    nears = [jnp.where(code >= slots, 1.0, 0.0) for code in codes]
    picks = [code - slots * near for code, near in zip(codes, nears)]

    sources = [source_of(me, i, count) for i in range(count)]
    lanes = lane_ids()
    halo_tiles = []
    for i in range(count):
        at = slice(i * LANES, (i + 1) * LANES)
        weights = [moments_ref[a : a + 1, tile_at(col_start + sources[i] * LANES)] for a in range(kinds)]
        values = [packed[i][s].astype(jnp.float32) for s in range(slots)]
        here = lanes == sources[i]
        for pick in picks:
            choice = jnp.sum(jnp.where(here, pick, 0.0), axis=1, keepdims=True)
            value = values[0]
            for s in range(1, slots):
                value = jnp.where(choice == s, values[s], value)
            values.append(value)
        for s, value in enumerate(values):
            for a in range(kinds):
                scaled_ref[s, a * excitations : (a + 1) * excitations, at] = (weights[a] * value).astype(jnp.bfloat16)
        near_right, near_left = [jnp.sum(jnp.where(here, near, 0.0), axis=1, keepdims=True) for near in nears]
        near = jnp.where(low, near_right, near_left)
        halo_tiles.append(
            jnp.where(near > 0.5, tiles_ref[p_tiles + 1, at].astype(jnp.float32), tiles_ref[p_tiles, at].astype(jnp.float32))
            .astype(jnp.bfloat16)
        )

    def weighted(product, weights):
        field = weights[0] * product[:excitations]
        for a in range(1, kinds):
            term = weights[a] * product[a * excitations : (a + 1) * excitations]
            field = field + term if a < kinds - 1 else field - term
        return (field * norm).astype(jnp.bfloat16)

    halo_tile = jnp.concatenate(halo_tiles, axis=0)
    product = jnp.where(
        low,
        jnp.dot(scaled_ref[slots], halo_tile, preferred_element_type=jnp.float32),
        jnp.dot(scaled_ref[slots + 1], halo_tile, preferred_element_type=jnp.float32),
    )
    out_ref[:, length:] = weighted(product, [halo_line(moments_ref, a, row_start, length) for a in range(kinds)])

    def one_tile(t):
        lhs = jnp.concatenate(
            [scaled_ref[shell_ref[sources[i], t], :, i * LANES : (i + 1) * LANES] for i in range(count)], axis=1
        )
        weights = [moments_ref[a : a + 1, tile_at(row_start + t * LANES)] for a in range(kinds)]
        product = jnp.dot(lhs, tiles_ref[t], preferred_element_type=jnp.float32)
        out_ref[:, tile_at(t * LANES)] = weighted(product, weights)

    group = max(1, 32 // q_tiles)
    while p_tiles % group:
        group -= 1

    def one_group(g, carry):
        for k in range(group):
            one_tile(g * group + k)
        return carry

    shell_copy.wait()
    if group == p_tiles:
        one_group(0, 0)
    else:
        lax.fori_loop(0, p_tiles // group, one_group, 0)

def s_tiles_kernel(centroids_ref, out_ref, column_ref):
    length, width = out_ref.shape
    row_start = lax.axis_index("row") * length
    col_start = lax.axis_index("col") * width

    def one_tile(t, carry):
        for axis in range(3):
            column_ref[axis] = columns(centroids_ref[axis : axis + 1, tile_at(row_start + t * LANES)])
        for k in range(width // LANES):
            line = [centroids_ref[axis : axis + 1, tile_at(col_start + k * LANES)] for axis in range(3)]
            for piece in range(LANES // CHUNK):
                at = slice(piece * CHUNK, (piece + 1) * CHUNK)
                dx = line[0] - column_ref[0, at, :]
                dy = line[1] - column_ref[1, at, :]
                dz = line[2] - column_ref[2, at, :]
                spacing = root(dx * dx + dy * dy + dz * dz)
                rows = pl.ds(pl.multiple_of(t * LANES + piece * CHUNK, CHUNK), CHUNK)
                out_ref[rows, k * LANES : (k + 1) * LANES] = inverse(spacing + SOFT_S).astype(jnp.bfloat16)
        return carry

    lax.fori_loop(0, length // LANES, one_tile, 0)


def sweep_kernel(*refs, slots, part_count, count):
    parts = refs[:part_count]
    halo_ref, diag_ref, off_ref, links_ref, tiles_ref, dual_moments_ref = refs[part_count : part_count + 6]
    dual_ref, *out_refs = refs[part_count + 6 : -3]
    iter_ref, scaled_ref, share_ref = refs[-3:]
    length = diag_ref.shape[1]
    tiles = length // LANES
    excitations = parts[0].shape[0]
    link_count = links_ref.shape[0]
    kinds = dual_moments_ref.shape[0]
    row_start = lax.axis_index("row") * length
    col_start = lax.axis_index("col") * tiles_ref.shape[1]
    lanes = lane_ids()
    low = lanes < HALF

    def halo(row):
        return halo_ref[0, row : row + 1]

    def sum2(row):
        return halo(row) + halo(row + 1)

    def tile(t):
        return slice(t * LANES, (t + 1) * LANES)

    field, diag = [], []
    for t in range(tiles + 1):
        total = parts[0][:, tile(t)].astype(jnp.float32)
        for part in parts[1:]:
            total = total + part[:, tile(t)].astype(jnp.float32)
        field.append(total)
        diag.append(diag_ref[:, tile(t)] if t < tiles else sum2(2 + link_count))

    dual = [f / d for f, d in zip(field, diag)]
    for sweep_id in range(SWEEPS):
        last = sweep_id == SWEEPS - 1
        updated = []
        for t in range(tiles if last else tiles + 1):
            around = jnp.where(low, dual[(t + 1) % (tiles + 1)], dual[t - 1])
            coupled = jnp.zeros_like(field[t])
            for m in range(link_count):
                if t < tiles:
                    source = links_ref[m : m + 1, tile(t)] - (row_start + t * LANES)
                    gram = off_ref[m : m + 1, tile(t)]
                else:
                    source = halo(2 + m).astype(jnp.int32) + lanes
                    gram = sum2(4 + link_count + 2 * m)
                inside = (source >= 0) & (source < LANES)
                index = jnp.broadcast_to(source & (LANES - 1), (excitations, LANES))
                here = jnp.take_along_axis(dual[t], index, axis=1)
                beside = jnp.take_along_axis(around, index, axis=1)
                coupled = coupled + gram * jnp.where(inside, here, beside)
            updated.append((field[t] - coupled) / diag[t])
        dual = updated

    for t in range(tiles):
        iter_ref[t] = dual[t]
        for a in range(kinds):
            weight = dual_moments_ref[a : a + 1, tile_at(row_start + t * LANES)]
            scaled_ref[a * excitations : (a + 1) * excitations, tile(t)] = (weight * dual[t]).astype(jnp.bfloat16)
    dual_ref[...] = iter_ref[lax.axis_index("col")]
    product = jnp.dot(scaled_ref[...], tiles_ref[...], preferred_element_type=jnp.float32)
    for k in range(count):
        term = jnp.zeros((excitations, LANES), jnp.float32)
        for a in range(kinds):
            weight = dual_moments_ref[a : a + 1, tile_at(col_start + k * LANES)]
            term = term + weight * product[a * excitations : (a + 1) * excitations, tile(k)]
        share_ref[k] = term
    me = lax.axis_index("row")
    for step, out_ref in zip(last_steps(count), out_refs):
        out_ref[...] = share_ref[target_of(me, step, count)].astype(out_ref.dtype)


def final_kernel(*refs, norm):
    *share_refs, dual_in_ref, incident_ref, out_ref, dual_ref = refs
    total = share_refs[0][...].astype(jnp.float32)
    for share_ref in share_refs[1:]:
        total = total + share_ref[...].astype(jnp.float32)
    out_ref[...] = incident_ref[...] - total * norm
    dual_ref[...] = dual_in_ref[...]


def swap(value, axis, step):
    count = lax.axis_size(axis)
    if count & (count - 1) == 0:
        pairs = [(i, i ^ step) for i in range(count)]
    else:
        pairs = [(i, (i + step) % count) for i in range(count)]
    return lax.ppermute(value, axis, pairs)


def order_of(count):
    return (0, 1, 3, 2) if count == 4 else tuple(range(count))


def last_steps(count):
    return (0,) + tuple(range(count - 1, 0, -1))


def exchange(value, axis):
    count = lax.axis_size(axis)
    if count == 1 or count & (count - 1):
        return [value] + [swap(value, axis, step) for step in range(1, count)]
    step = 1
    while step < count:
        radix = min(4, count // step)
        values = [value] + [swap(value, axis, step * k) for k in range(1, radix)]
        step *= radix
        if step < count:
            value = sum(values[k].astype(jnp.float32) for k in order_of(radix)).astype(value.dtype)
    return values


def late(value, after):
    return lax.optimization_barrier((value, after))[0]


def per_device(
    history,
    incident,
    centroids,
    moments,
    dual_moments,
    shell,
    near_mask,
    neighbours,
    gram_diag,
    gram_off,
):
    col_devices = lax.axis_size("col")
    slots, excitations, shard_len = history.shape
    p_tiles, q_tiles = shell.shape
    rows_t = gram_diag.shape[0]
    cols_t = q_tiles * LANES
    norm = 1.0 / math.sqrt(centroids.shape[1])
    shell, near_mask = shell.T, near_mask.T
    gram_diag = gram_diag.reshape(1, rows_t)

    line_rows = -(-(3 * (p_tiles + 1 + q_tiles) + p_tiles * q_tiles) // 8) * 8
    packed, lines = pl.pallas_call(
        pack_kernel,
        out_shape=(
            jax.ShapeDtypeStruct((slots + 1, excitations, shard_len), jnp.bfloat16),
            jax.ShapeDtypeStruct((line_rows, LANES), jnp.float32),
        ),
        in_specs=[VMEM, SMEM, SMEM, VMEM, VMEM, VMEM, VMEM],
        out_specs=(VMEM, VMEM),
        compiler_params=pltpu.CompilerParams(vmem_limit_bytes=56 * MIB),
    )(history, shell, near_mask, gram_diag, gram_off, neighbours, centroids)
    count = lax.axis_size("row")
    everyone = [packed] + [swap(packed, "row", step) for step in range(count - 1, 0, -1)][::-1]
    entries = rows_t * cols_t
    t_tiles = pl.pallas_call(
        functools.partial(t_tiles_kernel, p_tiles=p_tiles, q_tiles=q_tiles),
        out_shape=jax.ShapeDtypeStruct((p_tiles + 2, cols_t, LANES), jnp.bfloat16),
        in_specs=[VMEM],
        out_specs=VMEM,
        scratch_shapes=[pltpu.VMEM((3, cols_t, LANES), jnp.float32)],
        compiler_params=grant((p_tiles + 8, cols_t // 2, LANES), centroids.shape),
        cost_estimate=pl.CostEstimate(flops=16 * entries, bytes_accessed=2 * entries, transcendentals=3 * entries),
    )(lines)

    parts, halo = pl.pallas_call(
        functools.partial(t_kernel, norm=norm, slots=slots, count=count),
        out_shape=(
            jax.ShapeDtypeStruct((excitations, rows_t + LANES), jnp.bfloat16),
            jax.ShapeDtypeStruct((1, excitations, LANES), jnp.float32),
        ),
        in_specs=[VMEM] * (count + 2) + [pl.BlockSpec(memory_space=pl.ANY)],
        out_specs=(VMEM, VMEM),
        scratch_shapes=[
            pltpu.VMEM((slots + 2, moments.shape[0] * excitations, cols_t), jnp.bfloat16),
            pltpu.VMEM((count, 1, excitations, LANES), jnp.float32),
            pltpu.SMEM(shell.shape, jnp.int32),
            pltpu.SemaphoreType.DMA,
        ],
        compiler_params=grant(
            (p_tiles + 2, cols_t // 2, LANES),
            (excitations, rows_t),
            (slots + 2, moments.shape[0] * excitations, cols_t),
            moments.shape,
        ),
    )(*[everyone[step] for step in order_of(count)], t_tiles, moments, shell)
    parts = exchange(parts, "col")
    s_tiles = pl.pallas_call(
        s_tiles_kernel,
        out_shape=jax.ShapeDtypeStruct((rows_t, cols_t), jnp.bfloat16),
        in_specs=[VMEM],
        out_specs=VMEM,
        scratch_shapes=[pltpu.VMEM((3, LANES, LANES), jnp.float32)],
        compiler_params=grant((rows_t, cols_t // 2), centroids.shape),
        cost_estimate=pl.CostEstimate(flops=12 * entries, bytes_accessed=2 * entries, transcendentals=2 * entries),
    )(late(centroids, parts[0]))

    own_dual, *shares = pl.pallas_call(
        functools.partial(sweep_kernel, slots=slots, part_count=len(parts), count=count),
        out_shape=[jax.ShapeDtypeStruct((excitations, shard_len), jnp.float32)] * 2
        + [jax.ShapeDtypeStruct((excitations, shard_len), jnp.bfloat16)] * (count - 1),
        in_specs=[VMEM] * (len(parts) + 6),
        out_specs=[VMEM] * (count + 1),
        scratch_shapes=[
            pltpu.VMEM((p_tiles, excitations, LANES), jnp.float32),
            pltpu.VMEM((dual_moments.shape[0] * excitations, rows_t), jnp.bfloat16),
            pltpu.VMEM((q_tiles, excitations, LANES), jnp.float32),
        ],
        compiler_params=grant((col_devices, excitations, rows_t), (rows_t, cols_t // 2), (excitations, 8 * rows_t)),
    )(*parts, halo, gram_diag, gram_off, neighbours, s_tiles, dual_moments)
    shares = shares[:1] + [swap(share, "row", step) for step, share in zip(last_steps(count)[1:], shares[1:])]
    march_rhs, own_dual = pl.pallas_call(
        functools.partial(final_kernel, norm=norm),
        out_shape=[jax.ShapeDtypeStruct(incident.shape, jnp.float32)] * 2,
        in_specs=[VMEM] * (count + 2),
        out_specs=[VMEM, VMEM],
        compiler_params=grant((count, excitations, shard_len)),
    )(*shares, own_dual, incident)
    return (march_rhs, own_dual)


def solution(mesh):
    placed = (
        P(None, None, ("col", "row")),
        P(None, ("col", "row")),
        P(),
        P(),
        P(),
        P("row", "col"),
        P("row", "col"),
        P(None, "row"),
        P("row"),
        P(None, "row"),
    )
    return jax.shard_map(
        per_device,
        mesh=mesh,
        in_specs=placed,
        out_specs=(P(None, ("col", "row")), P(None, ("row", "col"))),
        check_vma=False,
    )
```

```python
import functools
import math

import jax
import jax.numpy as jnp
from jax import lax
from jax.experimental import pallas as pl
from jax.experimental.pallas import tpu as pltpu
from jax.sharding import PartitionSpec as P

SWEEPS = 2

SOFT_T = 0.05
SOFT_S = 0.1
NEAR_GAIN = 2.0
NEAR_REACH = 0.5

LANES = 128
HALF = LANES // 2
CHUNK = 64

VMEM = pl.BlockSpec(memory_space=pltpu.VMEM)
SMEM = pl.BlockSpec(memory_space=pltpu.SMEM)
LOG2_E = 1.4426950408889634
TINY = 1e-30
MIB = 1024 * 1024


def grant(*shapes):
    total = 0
    for shape in shapes:
        size = 4
        for extent in shape[:-2] + (-(-shape[-2] // 8) * 8, shape[-1]):
            size *= extent
        total += size
    return pltpu.CompilerParams(vmem_limit_bytes=min(56 * MIB, 2 * total + 2 * MIB))


def root(square):
    square = jnp.maximum(square, TINY)
    return square * lax.rsqrt(square)


def inverse(value):
    return pl.reciprocal(value, approx=True)


def lane_ids(rows=1):
    return lax.broadcasted_iota(jnp.int32, (rows, LANES), 1)


def tile_at(start):
    return pl.ds(pl.multiple_of(start, LANES), LANES)


def edges(ref, row, length):
    first = ref[row : row + 1, :LANES]
    last = ref[row : row + 1, length - LANES :]
    return jnp.where(lane_ids() < HALF, first, last)


def split2(value):
    high = value.astype(jnp.bfloat16).astype(jnp.float32)
    return [high, value - high]


def stack_rows(rows, height):
    row_ids = lax.broadcasted_iota(jnp.int32, (height, LANES), 0)
    out = jnp.zeros((height, LANES), jnp.float32)
    for position, row in enumerate(rows):
        out = jnp.where(row_ids == position, row, out)
    return out


def pack_kernel(history_ref, shell_ref, near_ref, diag_ref, off_ref, links_ref, centroids_ref, out_ref, lines_ref):
    slots, excitations = history_ref.shape[:2]
    length = diag_ref.shape[1]
    tiles = shell_ref.shape[1]
    lanes = lane_ids()
    rows = []
    for tile in (0, tiles - 1):
        code = jnp.zeros((1, LANES), jnp.float32)
        for j in range(shell_ref.shape[0]):
            value = (shell_ref[j, tile] + slots * near_ref[j, tile]).astype(jnp.float32)
            code = jnp.where(lanes == j, value, code)
        rows.append(code)
    here = lax.axis_index("row") * length + jnp.where(lanes < HALF, lanes, length - LANES + lanes)
    for m in range(links_ref.shape[0]):
        rows.append((edges(links_ref, m, length) - here).astype(jnp.float32))
    rows += split2(edges(diag_ref, 0, length))
    for m in range(off_ref.shape[0]):
        rows += split2(edges(off_ref, m, length))
    out_ref[:slots] = history_ref[...]
    out_ref[slots] = stack_rows(rows, excitations).astype(jnp.bfloat16)
    me = lax.axis_index("row")
    row_start = me * length
    q_tiles = shell_ref.shape[0]
    col_start = lax.axis_index("col") * (q_tiles * LANES)
    sources = [source_of(me, i, q_tiles) for i in range(q_tiles)]
    for t in range(tiles):
        for axis in range(3):
            lines_ref[3 * t + axis] = centroids_ref[axis, tile_at(row_start + t * LANES)]
    row = 3 * tiles
    for axis in range(3):
        lines_ref[row + axis : row + axis + 1] = halo_line(centroids_ref, axis, row_start, length)
    row += 3
    for i in range(q_tiles):
        for axis in range(3):
            lines_ref[row + axis] = centroids_ref[axis, tile_at(col_start + sources[i] * LANES)]
        row += 3
    for t in range(tiles):
        for i in range(q_tiles):
            gain = NEAR_GAIN * near_ref[sources[i], t].astype(jnp.float32)
            lines_ref[row : row + 1] = jnp.full((1, LANES), gain, jnp.float32)
            row += 1


def target_of(me, step, count):
    return me ^ step if count & (count - 1) == 0 else lax.rem(me + step, count)


def source_of(me, step, count):
    return me ^ step if count & (count - 1) == 0 else lax.rem(me + count - step, count)


def step_from(me, source, count):
    return me ^ source if count & (count - 1) == 0 else lax.rem(me + count - source, count)


def entries_t(line, column, gains):
    dx, dy, dz = [line[axis] - column[axis] for axis in range(3)]
    spacing = root(dx * dx + dy * dy + dz * dz)
    far, near = inverse(spacing + SOFT_T), jnp.exp2(spacing * (-LOG2_E / NEAR_REACH))
    return [(far + gain * near).astype(jnp.bfloat16) if gain is not None else far.astype(jnp.bfloat16) for gain in gains]


def columns(line):
    return jnp.broadcast_to(line, (LANES, LANES)).T


def halo_line(ref, row, row_start, length):
    total = ref.shape[1]
    right_start = lax.rem(row_start + length, total)
    left_start = lax.rem(row_start + total - LANES, total)
    return jnp.where(
        lane_ids() < HALF, ref[row : row + 1, tile_at(right_start)], ref[row : row + 1, tile_at(left_start)]
    )


def t_tiles_kernel(lines_ref, out_ref, column_ref, p_tiles, q_tiles):
    first_column = 3 * (p_tiles + 1)
    first_gain = first_column + 3 * q_tiles
    for i in range(q_tiles):
        for axis in range(3):
            row = first_column + 3 * i + axis
            column_ref[axis, i * LANES : (i + 1) * LANES, :] = columns(lines_ref[row : row + 1])

    def fill(first, gains_of):
        line = [lines_ref[pl.ds(3 * first + axis, 1)] for axis in range(3)]
        for i in range(q_tiles):
            gains = gains_of(i)
            for k in range(LANES // CHUNK):
                at = slice(i * LANES + k * CHUNK, i * LANES + (k + 1) * CHUNK)
                for offset, tile in enumerate(entries_t(line, [column_ref[axis, at, :] for axis in range(3)], gains)):
                    out_ref[first + offset, at, :] = tile

    group = max(1, 16 // q_tiles)
    while p_tiles % group:
        group -= 1

    def one_group(g, carry):
        for k in range(group):
            t = g * group + k
            fill(t, lambda i: [lines_ref[pl.ds(first_gain + t * q_tiles + i, 1)]])
        return carry

    lax.fori_loop(0, p_tiles // group, one_group, 0)
    fill(p_tiles, lambda i: [None, NEAR_GAIN])


def t_kernel(*refs, norm, slots, count):
    packed = [refs[order_of(count).index(step)] for step in range(count)]
    tiles_ref, moments_ref, shell_in = refs[count : count + 3]
    out_ref, halo_ref, scaled_ref, edge_ref, shell_ref, sem = refs[count + 3 :]
    shell_copy = pltpu.make_async_copy(shell_in, shell_ref, sem)
    shell_copy.start()
    q_tiles, p_tiles = shell_ref.shape
    excitations = out_ref.shape[0]
    kinds = moments_ref.shape[0]
    me = lax.axis_index("row")
    length = p_tiles * LANES
    row_start = me * length
    col_start = lax.axis_index("col") * (q_tiles * LANES)
    low = lane_ids() < HALF

    for i in range(count):
        edge_ref[i] = packed[i][slots:].astype(jnp.float32)
    right = edge_ref[step_from(me, lax.rem(me + 1, count), count)]
    left = edge_ref[step_from(me, lax.rem(me + count - 1, count), count)]
    halo_ref[...] = jnp.where(low[None], right, left)
    codes = right[0, 0:1], left[0, 1:2]
    nears = [jnp.where(code >= slots, 1.0, 0.0) for code in codes]
    picks = [code - slots * near for code, near in zip(codes, nears)]

    sources = [source_of(me, i, count) for i in range(count)]
    lanes = lane_ids()
    choices, halo_tiles = [], []
    for i in range(count):
        at = slice(i * LANES, (i + 1) * LANES)
        weights = [moments_ref[a : a + 1, tile_at(col_start + sources[i] * LANES)] for a in range(kinds)]
        for s in range(slots):
            value = packed[i][s].astype(jnp.float32)
            for a in range(kinds):
                scaled_ref[s, a * excitations : (a + 1) * excitations, at] = (weights[a] * value).astype(jnp.bfloat16)
        here = lanes == sources[i]
        choices.append([jnp.sum(jnp.where(here, pick, 0.0), axis=1, keepdims=True) for pick in picks])
        near_right, near_left = [jnp.sum(jnp.where(here, near, 0.0), axis=1, keepdims=True) for near in nears]
        near = jnp.where(low, near_right, near_left)
        halo_tiles.append(
            jnp.where(near > 0.5, tiles_ref[p_tiles + 1, at].astype(jnp.float32), tiles_ref[p_tiles, at].astype(jnp.float32))
            .astype(jnp.bfloat16)
        )

    def weighted(product, weights):
        field = weights[0] * product[:excitations]
        for a in range(1, kinds):
            term = weights[a] * product[a * excitations : (a + 1) * excitations]
            field = field + term if a < kinds - 1 else field - term
        return (field * norm).astype(jnp.bfloat16)

    def one_tile(t):
        lhs = jnp.concatenate(
            [scaled_ref[shell_ref[sources[i], t], :, i * LANES : (i + 1) * LANES] for i in range(count)], axis=1
        )
        weights = [moments_ref[a : a + 1, tile_at(row_start + t * LANES)] for a in range(kinds)]
        product = jnp.dot(lhs, tiles_ref[t], preferred_element_type=jnp.float32)
        out_ref[:, tile_at(t * LANES)] = weighted(product, weights)

    group = max(1, 32 // q_tiles)
    while p_tiles % group:
        group -= 1

    def one_group(g, carry):
        for k in range(group):
            one_tile(g * group + k)
        return carry

    shell_copy.wait()
    if group == p_tiles:
        one_group(0, 0)
    else:
        lax.fori_loop(0, p_tiles // group, one_group, 0)
    for side in range(2):
        for i in range(count):
            choice = choices[i][side]
            for a in range(kinds):
                rows = slice(a * excitations, (a + 1) * excitations)
                at = slice(i * LANES, (i + 1) * LANES)
                value = scaled_ref[0, rows, at].astype(jnp.float32)
                for s in range(1, slots):
                    value = jnp.where(choice == s, scaled_ref[s, rows, at].astype(jnp.float32), value)
                scaled_ref[slots + side, rows, at] = value.astype(jnp.bfloat16)
    halo_tile = jnp.concatenate(halo_tiles, axis=0)
    product = jnp.where(
        low,
        jnp.dot(scaled_ref[slots], halo_tile, preferred_element_type=jnp.float32),
        jnp.dot(scaled_ref[slots + 1], halo_tile, preferred_element_type=jnp.float32),
    )
    out_ref[:, length:] = weighted(product, [halo_line(moments_ref, a, row_start, length) for a in range(kinds)])


def s_tiles_kernel(centroids_ref, out_ref, column_ref):
    length, width = out_ref.shape
    row_start = lax.axis_index("row") * length
    col_start = lax.axis_index("col") * width

    def one_tile(t, carry):
        for axis in range(3):
            column_ref[axis] = columns(centroids_ref[axis : axis + 1, tile_at(row_start + t * LANES)])
        for k in range(width // LANES):
            line = [centroids_ref[axis : axis + 1, tile_at(col_start + k * LANES)] for axis in range(3)]
            for piece in range(LANES // CHUNK):
                at = slice(piece * CHUNK, (piece + 1) * CHUNK)
                dx = line[0] - column_ref[0, at, :]
                dy = line[1] - column_ref[1, at, :]
                dz = line[2] - column_ref[2, at, :]
                spacing = root(dx * dx + dy * dy + dz * dz)
                rows = pl.ds(pl.multiple_of(t * LANES + piece * CHUNK, CHUNK), CHUNK)
                out_ref[rows, k * LANES : (k + 1) * LANES] = inverse(spacing + SOFT_S).astype(jnp.bfloat16)
        return carry

    lax.fori_loop(0, length // LANES, one_tile, 0)


def sweep_kernel(*refs, slots, part_count, count):
    parts = refs[:part_count]
    halo_ref, diag_ref, off_ref, links_ref, tiles_ref, dual_moments_ref = refs[part_count : part_count + 6]
    dual_ref, *out_refs = refs[part_count + 6 : -3]
    iter_ref, scaled_ref, share_ref = refs[-3:]
    length = diag_ref.shape[1]
    tiles = length // LANES
    excitations = parts[0].shape[0]
    link_count = links_ref.shape[0]
    kinds = dual_moments_ref.shape[0]
    row_start = lax.axis_index("row") * length
    col_start = lax.axis_index("col") * tiles_ref.shape[1]
    lanes = lane_ids()
    low = lanes < HALF

    def halo(row):
        return halo_ref[0, row : row + 1]

    def sum2(row):
        return halo(row) + halo(row + 1)

    def tile(t):
        return slice(t * LANES, (t + 1) * LANES)

    field, diag = [], []
    for t in range(tiles + 1):
        total = parts[0][:, tile(t)].astype(jnp.float32)
        for part in parts[1:]:
            total = total + part[:, tile(t)].astype(jnp.float32)
        field.append(total)
        diag.append(diag_ref[:, tile(t)] if t < tiles else sum2(2 + link_count))

    dual = [f / d for f, d in zip(field, diag)]
    for sweep_id in range(SWEEPS):
        last = sweep_id == SWEEPS - 1
        updated = []
        for t in range(tiles if last else tiles + 1):
            around = jnp.where(low, dual[(t + 1) % (tiles + 1)], dual[t - 1])
            coupled = jnp.zeros_like(field[t])
            for m in range(link_count):
                if t < tiles:
                    source = links_ref[m : m + 1, tile(t)] - (row_start + t * LANES)
                    gram = off_ref[m : m + 1, tile(t)]
                else:
                    source = halo(2 + m).astype(jnp.int32) + lanes
                    gram = sum2(4 + link_count + 2 * m)
                inside = (source >= 0) & (source < LANES)
                index = jnp.broadcast_to(source & (LANES - 1), (excitations, LANES))
                here = jnp.take_along_axis(dual[t], index, axis=1)
                beside = jnp.take_along_axis(around, index, axis=1)
                coupled = coupled + gram * jnp.where(inside, here, beside)
            updated.append((field[t] - coupled) / diag[t])
        dual = updated

    for t in range(tiles):
        iter_ref[t] = dual[t]
        for a in range(kinds):
            weight = dual_moments_ref[a : a + 1, tile_at(row_start + t * LANES)]
            scaled_ref[a * excitations : (a + 1) * excitations, tile(t)] = (weight * dual[t]).astype(jnp.bfloat16)
    dual_ref[...] = iter_ref[lax.axis_index("col")]
    product = jnp.dot(scaled_ref[...], tiles_ref[...], preferred_element_type=jnp.float32)
    for k in range(count):
        term = jnp.zeros((excitations, LANES), jnp.float32)
        for a in range(kinds):
            weight = dual_moments_ref[a : a + 1, tile_at(col_start + k * LANES)]
            term = term + weight * product[a * excitations : (a + 1) * excitations, tile(k)]
        share_ref[k] = term
    me = lax.axis_index("row")
    for step, out_ref in zip(last_steps(count), out_refs):
        out_ref[...] = share_ref[target_of(me, step, count)].astype(out_ref.dtype)


def final_kernel(*refs, norm):
    *share_refs, dual_in_ref, incident_ref, out_ref, dual_ref = refs
    total = share_refs[0][...].astype(jnp.float32)
    for share_ref in share_refs[1:]:
        total = total + share_ref[...].astype(jnp.float32)
    out_ref[...] = incident_ref[...] - total * norm
    dual_ref[...] = dual_in_ref[...]


def swap(value, axis, step):
    count = lax.axis_size(axis)
    if count & (count - 1) == 0:
        pairs = [(i, i ^ step) for i in range(count)]
    else:
        pairs = [(i, (i + step) % count) for i in range(count)]
    return lax.ppermute(value, axis, pairs)


def order_of(count):
    return (0, 1, 3, 2) if count == 4 else tuple(range(count))


def last_steps(count):
    return (0,) + tuple(range(count - 1, 0, -1))


def exchange(value, axis):
    count = lax.axis_size(axis)
    if count == 1 or count & (count - 1):
        return [value] + [swap(value, axis, step) for step in range(1, count)]
    step = 1
    while step < count:
        radix = min(4, count // step)
        values = [value] + [swap(value, axis, step * k) for k in range(1, radix)]
        step *= radix
        if step < count:
            value = sum(values[k].astype(jnp.float32) for k in order_of(radix)).astype(value.dtype)
    return values


def late(value, after):
    return lax.optimization_barrier((value, after))[0]


def per_device(
    history,
    incident,
    centroids,
    moments,
    dual_moments,
    shell,
    near_mask,
    neighbours,
    gram_diag,
    gram_off,
):
    col_devices = lax.axis_size("col")
    slots, excitations, shard_len = history.shape
    p_tiles, q_tiles = shell.shape
    rows_t = gram_diag.shape[0]
    cols_t = q_tiles * LANES
    norm = 1.0 / math.sqrt(centroids.shape[1])
    shell, near_mask = shell.T, near_mask.T
    gram_diag = gram_diag.reshape(1, rows_t)

    line_rows = -(-(3 * (p_tiles + 1 + q_tiles) + p_tiles * q_tiles) // 8) * 8
    packed, lines = pl.pallas_call(
        pack_kernel,
        out_shape=(
            jax.ShapeDtypeStruct((slots + 1, excitations, shard_len), jnp.bfloat16),
            jax.ShapeDtypeStruct((line_rows, LANES), jnp.float32),
        ),
        in_specs=[VMEM, SMEM, SMEM, VMEM, VMEM, VMEM, VMEM],
        out_specs=(VMEM, VMEM),
        compiler_params=pltpu.CompilerParams(vmem_limit_bytes=56 * MIB),
    )(history, shell, near_mask, gram_diag, gram_off, neighbours, centroids)
    count = lax.axis_size("row")
    everyone = [packed] + [swap(packed, "row", step) for step in range(count - 1, 0, -1)][::-1]
    entries = rows_t * cols_t
    t_tiles = pl.pallas_call(
        functools.partial(t_tiles_kernel, p_tiles=p_tiles, q_tiles=q_tiles),
        out_shape=jax.ShapeDtypeStruct((p_tiles + 2, cols_t, LANES), jnp.bfloat16),
        in_specs=[VMEM],
        out_specs=VMEM,
        scratch_shapes=[pltpu.VMEM((3, cols_t, LANES), jnp.float32)],
        compiler_params=grant((p_tiles + 8, cols_t // 2, LANES), centroids.shape),
        cost_estimate=pl.CostEstimate(flops=16 * entries, bytes_accessed=2 * entries, transcendentals=3 * entries),
    )(lines)

    parts, halo = pl.pallas_call(
        functools.partial(t_kernel, norm=norm, slots=slots, count=count),
        out_shape=(
            jax.ShapeDtypeStruct((excitations, rows_t + LANES), jnp.bfloat16),
            jax.ShapeDtypeStruct((1, excitations, LANES), jnp.float32),
        ),
        in_specs=[VMEM] * (count + 2) + [pl.BlockSpec(memory_space=pl.ANY)],
        out_specs=(VMEM, VMEM),
        scratch_shapes=[
            pltpu.VMEM((slots + 2, moments.shape[0] * excitations, cols_t), jnp.bfloat16),
            pltpu.VMEM((count, 1, excitations, LANES), jnp.float32),
            pltpu.SMEM(shell.shape, jnp.int32),
            pltpu.SemaphoreType.DMA,
        ],
        compiler_params=grant(
            (p_tiles + 2, cols_t // 2, LANES),
            (excitations, rows_t),
            (slots + 2, moments.shape[0] * excitations, cols_t),
            moments.shape,
        ),
    )(*[everyone[step] for step in order_of(count)], t_tiles, moments, shell)
    parts = exchange(parts, "col")
    s_tiles = pl.pallas_call(
        s_tiles_kernel,
        out_shape=jax.ShapeDtypeStruct((rows_t, cols_t), jnp.bfloat16),
        in_specs=[VMEM],
        out_specs=VMEM,
        scratch_shapes=[pltpu.VMEM((3, LANES, LANES), jnp.float32)],
        compiler_params=grant((rows_t, cols_t // 2), centroids.shape),
        cost_estimate=pl.CostEstimate(flops=12 * entries, bytes_accessed=2 * entries, transcendentals=2 * entries),
    )(late(centroids, parts[0]))

    own_dual, *shares = pl.pallas_call(
        functools.partial(sweep_kernel, slots=slots, part_count=len(parts), count=count),
        out_shape=[jax.ShapeDtypeStruct((excitations, shard_len), jnp.float32)] * 2
        + [jax.ShapeDtypeStruct((excitations, shard_len), jnp.bfloat16)] * (count - 1),
        in_specs=[VMEM] * (len(parts) + 6),
        out_specs=[VMEM] * (count + 1),
        scratch_shapes=[
            pltpu.VMEM((p_tiles, excitations, LANES), jnp.float32),
            pltpu.VMEM((dual_moments.shape[0] * excitations, rows_t), jnp.bfloat16),
            pltpu.VMEM((q_tiles, excitations, LANES), jnp.float32),
        ],
        compiler_params=grant((col_devices, excitations, rows_t), (rows_t, cols_t // 2), (excitations, 8 * rows_t)),
    )(*parts, halo, gram_diag, gram_off, neighbours, s_tiles, dual_moments)
    shares = shares[:1] + [swap(share, "row", step) for step, share in zip(last_steps(count)[1:], shares[1:])]
    march_rhs, own_dual = pl.pallas_call(
        functools.partial(final_kernel, norm=norm),
        out_shape=[jax.ShapeDtypeStruct(incident.shape, jnp.float32)] * 2,
        in_specs=[VMEM] * (count + 2),
        out_specs=[VMEM, VMEM],
        compiler_params=grant((count, excitations, shard_len)),
    )(*shares, own_dual, incident)
    return (march_rhs, own_dual)


def solution(mesh):
    placed = (
        P(None, None, ("col", "row")),
        P(None, ("col", "row")),
        P(),
        P(),
        P(),
        P("row", "col"),
        P("row", "col"),
        P(None, "row"),
        P("row"),
        P(None, "row"),
    )
    return jax.shard_map(
        per_device,
        mesh=mesh,
        in_specs=placed,
        out_specs=(P(None, ("col", "row")), P(None, ("row", "col"))),
        check_vma=False,
    )
```

```python
import functools
import math

import jax
import jax.numpy as jnp
from jax import lax
from jax.experimental import pallas as pl
from jax.experimental.pallas import tpu as pltpu
from jax.sharding import PartitionSpec as P

SWEEPS = 2

SOFT_T = 0.05
SOFT_S = 0.1
NEAR_GAIN = 2.0
NEAR_REACH = 0.5

LANES = 128
HALF = LANES // 2
CHUNK = 64

VMEM = pl.BlockSpec(memory_space=pltpu.VMEM)
SMEM = pl.BlockSpec(memory_space=pltpu.SMEM)
LOG2_E = 1.4426950408889634
TINY = 1e-30
MIB = 1024 * 1024


def grant(*shapes):
    total = 0
    for shape in shapes:
        size = 4
        for extent in shape[:-2] + (-(-shape[-2] // 8) * 8, shape[-1]):
            size *= extent
        total += size
    return pltpu.CompilerParams(vmem_limit_bytes=min(56 * MIB, 2 * total + 2 * MIB))


def root(square):
    square = jnp.maximum(square, TINY)
    return square * lax.rsqrt(square)


def inverse(value):
    return pl.reciprocal(value, approx=True)


def lane_ids(rows=1):
    return lax.broadcasted_iota(jnp.int32, (rows, LANES), 1)


def tile_at(start):
    return pl.ds(pl.multiple_of(start, LANES), LANES)


def edges(ref, row, length):
    first = ref[row : row + 1, :LANES]
    last = ref[row : row + 1, length - LANES :]
    return jnp.where(lane_ids() < HALF, first, last)


def split2(value):
    high = value.astype(jnp.bfloat16).astype(jnp.float32)
    return [high, value - high]


def stack_rows(rows, height):
    row_ids = lax.broadcasted_iota(jnp.int32, (height, LANES), 0)
    out = jnp.zeros((height, LANES), jnp.float32)
    for position, row in enumerate(rows):
        out = jnp.where(row_ids == position, row, out)
    return out


def pack_kernel(history_ref, shell_ref, near_ref, diag_ref, off_ref, links_ref, centroids_ref, out_ref, lines_ref):
    slots, excitations = history_ref.shape[:2]
    length = diag_ref.shape[1]
    tiles = shell_ref.shape[1]
    lanes = lane_ids()
    rows = []
    for tile in (0, tiles - 1):
        code = jnp.zeros((1, LANES), jnp.float32)
        for j in range(shell_ref.shape[0]):
            value = (shell_ref[j, tile] + slots * near_ref[j, tile]).astype(jnp.float32)
            code = jnp.where(lanes == j, value, code)
        rows.append(code)
    here = lax.axis_index("row") * length + jnp.where(lanes < HALF, lanes, length - LANES + lanes)
    for m in range(links_ref.shape[0]):
        rows.append((edges(links_ref, m, length) - here).astype(jnp.float32))
    rows += split2(edges(diag_ref, 0, length))
    for m in range(off_ref.shape[0]):
        rows += split2(edges(off_ref, m, length))
    out_ref[:slots] = history_ref[...]
    out_ref[slots] = stack_rows(rows, excitations).astype(jnp.bfloat16)
    me = lax.axis_index("row")
    row_start = me * length
    q_tiles = shell_ref.shape[0]
    col_start = lax.axis_index("col") * (q_tiles * LANES)
    sources = [source_of(me, i, q_tiles) for i in range(q_tiles)]
    for t in range(tiles):
        for axis in range(3):
            lines_ref[3 * t + axis] = centroids_ref[axis, tile_at(row_start + t * LANES)]
    row = 3 * tiles
    for axis in range(3):
        lines_ref[row + axis : row + axis + 1] = halo_line(centroids_ref, axis, row_start, length)
    row += 3
    for i in range(q_tiles):
        for axis in range(3):
            lines_ref[row + axis] = centroids_ref[axis, tile_at(col_start + sources[i] * LANES)]
        row += 3
    for t in range(tiles):
        for i in range(q_tiles):
            gain = NEAR_GAIN * near_ref[sources[i], t].astype(jnp.float32)
            lines_ref[row : row + 1] = jnp.full((1, LANES), gain, jnp.float32)
            row += 1


def target_of(me, step, count):
    return me ^ step if count & (count - 1) == 0 else lax.rem(me + step, count)


def source_of(me, step, count):
    return me ^ step if count & (count - 1) == 0 else lax.rem(me + count - step, count)


def step_from(me, source, count):
    return me ^ source if count & (count - 1) == 0 else lax.rem(me + count - source, count)


def entries_t(line, column, gains):
    dx, dy, dz = [line[axis] - column[axis] for axis in range(3)]
    spacing = root(dx * dx + dy * dy + dz * dz)
    far, near = inverse(spacing + SOFT_T), jnp.exp2(spacing * (-LOG2_E / NEAR_REACH))
    return [(far + gain * near).astype(jnp.bfloat16) if gain is not None else far.astype(jnp.bfloat16) for gain in gains]


def columns(line):
    return jnp.broadcast_to(line, (LANES, LANES)).T


def halo_line(ref, row, row_start, length):
    total = ref.shape[1]
    right_start = lax.rem(row_start + length, total)
    left_start = lax.rem(row_start + total - LANES, total)
    return jnp.where(
        lane_ids() < HALF, ref[row : row + 1, tile_at(right_start)], ref[row : row + 1, tile_at(left_start)]
    )


def t_tiles_kernel(lines_ref, out_ref, column_ref, p_tiles, q_tiles):
    first_column = 3 * (p_tiles + 1)
    first_gain = first_column + 3 * q_tiles
    for i in range(q_tiles):
        for axis in range(3):
            row = first_column + 3 * i + axis
            column_ref[axis, i * LANES : (i + 1) * LANES, :] = columns(lines_ref[row : row + 1])

    def fill(first, gains_of):
        line = [lines_ref[pl.ds(3 * first + axis, 1)] for axis in range(3)]
        for i in range(q_tiles):
            gains = gains_of(i)
            for k in range(LANES // CHUNK):
                at = slice(i * LANES + k * CHUNK, i * LANES + (k + 1) * CHUNK)
                for offset, tile in enumerate(entries_t(line, [column_ref[axis, at, :] for axis in range(3)], gains)):
                    out_ref[first + offset, at, :] = tile

    group = max(1, 16 // q_tiles)
    while p_tiles % group:
        group -= 1

    def one_group(g, carry):
        for k in range(group):
            t = g * group + k
            fill(t, lambda i: [lines_ref[pl.ds(first_gain + t * q_tiles + i, 1)]])
        return carry

    lax.fori_loop(0, p_tiles // group, one_group, 0)
    fill(p_tiles, lambda i: [None, NEAR_GAIN])


def t_kernel(*refs, norm, slots, count):
    packed = [refs[order_of(count).index(step)] for step in range(count)]
    tiles_ref, moments_ref, shell_in = refs[count : count + 3]
    out_ref, halo_ref, scaled_ref, edge_ref, shell_ref, sem = refs[count + 3 :]
    shell_copy = pltpu.make_async_copy(shell_in, shell_ref, sem)
    shell_copy.start()
    q_tiles, p_tiles = shell_ref.shape
    excitations = out_ref.shape[0]
    kinds = moments_ref.shape[0]
    me = lax.axis_index("row")
    length = p_tiles * LANES
    row_start = me * length
    col_start = lax.axis_index("col") * (q_tiles * LANES)
    low = lane_ids() < HALF

    for i in range(count):
        edge_ref[i] = packed[i][slots:].astype(jnp.float32)
    right = edge_ref[step_from(me, lax.rem(me + 1, count), count)]
    left = edge_ref[step_from(me, lax.rem(me + count - 1, count), count)]
    halo_ref[...] = jnp.where(low[None], right, left)
    codes = right[0, 0:1], left[0, 1:2]
    nears = [jnp.where(code >= slots, 1.0, 0.0) for code in codes]
    picks = [code - slots * near for code, near in zip(codes, nears)]

    sources = [source_of(me, i, count) for i in range(count)]
    lanes = lane_ids()
    halo_tiles = []
    for i in range(count):
        at = slice(i * LANES, (i + 1) * LANES)
        weights = [moments_ref[a : a + 1, tile_at(col_start + sources[i] * LANES)] for a in range(kinds)]
        values = [packed[i][s].astype(jnp.float32) for s in range(slots)]
        here = lanes == sources[i]
        for pick in picks:
            choice = jnp.sum(jnp.where(here, pick, 0.0), axis=1, keepdims=True)
            value = values[0]
            for s in range(1, slots):
                value = jnp.where(choice == s, values[s], value)
            values.append(value)
        for s, value in enumerate(values):
            for a in range(kinds):
                scaled_ref[s, a * excitations : (a + 1) * excitations, at] = (weights[a] * value).astype(jnp.bfloat16)
        near_right, near_left = [jnp.sum(jnp.where(here, near, 0.0), axis=1, keepdims=True) for near in nears]
        near = jnp.where(low, near_right, near_left)
        halo_tiles.append(
            jnp.where(near > 0.5, tiles_ref[p_tiles + 1, at].astype(jnp.float32), tiles_ref[p_tiles, at].astype(jnp.float32))
            .astype(jnp.bfloat16)
        )

    def weighted(product, weights):
        field = weights[0] * product[:excitations]
        for a in range(1, kinds):
            term = weights[a] * product[a * excitations : (a + 1) * excitations]
            field = field + term if a < kinds - 1 else field - term
        return (field * norm).astype(jnp.bfloat16)

    halo_tile = jnp.concatenate(halo_tiles, axis=0)
    product = jnp.where(
        low,
        jnp.dot(scaled_ref[slots], halo_tile, preferred_element_type=jnp.float32),
        jnp.dot(scaled_ref[slots + 1], halo_tile, preferred_element_type=jnp.float32),
    )
    out_ref[:, length:] = weighted(product, [halo_line(moments_ref, a, row_start, length) for a in range(kinds)])

    def one_tile(t):
        lhs = jnp.concatenate(
            [scaled_ref[shell_ref[sources[i], t], :, i * LANES : (i + 1) * LANES] for i in range(count)], axis=1
        )
        weights = [moments_ref[a : a + 1, tile_at(row_start + t * LANES)] for a in range(kinds)]
        product = jnp.dot(lhs, tiles_ref[t], preferred_element_type=jnp.float32)
        out_ref[:, tile_at(t * LANES)] = weighted(product, weights)

    group = max(1, 32 // q_tiles)
    while p_tiles % group:
        group -= 1

    def one_group(g, carry):
        for k in range(group):
            one_tile(g * group + k)
        return carry

    shell_copy.wait()
    if group == p_tiles:
        one_group(0, 0)
    else:
        lax.fori_loop(0, p_tiles // group, one_group, 0)

def s_tiles_kernel(centroids_ref, out_ref, column_ref):
    length, width = out_ref.shape
    row_start = lax.axis_index("row") * length
    col_start = lax.axis_index("col") * width

    def one_tile(t, carry):
        for axis in range(3):
            column_ref[axis] = columns(centroids_ref[axis : axis + 1, tile_at(row_start + t * LANES)])
        for k in range(width // LANES):
            line = [centroids_ref[axis : axis + 1, tile_at(col_start + k * LANES)] for axis in range(3)]
            for piece in range(LANES // CHUNK):
                at = slice(piece * CHUNK, (piece + 1) * CHUNK)
                dx = line[0] - column_ref[0, at, :]
                dy = line[1] - column_ref[1, at, :]
                dz = line[2] - column_ref[2, at, :]
                spacing = root(dx * dx + dy * dy + dz * dz)
                rows = pl.ds(pl.multiple_of(t * LANES + piece * CHUNK, CHUNK), CHUNK)
                out_ref[rows, k * LANES : (k + 1) * LANES] = inverse(spacing + SOFT_S).astype(jnp.bfloat16)
        return carry

    lax.fori_loop(0, length // LANES, one_tile, 0)


def sweep_kernel(*refs, slots, part_count, count):
    parts = refs[:part_count]
    halo_ref, diag_ref, off_ref, links_ref, tiles_ref, dual_moments_ref = refs[part_count : part_count + 6]
    dual_ref, *out_refs = refs[part_count + 6 : -3]
    iter_ref, scaled_ref, share_ref = refs[-3:]
    length = diag_ref.shape[1]
    tiles = length // LANES
    excitations = parts[0].shape[0]
    link_count = links_ref.shape[0]
    kinds = dual_moments_ref.shape[0]
    row_start = lax.axis_index("row") * length
    col_start = lax.axis_index("col") * tiles_ref.shape[1]
    lanes = lane_ids()
    low = lanes < HALF

    def halo(row):
        return halo_ref[0, row : row + 1]

    def sum2(row):
        return halo(row) + halo(row + 1)

    def tile(t):
        return slice(t * LANES, (t + 1) * LANES)

    field, diag = [], []
    for t in range(tiles + 1):
        total = parts[0][:, tile(t)].astype(jnp.float32)
        for part in parts[1:]:
            total = total + part[:, tile(t)].astype(jnp.float32)
        field.append(total)
        diag.append(diag_ref[:, tile(t)] if t < tiles else sum2(2 + link_count))

    dual = [f / d for f, d in zip(field, diag)]
    for sweep_id in range(SWEEPS):
        last = sweep_id == SWEEPS - 1
        updated = []
        for t in range(tiles if last else tiles + 1):
            around = jnp.where(low, dual[(t + 1) % (tiles + 1)], dual[t - 1])
            coupled = jnp.zeros_like(field[t])
            for m in range(link_count):
                if t < tiles:
                    source = links_ref[m : m + 1, tile(t)] - (row_start + t * LANES)
                    gram = off_ref[m : m + 1, tile(t)]
                else:
                    source = halo(2 + m).astype(jnp.int32) + lanes
                    gram = sum2(4 + link_count + 2 * m)
                inside = (source >= 0) & (source < LANES)
                index = jnp.broadcast_to(source & (LANES - 1), (excitations, LANES))
                here = jnp.take_along_axis(dual[t], index, axis=1)
                beside = jnp.take_along_axis(around, index, axis=1)
                coupled = coupled + gram * jnp.where(inside, here, beside)
            updated.append((field[t] - coupled) / diag[t])
        dual = updated

    for t in range(tiles):
        iter_ref[t] = dual[t]
        for a in range(kinds):
            weight = dual_moments_ref[a : a + 1, tile_at(row_start + t * LANES)]
            scaled_ref[a * excitations : (a + 1) * excitations, tile(t)] = (weight * dual[t]).astype(jnp.bfloat16)
    dual_ref[...] = iter_ref[lax.axis_index("col")]
    product = jnp.dot(scaled_ref[...], tiles_ref[...], preferred_element_type=jnp.float32)
    for k in range(count):
        term = jnp.zeros((excitations, LANES), jnp.float32)
        for a in range(kinds):
            weight = dual_moments_ref[a : a + 1, tile_at(col_start + k * LANES)]
            term = term + weight * product[a * excitations : (a + 1) * excitations, tile(k)]
        share_ref[k] = term
    me = lax.axis_index("row")
    for step, out_ref in zip(last_steps(count), out_refs):
        out_ref[...] = share_ref[target_of(me, step, count)].astype(out_ref.dtype)


def final_kernel(*refs, norm):
    *share_refs, dual_in_ref, incident_ref, out_ref, dual_ref = refs
    total = share_refs[0][...].astype(jnp.float32)
    for share_ref in share_refs[1:]:
        total = total + share_ref[...].astype(jnp.float32)
    out_ref[...] = incident_ref[...] - total * norm
    dual_ref[...] = dual_in_ref[...]


def swap(value, axis, step):
    count = lax.axis_size(axis)
    if count & (count - 1) == 0:
        pairs = [(i, i ^ step) for i in range(count)]
    else:
        pairs = [(i, (i + step) % count) for i in range(count)]
    return lax.ppermute(value, axis, pairs)


def order_of(count):
    return (0, 1, 3, 2) if count == 4 else tuple(range(count))


def last_steps(count):
    return (0,) + tuple(range(count - 1, 0, -1))


def exchange(value, axis):
    count = lax.axis_size(axis)
    if count == 1 or count & (count - 1):
        return [value] + [swap(value, axis, step) for step in range(1, count)]
    step = 1
    while step < count:
        radix = min(4, count // step)
        values = [value] + [swap(value, axis, step * k) for k in range(1, radix)]
        step *= radix
        if step < count:
            value = sum(part.astype(jnp.float32) for part in values).astype(value.dtype)
    return values


def late(value, after):
    return lax.optimization_barrier((value, after))[0]


def per_device(
    history,
    incident,
    centroids,
    moments,
    dual_moments,
    shell,
    near_mask,
    neighbours,
    gram_diag,
    gram_off,
):
    col_devices = lax.axis_size("col")
    slots, excitations, shard_len = history.shape
    p_tiles, q_tiles = shell.shape
    rows_t = gram_diag.shape[0]
    cols_t = q_tiles * LANES
    norm = 1.0 / math.sqrt(centroids.shape[1])
    shell, near_mask = shell.T, near_mask.T
    gram_diag = gram_diag.reshape(1, rows_t)

    line_rows = -(-(3 * (p_tiles + 1 + q_tiles) + p_tiles * q_tiles) // 8) * 8
    packed, lines = pl.pallas_call(
        pack_kernel,
        out_shape=(
            jax.ShapeDtypeStruct((slots + 1, excitations, shard_len), jnp.bfloat16),
            jax.ShapeDtypeStruct((line_rows, LANES), jnp.float32),
        ),
        in_specs=[VMEM, SMEM, SMEM, VMEM, VMEM, VMEM, VMEM],
        out_specs=(VMEM, VMEM),
        compiler_params=pltpu.CompilerParams(vmem_limit_bytes=56 * MIB),
    )(history, shell, near_mask, gram_diag, gram_off, neighbours, centroids)
    count = lax.axis_size("row")
    everyone = [packed] + [swap(packed, "row", step) for step in range(count - 1, 0, -1)][::-1]
    entries = rows_t * cols_t
    t_tiles = pl.pallas_call(
        functools.partial(t_tiles_kernel, p_tiles=p_tiles, q_tiles=q_tiles),
        out_shape=jax.ShapeDtypeStruct((p_tiles + 2, cols_t, LANES), jnp.bfloat16),
        in_specs=[VMEM],
        out_specs=VMEM,
        scratch_shapes=[pltpu.VMEM((3, cols_t, LANES), jnp.float32)],
        compiler_params=grant((p_tiles + 8, cols_t // 2, LANES), centroids.shape),
        cost_estimate=pl.CostEstimate(flops=16 * entries, bytes_accessed=2 * entries, transcendentals=3 * entries),
    )(lines)

    parts, halo = pl.pallas_call(
        functools.partial(t_kernel, norm=norm, slots=slots, count=count),
        out_shape=(
            jax.ShapeDtypeStruct((excitations, rows_t + LANES), jnp.bfloat16),
            jax.ShapeDtypeStruct((1, excitations, LANES), jnp.float32),
        ),
        in_specs=[VMEM] * (count + 2) + [pl.BlockSpec(memory_space=pl.ANY)],
        out_specs=(VMEM, VMEM),
        scratch_shapes=[
            pltpu.VMEM((slots + 2, moments.shape[0] * excitations, cols_t), jnp.bfloat16),
            pltpu.VMEM((count, 1, excitations, LANES), jnp.float32),
            pltpu.SMEM(shell.shape, jnp.int32),
            pltpu.SemaphoreType.DMA,
        ],
        compiler_params=grant(
            (p_tiles + 2, cols_t // 2, LANES),
            (excitations, rows_t),
            (slots + 2, moments.shape[0] * excitations, cols_t),
            moments.shape,
        ),
    )(*[everyone[step] for step in order_of(count)], t_tiles, moments, shell)
    parts = exchange(parts, "col")
    s_tiles = pl.pallas_call(
        s_tiles_kernel,
        out_shape=jax.ShapeDtypeStruct((rows_t, cols_t), jnp.bfloat16),
        in_specs=[VMEM],
        out_specs=VMEM,
        scratch_shapes=[pltpu.VMEM((3, LANES, LANES), jnp.float32)],
        compiler_params=grant((rows_t, cols_t // 2), centroids.shape),
        cost_estimate=pl.CostEstimate(flops=12 * entries, bytes_accessed=2 * entries, transcendentals=2 * entries),
    )(late(centroids, parts[0]))

    own_dual, *shares = pl.pallas_call(
        functools.partial(sweep_kernel, slots=slots, part_count=len(parts), count=count),
        out_shape=[jax.ShapeDtypeStruct((excitations, shard_len), jnp.float32)] * 2
        + [jax.ShapeDtypeStruct((excitations, shard_len), jnp.bfloat16)] * (count - 1),
        in_specs=[VMEM] * (len(parts) + 6),
        out_specs=[VMEM] * (count + 1),
        scratch_shapes=[
            pltpu.VMEM((p_tiles, excitations, LANES), jnp.float32),
            pltpu.VMEM((dual_moments.shape[0] * excitations, rows_t), jnp.bfloat16),
            pltpu.VMEM((q_tiles, excitations, LANES), jnp.float32),
        ],
        compiler_params=grant((col_devices, excitations, rows_t), (rows_t, cols_t // 2), (excitations, 8 * rows_t)),
    )(*parts, halo, gram_diag, gram_off, neighbours, s_tiles, dual_moments)
    shares = shares[:1] + [swap(share, "row", step) for step, share in zip(last_steps(count)[1:], shares[1:])]
    march_rhs, own_dual = pl.pallas_call(
        functools.partial(final_kernel, norm=norm),
        out_shape=[jax.ShapeDtypeStruct(incident.shape, jnp.float32)] * 2,
        in_specs=[VMEM] * (count + 2),
        out_specs=[VMEM, VMEM],
        compiler_params=grant((count, excitations, shard_len)),
    )(*shares, own_dual, incident)
    return (march_rhs, own_dual)


def solution(mesh):
    placed = (
        P(None, None, ("col", "row")),
        P(None, ("col", "row")),
        P(),
        P(),
        P(),
        P("row", "col"),
        P("row", "col"),
        P(None, "row"),
        P("row"),
        P(None, "row"),
    )
    return jax.shard_map(
        per_device,
        mesh=mesh,
        in_specs=placed,
        out_specs=(P(None, ("col", "row")), P(None, ("row", "col"))),
        check_vma=False,
    )
```
